32 devices in a mesh: req: 8 (over z, x), tp: 4 (over y, core).
Axes of the slice: x: 2, y: 2, z: 4, core: 2. Of those that a mesh axis runs over, the one named last changes fastest.
Arguments:
- tokens: bfloat16 [6144, 2048], P('req'), may hold values from -6 to 6
- lengths: int32 [8, 8], P('req'), may hold values from 1 to 384, 768 in all within a row
- request_adapter: int32 [8, 8], P('req'), may hold values from 0 to 15
- w_qkv: bfloat16 [2048, 3, 2048], P('req', None, 'tp'), may hold values from -2 to 2
- w_out: bfloat16 [2048, 2048], P('tp', 'req'), may hold values from -0.125 to 0.125
- w_gate: bfloat16 [2048, 8192], P('req', 'tp'), may hold values from -0.125 to 0.125
- w_up: bfloat16 [2048, 8192], P('req', 'tp'), may hold values from -0.125 to 0.125
- w_down: bfloat16 [8192, 2048], P('tp', 'req'), may hold values from -0.0625 to 0.0625
- a_qkv: bfloat16 [2048, 256], replicated, may hold values from -0.125 to 0.125
- b_qkv: bfloat16 [256, 3, 2048], P(None, None, 'tp'), may hold values from -0.75 to 0.75
- a_out: bfloat16 [2048, 256], P('tp'), may hold values from -0.125 to 0.125
- b_out: bfloat16 [256, 2048], replicated, may hold values from -0.75 to 0.75
- a_gate: bfloat16 [2048, 256], replicated, may hold values from -0.125 to 0.125
- b_gate: bfloat16 [256, 8192], P(None, 'tp'), may hold values from -0.75 to 0.75
- a_up: bfloat16 [2048, 256], replicated, may hold values from -0.125 to 0.125
- b_up: bfloat16 [256, 8192], P(None, 'tp'), may hold values from -0.75 to 0.75
- a_down: bfloat16 [8192, 256], P('tp'), may hold values from -0.0625 to 0.0625
- b_down: bfloat16 [256, 2048], replicated, may hold values from -0.75 to 0.75
Outputs:
- layer_out: bfloat16 [6144, 2048], P('req')
The draws below stay inside these ranges and needn't reach their ends.
Inputs may be any that keep to these rules, and one draw needn't show every extreme that they name: Each row of lengths sums to 768, so the requests of one index of req fill all its slots; each row's largest length is 384.
All inputs are finite; a program needn't handle non-finite values.
Results may differ from the reference program's by a relative error of at most 0.017.
Values may be sent and summed in bfloat16 or wider, within the bound.
No kernel may reach another device: no remote copies, remote signals or barrier semaphores. Data moves between devices by JAX's collectives and lax.ppermute only.
A program may use at most 128 MiB of HBM per device.

```python
import math
from functools import partial
import jax
import jax.numpy as jnp
import numpy as np
from jax import lax

D = 2048
H = 16
HD = 128
FF = 8192
ADAPTERS = 16
RANK = 16
TOK_DEV = 768
RPD = 8
MOST = 384
SHARDS = 8
TOKENS = 6144
N_TP = 4


def draw_w_qkv(key, part):
    noise_key = jax.random.fold_in(key, 0)
    unit_scale = 1.0 / math.sqrt(D)
    return (jax.random.truncated_normal(noise_key, -4.0, 4.0, (D, 3, D), jnp.float32) * unit_scale).astype(jnp.bfloat16)


def plant(result, key, least, high):
    index_at = [jax.random.randint(jax.random.fold_in(key, axis), (), 0, length) for axis, length in enumerate(result.shape)]
    widest = result.shape.index(max(result.shape))
    neighbour = index_at[:widest] + [(index_at[widest] + 1) % result.shape[widest]] + index_at[widest + 1:]
    return result.at[tuple(index_at)].set(least).at[tuple(neighbour)].set(high)


def levels(rng, shape, pieces, least, top_value):
    loudness, own = 1.0, jax.random.fold_in(rng, 6)
    for axis_at, blocks in pieces:
        draws = jnp.exp(jax.random.uniform(jax.random.fold_in(own, axis_at), (blocks,), jnp.float32, least / len(pieces), top_value / len(pieces)))
        loudness = loudness * jnp.repeat(draws, shape[axis_at] // blocks).reshape([-1 if axis == axis_at else 1 for axis in range(len(shape))])
    return loudness


def length_profile(count, total, reach, slope):
    portions = [(1 << 20) // math.isqrt(standing ** slope) + 1 for standing in range(2, count + 1)]
    spare, counts = total - reach - (count - 1), [1] * (count - 1)
    while spare > 0:
        movable = [i for i in range(count - 1) if counts[i] < reach]
        whole, budget = sum([portions[i] for i in movable]), spare
        for i in movable:
            addition = min(reach - counts[i], max(1, budget * portions[i] // whole), spare)
            counts[i] = counts[i] + addition
            spare = spare - addition
    return np.array([reach] + counts)


def uneven(rng, amount, total, most, slope):
    if amount == 2:
        one = jax.random.randint(rng, (), max(1, total - most), min(most, total - 1) + 1)
        return jnp.stack([one, total - one])
    sizes = jnp.asarray(length_profile(amount, total, most, slope), jnp.int32)
    twos = (amount - 1) // 2
    source_of, receiver = sizes[1:1 + 2 * twos:2], sizes[2:2 + 2 * twos:2]
    margin = jnp.minimum(source_of - 1, most - receiver)
    passed = jax.random.randint(jax.random.fold_in(rng, 1), (twos,), 0, 1 << 20) % (margin + 1)
    sizes = sizes.at[1:1 + 2 * twos:2].set(source_of - passed).at[2:2 + 2 * twos:2].set(receiver + passed)
    return sizes[jax.random.permutation(jax.random.fold_in(rng, 2), amount)]


def bell_draw(stream_key, dims, scale, most, cuts=(), held_as=jnp.bfloat16):
    values = scale * jax.random.normal(stream_key, dims, jnp.float32)
    if cuts:
        values = values * levels(stream_key, dims, cuts, -0.22, 0.18)
    return jnp.clip(values, -most, most).astype(held_as)


def setup_inputs(seed: int = 0) -> dict:
    seeds = jax.random.split(jax.random.key(seed), 19)
    return {
        "tokens": bell_draw(seeds[0], (TOKENS, D), 1.0, 6.0, ((0, 8),)),
        "lengths": jax.vmap(lambda own: uneven(own, RPD, TOK_DEV, MOST, 2))(jax.random.split(seeds[1], SHARDS)).reshape((SHARDS, RPD)).astype(jnp.int32),
        "request_adapter": plant(jax.random.randint(seeds[2], (SHARDS, RPD), 0, ADAPTERS), jax.random.fold_in(seeds[2], 1), 0, ADAPTERS - 1).astype(jnp.int32),
        "w_qkv": draw_w_qkv(jax.random.fold_in(seeds[18], 71), 0),
        "w_out": bell_draw(seeds[4], (D, D), D ** -0.5, 0.125, ((0, 4), (1, 8))),
        "w_gate": bell_draw(seeds[5], (D, FF), D ** -0.5, 0.125, ((0, 8), (1, 4))),
        "w_up": bell_draw(seeds[6], (D, FF), D ** -0.5, 0.125, ((0, 8), (1, 4))),
        "w_down": bell_draw(seeds[7], (FF, D), FF ** -0.5, 0.0625, ((0, 4), (1, 8))),
        "a_qkv": bell_draw(seeds[8], (D, ADAPTERS * RANK), D ** -0.5, 0.125),
        "b_qkv": bell_draw(seeds[9], (ADAPTERS * RANK, 3, D), (4 * RANK) ** -0.5, 0.75, ((2, 4),)),
        "a_out": bell_draw(seeds[10], (D, ADAPTERS * RANK), D ** -0.5, 0.125, ((0, 4),)),
        "b_out": bell_draw(seeds[11], (ADAPTERS * RANK, D), (4 * RANK) ** -0.5, 0.75),
        "a_gate": bell_draw(seeds[12], (D, ADAPTERS * RANK), D ** -0.5, 0.125),
        "b_gate": bell_draw(seeds[13], (ADAPTERS * RANK, FF), (4 * RANK) ** -0.5, 0.75, ((1, 4),)),
        "a_up": bell_draw(seeds[14], (D, ADAPTERS * RANK), D ** -0.5, 0.125),
        "b_up": bell_draw(seeds[15], (ADAPTERS * RANK, FF), (4 * RANK) ** -0.5, 0.75, ((1, 4),)),
        "a_down": bell_draw(seeds[16], (FF, ADAPTERS * RANK), FF ** -0.5, 0.0625, ((0, 4),)),
        "b_down": bell_draw(seeds[17], (ADAPTERS * RANK, D), (4 * RANK) ** -0.5, 0.75),
    }


epsilon = 1e-05
rope_base = 10000.0

def layer_norm(values):
    row_mean = lax.optimization_barrier(jnp.mean(values, axis=-1, keepdims=True))
    centred = values - row_mean
    spread = lax.optimization_barrier(jnp.mean(centred * centred, axis=-1, keepdims=True))
    return (centred * lax.rsqrt(spread + epsilon)).astype(jnp.bfloat16)

def slot_layout(lengths_row, adapters_row, slot_count):
    request_ends = jnp.cumsum(lengths_row).astype(jnp.int32)
    request_starts = (request_ends - lengths_row).astype(jnp.int32)
    slot_index = jnp.arange(slot_count, dtype=jnp.int32)
    request_of = lax.optimization_barrier(jnp.sum((slot_index[:, None] >= request_ends[None, :]).astype(jnp.int32), axis=1)).astype(jnp.int32)
    member = request_of[:, None] == jnp.arange(lengths_row.shape[0], dtype=jnp.int32)[None, :]
    position = (slot_index - lax.optimization_barrier(jnp.sum(jnp.where(member, request_starts[None, :], 0), axis=1))).astype(jnp.int32)
    adapter = lax.optimization_barrier(jnp.sum(jnp.where(member, adapters_row[None, :], 0), axis=1)).astype(jnp.int32)
    return (request_of, position, adapter)

def rotate(values, position):
    half_width = values.shape[-1] // 2
    frequency = jnp.exp(-math.log(rope_base) * 2.0 * jnp.arange(half_width, dtype=jnp.float32) / values.shape[-1])
    angles = position.astype(jnp.float32)[:, None] * frequency[None, :]
    cosine = jnp.cos(angles)[:, None, :]
    sine_part = jnp.sin(angles)[:, None, :]
    lower_half = values[..., :half_width]
    upper_half = values[..., half_width:]
    return jnp.concatenate([lower_half * cosine - upper_half * sine_part, upper_half * cosine + lower_half * sine_part], axis=-1)

def rounded(values):
    return lax.optimization_barrier(values.astype(jnp.bfloat16)).astype(jnp.float32)

def reference(tokens, lengths, request_adapter, w_qkv, w_out, w_gate, w_up, w_down, a_qkv, b_qkv, a_out, b_out, a_gate, b_gate, a_up, b_up, a_down, b_down):
    total_slots = tokens.shape[0]
    request_of, position, adapter = jax.vmap(partial(slot_layout, slot_count=TOK_DEV))(lengths, request_adapter)
    adapter_flat = adapter.reshape(-1)
    select = adapter_flat[:, None] == (jnp.arange(ADAPTERS * RANK, dtype=jnp.int32) // RANK)[None, :]

    def low_rank(inner, b_matrix):
        masked = jnp.where(select, inner, jnp.float32(0.0)).astype(jnp.bfloat16)
        return jnp.dot(masked, b_matrix, preferred_element_type=jnp.float32)
    normed = layer_norm(tokens.astype(jnp.float32))
    joined = jnp.dot(normed, w_qkv.reshape(D, 3 * D), preferred_element_type=jnp.float32)
    joined = joined + low_rank(jnp.dot(normed, a_qkv, preferred_element_type=jnp.float32), b_qkv.reshape(ADAPTERS * RANK, 3 * D))
    joined = joined.reshape(total_slots, 3, H, HD)
    position_flat = position.reshape(-1)
    query = rotate(joined[:, 0], position_flat).astype(jnp.bfloat16)
    key_rot = rotate(joined[:, 1], position_flat).astype(jnp.bfloat16)
    value_part = joined[:, 2].astype(jnp.bfloat16)
    score_scale = 1.0 / math.sqrt(HD)

    def attend(items):
        query_block, key_block, value_block, request_block = items
        slot_index = jnp.arange(TOK_DEV, dtype=jnp.int32)
        allowed = (request_block[:, None] == request_block[None, :]) & (slot_index[:, None] >= slot_index[None, :])
        scores = jnp.einsum('qhd,khd->hqk', query_block.astype(jnp.float32), key_block.astype(jnp.float32)) * score_scale
        scores = jnp.where(allowed[None], scores, jnp.float32(-1e+30))
        top_score = lax.optimization_barrier(jnp.max(scores, axis=-1, keepdims=True))
        expo = jnp.exp(scores - top_score)
        weights = (expo / lax.optimization_barrier(jnp.sum(expo, axis=-1, keepdims=True))).astype(jnp.bfloat16)
        mixed = jnp.einsum('hqk,khd->qhd', weights.astype(jnp.float32), value_block.astype(jnp.float32))
        return mixed.astype(jnp.bfloat16)
    attn = lax.map(attend, (query.reshape(SHARDS, TOK_DEV, H, HD), key_rot.reshape(SHARDS, TOK_DEV, H, HD), value_part.reshape(SHARDS, TOK_DEV, H, HD), request_of))
    attn_flat = attn.reshape(total_slots, D)
    group_width = D // N_TP
    attn_part = jnp.zeros((total_slots, D), jnp.float32)
    low_attn = jnp.zeros((total_slots, ADAPTERS * RANK), jnp.float32)
    for group in range(N_TP):
        columns = attn_flat[:, group * group_width:(group + 1) * group_width]
        attn_part = attn_part + rounded(jnp.dot(columns, w_out[group * group_width:(group + 1) * group_width], preferred_element_type=jnp.float32))
        low_attn = low_attn + rounded(jnp.dot(columns, a_out[group * group_width:(group + 1) * group_width], preferred_element_type=jnp.float32))
    hidden_state = tokens.astype(jnp.float32) + attn_part + low_rank(low_attn, b_out)
    normed2 = layer_norm(hidden_state)
    gate_proj = jnp.dot(normed2, w_gate, preferred_element_type=jnp.float32) + low_rank(jnp.dot(normed2, a_gate, preferred_element_type=jnp.float32), b_gate)
    up_proj = jnp.dot(normed2, w_up, preferred_element_type=jnp.float32) + low_rank(jnp.dot(normed2, a_up, preferred_element_type=jnp.float32), b_up)
    hidden = (jax.nn.silu(gate_proj) * up_proj).astype(jnp.bfloat16)
    unit_width = FF // N_TP
    down_part = jnp.zeros((total_slots, D), jnp.float32)
    low_down = jnp.zeros((total_slots, ADAPTERS * RANK), jnp.float32)
    for group in range(N_TP):
        columns = hidden[:, group * unit_width:(group + 1) * unit_width]
        down_part = down_part + rounded(jnp.dot(columns, w_down[group * unit_width:(group + 1) * unit_width], preferred_element_type=jnp.float32))
        low_down = low_down + rounded(jnp.dot(columns, a_down[group * unit_width:(group + 1) * unit_width], preferred_element_type=jnp.float32))
    return (hidden_state + down_part + low_rank(low_down, b_down)).astype(jnp.bfloat16)
```

```python
import math

import jax
import jax.numpy as jnp
from jax import lax
from jax.sharding import PartitionSpec as P

HD = 128
RANK = 16
AXES = ("req", "tp")
epsilon = 1e-05
rope_base = 10000.0
F32 = jnp.float32
BF16 = jnp.bfloat16


def layer_norm(values):
    row_mean = jnp.mean(values, axis=-1, keepdims=True)
    centred = values - row_mean
    spread = jnp.mean(centred * centred, axis=-1, keepdims=True)
    return (centred * lax.rsqrt(spread + epsilon)).astype(BF16)


def slot_layout(lengths_row, adapters_row, slot_count):
    request_ends = jnp.cumsum(lengths_row)
    request_starts = request_ends - lengths_row
    slot_index = jnp.arange(slot_count, dtype=jnp.int32)
    request_of = jnp.sum((slot_index[:, None] >= request_ends[None, :]).astype(jnp.int32), axis=1)
    member = request_of[:, None] == jnp.arange(lengths_row.shape[0], dtype=jnp.int32)[None, :]
    position = slot_index - jnp.sum(jnp.where(member, request_starts[None, :], 0), axis=1)
    adapter = jnp.sum(jnp.where(member, adapters_row[None, :], 0), axis=1)
    return (request_of, position, adapter)


def rotate(values, position):
    half_width = values.shape[-1] // 2
    frequency = jnp.exp(
        -math.log(rope_base) * 2.0 * jnp.arange(half_width, dtype=F32) / values.shape[-1]
    )
    angles = position.astype(F32)[:, None] * frequency[None, :]
    cosine = jnp.cos(angles)[:, None, :]
    sine_part = jnp.sin(angles)[:, None, :]
    lower_half = values[..., :half_width]
    upper_half = values[..., half_width:]
    return jnp.concatenate(
        [
            lower_half * cosine - upper_half * sine_part,
            upper_half * cosine + lower_half * sine_part,
        ],
        axis=-1,
    )


def dot(a, b):
    return jnp.dot(a, b, preferred_element_type=F32)


def attend(query_rot, key_rot, value_part, request_of):
    slot_index = jnp.arange(query_rot.shape[0], dtype=jnp.int32)
    allowed = (request_of[:, None] == request_of[None, :]) & (
        slot_index[:, None] >= slot_index[None, :]
    )
    scores = jnp.einsum("qhd,khd->hqk", query_rot, key_rot, preferred_element_type=F32) * (
        1.0 / math.sqrt(HD)
    )
    scores = jnp.where(allowed[None], scores, F32(-1e30))
    top_score = jnp.max(scores, axis=-1, keepdims=True)
    expo = jnp.exp(scores - top_score)
    weights = (expo / jnp.sum(expo, axis=-1, keepdims=True)).astype(BF16)
    return jnp.einsum("hqk,khd->qhd", weights, value_part, preferred_element_type=F32).astype(BF16)


def make_body(R, T):
    Z, ZH, Y = R // 2, R // 4, T // 2

    def move(f):
        pairs = []
        for r in range(R):
            for t in range(T):
                z, x, y, c = f(r // 2, r % 2, t // 2, t % 2)
                pairs.append((r * T + t, (z * 2 + x) * T + y * 2 + c))
        return pairs

    def send(value, pairs):
        return lax.ppermute(value, AXES, pairs)

    to_core = move(lambda z, x, y, c: (z, x, y, 1 - c))
    to_x = move(lambda z, x, y, c: (z, 1 - x, y, c))
    to_xz = {
        (i, j): move(lambda z, x, y, c: (z ^ j, x ^ i, y, c)) for i in (0, 1) for j in (0, 1)
    }
    z_up = move(lambda z, x, y, c: ((z + 1) % Z, x, y, c))
    z_down = move(lambda z, x, y, c: ((z - 1) % Z, x, y, c))
    from_y = {k: move(lambda z, x, y, c: (z, x, (y - k) % Y, c)) for k in range(1, Y)}
    from_zh = {
        k: move(lambda z, x, y, c: ((z - 2 * k) % Z, x, y, c)) for k in range(1, ZH)
    }

    def ring(halves):
        got = {0: halves}
        left, right = halves, halves
        for k in range(1, Z // 2):
            left = [send(h, z_up) for h in left]
            right = [send(h, z_down) for h in right]
            got[Z - k], got[k] = left, right
        got[Z // 2] = [send(left[0], z_up), send(right[1], z_down)]
        return got

    def body(
        tokens, lengths, request_adapter, w_qkv, w_out, w_gate, w_up, w_down,
        a_qkv, b_qkv, a_out, b_out, a_gate, b_gate, a_up, b_up, a_down, b_down,
    ):
        r, t = lax.axis_index("req"), lax.axis_index("tp")
        z, x, y, c = r // 2, r % 2, t // 2, t % 2
        zh, zl = z // 2, z % 2
        slots, width = tokens.shape
        piece = slots // T
        block = width // R
        local = w_qkv.shape[2]
        rank_all = a_qkv.shape[1]
        quarter = w_gate.shape[1] // 4
        span = width // ZH

        def cut(array, start, size, axis):
            return lax.dynamic_slice_in_dim(array, start, size, axis)

        own_qkv = w_qkv.reshape(block, 3 * local)
        got = ring([own_qkv[: block // 2], own_qkv[block // 2 :]])
        qkv_blocks = []
        for k in range(Z):
            here = jnp.concatenate(got[k], axis=0)
            qkv_blocks += [here, send(here, to_x)]
        w_qkv_all = jnp.concatenate(qkv_blocks, axis=0)
        got = ring([w_out[: local // 2], w_out[local // 2 :]])
        out_blocks = []
        for k in range(Z):
            here = jnp.concatenate(got[k], axis=0)
            out_blocks += [here, send(here, to_x)]
        w_out_all = jnp.concatenate(out_blocks, axis=1)
        order = [((z + k) % Z) * 2 + (x ^ i) for k in range(Z) for i in (0, 1)]

        def scatter(parts, axis, join):
            pieces = {}
            for i in (0, 1):
                for j in (0, 1):
                    at = ((zl ^ j) * 2 + (x ^ i)) * quarter
                    p = jnp.concatenate([cut(w, at, quarter, axis) for w in parts], axis=axis)
                    pieces[(i, j)] = p if i == j == 0 else send(p, to_xz[(i, j)])
            stacked = jnp.stack([pieces[(i, j)] for j in (0, 1) for i in (0, 1)])
            me = zl * 2 + x
            return jnp.concatenate(
                [lax.dynamic_index_in_dim(stacked, me ^ b, 0, keepdims=False) for b in range(4)],
                axis=join,
            )

        mine = (zl * 2 + x) * quarter
        gu_own = scatter([w_gate, w_up], 1, 0)
        down_own = scatter([w_down], 0, 1)
        b_own = jnp.concatenate(
            [cut(b_gate, mine, quarter, 1), cut(b_up, mine, quarter, 1)], axis=1
        )
        a_down_own = cut(a_down, mine, quarter, 0)
        gu, down, b_gu, a_dn = {(0, 0): gu_own}, {(0, 0): down_own}, [b_own], [a_down_own]
        for k in range(1, ZH):
            gu[(k, 0)] = send(gu_own, from_zh[k])
            down[(k, 0)] = send(down_own, from_zh[k])
        for k in range(1, Y):
            both = send(jnp.concatenate([gu_own, b_own], axis=0), from_y[k])
            gu[(0, k)] = both[: gu_own.shape[0]]
            b_gu.append(both[gu_own.shape[0] :])
            both = send(jnp.concatenate([down_own, a_down_own], axis=1), from_y[k])
            down[(0, k)] = both[:, : down_own.shape[1]]
            a_dn.append(both[:, down_own.shape[1] :])
            for h in range(1, ZH):
                gu[(h, k)] = send(gu[(h, 0)], from_y[k])
                down[(h, k)] = send(down[(h, 0)], from_y[k])

        request_of, position, adapter = slot_layout(lengths[0], request_adapter[0], slots)
        column_adapter = jnp.arange(rank_all, dtype=jnp.int32) // RANK

        def masked(inner, adapter_rows):
            chosen = adapter_rows[:, None] == column_adapter[None, :]
            return jnp.where(chosen, inner, F32(0.0)).astype(BF16)

        normed = layer_norm(tokens.astype(F32))
        normed_rel = jnp.concatenate([cut(normed, b * block, block, 1) for b in order], axis=1)
        low = masked(dot(normed, a_qkv), adapter)
        joined = dot(normed_rel, w_qkv_all) + dot(low, b_qkv.reshape(rank_all, 3 * local))
        joined = joined.reshape(slots, 3, local // HD, HD)
        query_rot = rotate(joined[:, 0], position).astype(BF16)
        key_rot = rotate(joined[:, 1], position).astype(BF16)
        attn = attend(query_rot, key_rot, joined[:, 2].astype(BF16), request_of)
        attn = attn.reshape(slots, local)
        low = masked(dot(attn, a_out), adapter)
        b_out_rel = jnp.concatenate([cut(b_out, b * block, block, 1) for b in order], axis=1)
        part = (dot(attn, w_out_all) + dot(low, b_out_rel)).astype(BF16)
        part = part.reshape(Y, 2, piece, width)
        keep = lax.dynamic_index_in_dim(part, c, 1, keepdims=False)
        give = lax.dynamic_index_in_dim(part, 1 - c, 1, keepdims=False)
        pair = (keep.astype(F32) + send(give, to_core).astype(F32)).astype(BF16)
        total = lax.dynamic_index_in_dim(pair, y, 0, keepdims=False).astype(F32)
        for k in range(1, Y):
            p = lax.dynamic_index_in_dim(pair, (y - k) % Y, 0, keepdims=False)
            total = total + send(p, from_y[k]).astype(F32)
        back = [((b // 2 - z) % Z) * 2 + ((b % 2) ^ x) for b in range(R)]
        total = jnp.concatenate([cut(total, b * block, block, 1) for b in back], axis=1)
        hidden_state = cut(tokens, t * piece, piece, 0).astype(F32) + total
        normed2 = layer_norm(hidden_state)

        others = [(1, 0), (0, 1), (1, 1)]
        rows = jnp.concatenate([normed2] + [send(normed2, to_xz[o]) for o in others], axis=0)
        rows = jnp.concatenate([rows, send(rows, to_core)], axis=0)
        adapters = jnp.stack([adapter] + [send(adapter, to_xz[o]) for o in others])
        adapters = jnp.concatenate(
            [cut(adapters, (y * 2 + (c ^ s)) * piece, piece, 1).reshape(-1) for s in (0, 1)]
        )
        low_gate = masked(dot(rows, a_gate), adapters)
        low_up = masked(dot(rows, a_up), adapters)
        hidden = []
        columns = [cut(rows, ((zh + k) % ZH) * span, span, 1) for k in range(ZH)]
        for k in range(Y):
            gate_proj = dot(low_gate, b_gu[k][:, :quarter])
            up_proj = dot(low_up, b_gu[k][:, quarter:])
            for h in range(ZH):
                gate_proj = gate_proj + dot(columns[h], gu[(h, k)][:, :quarter])
                up_proj = up_proj + dot(columns[h], gu[(h, k)][:, quarter:])
            hidden.append((jax.nn.silu(gate_proj) * up_proj).astype(BF16))
        low_down = dot(hidden[0], a_dn[0])
        for k in range(1, Y):
            low_down = low_down + dot(hidden[k], a_dn[k])
        low_down = masked(low_down, adapters)
        out = jnp.zeros((slots, width), BF16)
        for h in range(ZH):
            at = ((zh + h) % ZH) * span
            part = dot(low_down, cut(b_down, at, span, 1))
            for k in range(Y):
                part = part + dot(hidden[k], down[(h, k)])
            part = part.astype(BF16)
            half = part.shape[0] // 2
            pair = part[:half].astype(F32) + send(part[half:], to_core).astype(F32)
            total = cut(hidden_state, at, span, 1) + pair[:piece]
            pair = pair.astype(BF16)
            for n, o in enumerate(others):
                total = total + send(pair[(n + 1) * piece : (n + 2) * piece], to_xz[o]).astype(F32)
            done = total.astype(BF16)
            held = {0: done}
            for k in range(1, Y):
                held[k] = send(done, from_y[k])
            for k in range(Y):
                there = send(held[k], to_core)
                row = ((y + k) % Y) * 2 * piece
                out = lax.dynamic_update_slice(out, held[k], (row + c * piece, at))
                out = lax.dynamic_update_slice(out, there, (row + (1 - c) * piece, at))
        return out

    return body


def solution(mesh):
    in_specs = (
        P("req", None),
        P("req", None),
        P("req", None),
        P("req", None, "tp"),
        P("tp", "req"),
        P("req", "tp"),
        P("req", "tp"),
        P("tp", "req"),
        P(),
        P(None, None, "tp"),
        P("tp", None),
        P(),
        P(),
        P(None, "tp"),
        P(),
        P(None, "tp"),
        P("tp", None),
        P(),
    )
    return jax.shard_map(
        make_body(mesh.shape["req"], mesh.shape["tp"]),
        mesh=mesh, in_specs=in_specs, out_specs=P("req", None), check_vma=False,
    )
```

```python
import functools
import math

import jax
import jax.numpy as jnp
from jax import lax
from jax.experimental import pallas as pl
from jax.experimental.pallas import tpu as pltpu
from jax.sharding import PartitionSpec as P

HD = 128
RANK = 16
AXES = ("req", "tp")
epsilon = 1e-05
rope_base = 10000.0
F32 = jnp.float32
BF16 = jnp.bfloat16
VM = pltpu.VMEM
PARAMS = pltpu.CompilerParams(vmem_limit_bytes=56 * 2**20)
COST = pl.CostEstimate(flops=1000, bytes_accessed=1000, transcendentals=0)


def dot(a, b):
    return jnp.dot(a, b, preferred_element_type=F32)


def layer_norm(values):
    row_mean = jnp.mean(values, axis=-1, keepdims=True)
    centred = values - row_mean
    spread = jnp.mean(centred * centred, axis=-1, keepdims=True)
    return (centred * lax.rsqrt(spread + epsilon)).astype(BF16)


def slot_layout(lengths_row, adapters_row, slot_count):
    request_ends = jnp.cumsum(lengths_row)
    request_starts = request_ends - lengths_row
    slot_index = jnp.arange(slot_count, dtype=jnp.int32)
    request_of = jnp.sum((slot_index[:, None] >= request_ends[None, :]).astype(jnp.int32), axis=1)
    member = request_of[:, None] == jnp.arange(lengths_row.shape[0], dtype=jnp.int32)[None, :]
    position = slot_index - jnp.sum(jnp.where(member, request_starts[None, :], 0), axis=1)
    adapter = jnp.sum(jnp.where(member, adapters_row[None, :], 0), axis=1)
    return (request_of, position, adapter)


def rope_tables(position):
    half = HD // 2
    frequency = jnp.exp(-math.log(rope_base) * 2.0 * jnp.arange(half, dtype=F32) / HD)
    angles = position.astype(F32)[:, None] * frequency[None, :]
    cosine, sine = jnp.cos(angles), jnp.sin(angles)
    return jnp.concatenate([cosine, cosine], 1), jnp.concatenate([-sine, sine], 1)


def masked(inner, adapter_column):
    rank = lax.broadcasted_iota(jnp.int32, inner.shape, 1) // RANK
    return jnp.where(adapter_column == rank, inner, F32(0.0)).astype(BF16)


def whole(array):
    return pl.BlockSpec(array.shape, lambda *_: (0,) * array.ndim, pipeline_mode=pl.Buffered(1))


def mm(start, size):
    return pl.ds(pl.multiple_of(start * size, size), size)


def qkv_kernel(blocks, half_tiles, rotated, order, x, low, b, cosine, sine, *refs):
    weights, out = refs[:-1], refs[-1]
    n = pl.program_id(0)
    size = x.shape[1] // blocks
    total = dot(low[...], b[...])
    for at in range(blocks):
        w = weights[2 * at][...]
        if weights[2 * at + 1] is not None:
            w = jnp.where(n < half_tiles, w, weights[2 * at + 1][...])
        total = total + dot(x[:, mm(order[at], size)], w)

    @pl.when(n < rotated)
    def _():
        for h in range(total.shape[1] // HD):
            v = total[:, h * HD : (h + 1) * HD]
            turned = v * cosine[...] + pltpu.roll(v, HD // 2, 1) * sine[...]
            out[:, h * HD : (h + 1) * HD] = turned.astype(BF16)

    @pl.when(n >= rotated)
    def _():
        out[...] = total.astype(BF16)


def project_qkv(x, low, b, cosine, sine, weights, order):
    slots, columns = x.shape[0], b.shape[1]
    tile = 256 if columns % 512 == 0 and columns % 768 == 0 else HD
    half = columns // 2 // tile
    specs, flat, kept = [], [], []
    for w in weights:
        size = w[0].shape[0]
        if len(w) == 1:
            specs.append(pl.BlockSpec((size, tile), lambda n, o: (0, n)))
            flat.append(w[0])
            kept += [True, False]
        else:
            specs.append(pl.BlockSpec((size, tile), lambda n, o: (0, jnp.minimum(n, half - 1))))
            specs.append(pl.BlockSpec((size, tile), lambda n, o: (0, jnp.maximum(n - half, 0))))
            flat += list(w)
            kept += [True, True]

    def kernel(order_ref, x_ref, low_ref, b_ref, cos_ref, sin_ref, *refs):
        it = iter(refs[:-1])
        spread = [next(it) if k else None for k in kept]
        qkv_kernel(
            len(weights), half, columns // 3 * 2 // tile,
            order_ref, x_ref, low_ref, b_ref, cos_ref, sin_ref, *spread, refs[-1],
        )

    return pl.pallas_call(
        kernel,
        grid_spec=pltpu.PrefetchScalarGridSpec(
            num_scalar_prefetch=1,
            grid=(columns // tile,),
            in_specs=[
                whole(x),
                whole(low),
                pl.BlockSpec((b.shape[0], tile), lambda n, o: (0, n)),
                whole(cosine),
                whole(sine),
                *specs,
            ],
            out_specs=pl.BlockSpec((slots, tile), lambda n, o: (0, n)),
        ),
        out_shape=jax.ShapeDtypeStruct((slots, columns), BF16),
        compiler_params=PARAMS,
        cost_estimate=COST,
        name="project_qkv",
    )(order, x, low, b, cosine, sine, *flat)


def attend(qkv, request_of):
    slots, heads = qkv.shape[0], qkv.shape[1] // 3 // HD
    rows = 256 if slots % 256 == 0 else slots
    column, line = request_of[:, None], request_of[None, :]

    def kernel(q, k, v, column_ref, line_ref, out):
        for at in range(0, slots, rows):
            seen = at + rows
            s = lax.dot_general(
                q[at:seen], k[:seen], (((1,), (1,)), ((), ())), preferred_element_type=F32
            )
            s = s * (1.0 / math.sqrt(HD))
            here = at + lax.broadcasted_iota(jnp.int32, s.shape, 0)
            there = lax.broadcasted_iota(jnp.int32, s.shape, 1)
            allowed = (column_ref[at:seen] == line_ref[:, :seen]) & (here >= there)
            s = jnp.where(allowed, s, F32(-1e30))
            e = jnp.exp(s - jnp.max(s, axis=1, keepdims=True))
            weights = (e * (1.0 / jnp.sum(e, axis=1, keepdims=True))).astype(BF16)
            out[at:seen] = dot(weights, v[:seen]).astype(BF16)

    return pl.pallas_call(
        kernel,
        grid=(heads,),
        in_specs=[
            pl.BlockSpec((slots, HD), lambda h: (0, h)),
            pl.BlockSpec((slots, HD), lambda h: (0, heads + h)),
            pl.BlockSpec((slots, HD), lambda h: (0, 2 * heads + h)),
            whole(column),
            whole(line),
        ],
        out_specs=pl.BlockSpec((slots, HD), lambda h: (0, h)),
        out_shape=jax.ShapeDtypeStruct((slots, heads * HD), BF16),
        compiler_params=PARAMS,
        cost_estimate=COST,
        name="attend",
    )(qkv, qkv, qkv, column, line)


def project_out(attn, adapter, a, b, weights, order, row_order, chunks):
    slots, width = attn.shape[0], b.shape[1]
    size, n = width // len(weights), len(weights)
    piece = slots // row_order.shape[0]
    flat = [p for w in weights for p in w]
    column = adapter[:, None]
    shape = jax.ShapeDtypeStruct((slots // 2, width // chunks), BF16)

    def kernel(order_ref, rows_ref, attn_ref, adapter_ref, a_ref, b_ref, *refs):
        ws, outs, rows, low = refs[: len(flat)], refs[len(flat) : -2], refs[-2], refs[-1]
        for q in range(row_order.shape[0]):
            here = mm(rows_ref[q], piece)
            part = attn_ref[here, :]
            rows[q * piece : (q + 1) * piece] = part
            low[q * piece : (q + 1) * piece] = masked(dot(part, a_ref[...]), adapter_ref[here, :])
        it = iter(ws)
        for at, w in enumerate(weights):
            total = dot(low[...], b_ref[:, mm(order_ref[at], size)])
            start = 0
            for p in w:
                total = total + dot(rows[:, start : start + p.shape[0]], next(it)[...])
                start += p.shape[0]
            total = total.astype(BF16)
            chunk, place = divmod(at, n // chunks)
            to = slice(place * size, (place + 1) * size)
            outs[2 * chunk][:, to] = total[: slots // 2]
            outs[2 * chunk + 1][:, to] = total[slots // 2 :]

    smem = pl.BlockSpec(memory_space=pltpu.SMEM)
    out = pl.pallas_call(
        kernel,
        in_specs=[smem, smem] + [pl.BlockSpec(memory_space=VM)] * (4 + len(flat)),
        out_specs=[pl.BlockSpec(memory_space=VM)] * (2 * chunks),
        out_shape=[shape] * (2 * chunks),
        scratch_shapes=[VM(attn.shape, BF16), VM((slots, a.shape[1]), BF16)],
        compiler_params=PARAMS,
        cost_estimate=COST,
        name="project_out",
    )(order, row_order, attn, column, a, b, *flat)
    return [(out[2 * i], out[2 * i + 1]) for i in range(chunks)]


def residual_norm(tokens, row, order, chunks):
    width, n = tokens.shape[1], order.shape[0]
    piece, size = chunks[0][-1].shape[0], width // n
    flat = [p for c in chunks for p in c]
    per = n // len(chunks)

    def kernel(row_ref, order_ref, tok_ref, *refs):
        parts, hidden, normed = refs[: len(flat)], refs[-2], refs[-1]
        it = iter(parts)
        for c, group in enumerate(chunks):
            total = None
            for _ in group:
                p = next(it)[...].astype(F32)
                total = p if total is None else total + p
            for place in range(per):
                to = mm(order_ref[c * per + place], size)
                hidden[:, to] = tok_ref[:, to].astype(F32) + total[:, place * size : (place + 1) * size]
        normed[...] = layer_norm(hidden[...])

    return pl.pallas_call(
        kernel,
        grid_spec=pltpu.PrefetchScalarGridSpec(
            num_scalar_prefetch=2,
            grid=(1,),
            in_specs=[
                pl.BlockSpec((piece, width), lambda n, r, o: (r[0], 0)),
                *[pl.BlockSpec((piece, p.shape[1]), lambda n, r, o: (0, 0)) for p in flat],
            ],
            out_specs=[pl.BlockSpec((piece, width), lambda n, r, o: (0, 0))] * 2,
        ),
        out_shape=[
            jax.ShapeDtypeStruct((piece, width), F32),
            jax.ShapeDtypeStruct((piece, width), BF16),
        ],
        compiler_params=PARAMS,
        cost_estimate=COST,
        name="residual_norm",
    )(row, order, tokens, *flat)


def gated(rows, adapters, a_gate, a_up, sets, order):
    piece, width = rows[0].shape
    total_rows = piece * len(rows)
    n_blocks = len(sets[0][0])
    size = width // n_blocks
    units = sets[0][1].shape[1] // 2
    tile = min(256, units)
    tiles = units // tile
    rank = a_gate.shape[1]
    column = adapters[:, None]
    flat = [w for s in sets for w in s[0]]
    bs = [s[1] for s in sets]
    downs = [s[2] for s in sets]
    n_rows, n_sets = len(rows), len(sets)
    steps = n_sets * tiles
    chunk = total_rows // 4 if total_rows % 64 == 0 else total_rows

    def kernel(order_ref, adapter_ref, ag_ref, au_ref, *refs):
        it = iter(refs)
        take = lambda k: [next(it) for _ in range(k)]
        x_in, w_in, b_in, d_in = take(n_rows), take(len(flat)), take(n_sets), take(n_sets)
        hidden, low_out, x, w, bb, lg, lu, ld, x_sem, w_sem, b_sem = take(11)

        def weight_copies(step, slot):
            s, t = divmod(step, tiles)
            for at in range(n_blocks):
                for g in range(2):
                    yield pltpu.make_async_copy(
                        w_in[s * n_blocks + at].at[:, pl.ds(g * units + t * tile, tile)],
                        w.at[slot, g, mm(order_ref[at], size), :],
                        w_sem.at[slot, g, at],
                    )
            for g in range(2):
                yield pltpu.make_async_copy(
                    b_in[s].at[:, pl.ds(g * units + t * tile, tile)],
                    bb.at[slot, g],
                    b_sem.at[slot, g],
                )

        x_copies = [
            pltpu.make_async_copy(x_in[i], x.at[pl.ds(i * piece, piece), :], x_sem.at[i])
            for i in range(n_rows)
        ]
        for copy in weight_copies(0, 0):
            copy.start()
        for copy in x_copies:
            copy.start()
        for copy in x_copies:
            copy.wait()
        for step in range(steps):
            slot = step % 2
            if step + 1 < steps:
                for copy in weight_copies(step + 1, 1 - slot):
                    copy.start()
            for copy in weight_copies(step, slot):
                copy.wait()
            s, t = divmod(step, tiles)

            @pl.loop(0, total_rows // chunk)
            def _(m):
                at = mm(m, chunk)
                xs = x[at, :]
                if step == 0:
                    lg[at, :] = masked(dot(xs, ag_ref[...]), adapter_ref[at, :])
                    lu[at, :] = masked(dot(xs, au_ref[...]), adapter_ref[at, :])
                gate = dot(xs, w[slot, 0]) + dot(lg[at, :], bb[slot, 0])
                up = dot(xs, w[slot, 1]) + dot(lu[at, :], bb[slot, 1])
                h = (gate / (1.0 + jnp.exp(-gate)) * up).astype(BF16)
                hidden[at, step * tile : (step + 1) * tile] = h
                more = dot(h, d_in[s][t * tile : (t + 1) * tile, :])
                if step == 0:
                    ld[at, :] = more
                else:
                    ld[at, :] = ld[at, :] + more
                if step == steps - 1:
                    low_out[at, :] = masked(ld[at, :], adapter_ref[at, :])

    smem = pl.BlockSpec(memory_space=pltpu.SMEM)
    vmem = pl.BlockSpec(memory_space=VM)
    hbm = pl.BlockSpec(memory_space=pl.ANY)
    return pl.pallas_call(
        kernel,
        in_specs=[smem, vmem, vmem, vmem]
        + [hbm] * (n_rows + len(flat) + n_sets)
        + [vmem] * n_sets,
        out_specs=[vmem, vmem],
        out_shape=[
            jax.ShapeDtypeStruct((total_rows, n_sets * units), BF16),
            jax.ShapeDtypeStruct((total_rows, rank), BF16),
        ],
        scratch_shapes=[
            VM((total_rows, width), BF16),
            VM((2, 2, width, tile), BF16),
            VM((2, 2, rank, tile), BF16),
            VM((total_rows, rank), BF16),
            VM((total_rows, rank), BF16),
            VM((total_rows, rank), F32),
            pltpu.SemaphoreType.DMA((n_rows,)),
            pltpu.SemaphoreType.DMA((2, 2, n_blocks)),
            pltpu.SemaphoreType.DMA((2, 2)),
        ],
        compiler_params=PARAMS,
        cost_estimate=COST,
        name="gated",
    )(order, column, a_gate, a_up, *rows, *flat, *bs, *downs)


def project_down(hidden, low, b, blocks, order):
    total_rows = hidden.shape[0]
    flat = [w for block in blocks for w in block]
    units, size = flat[0].shape
    half = total_rows // 2
    chunk = half // 2 if half % 32 == 0 else half

    def kernel(order_ref, h_ref, low_ref, b_ref, *refs):
        ws, outs = refs[: len(flat)], refs[len(flat) :]
        for at, block in enumerate(blocks):
            to = mm(order_ref[at], size)
            for o in range(2):

                @pl.loop(0, half // chunk)
                def _(m):
                    here = mm(m + o * (half // chunk), chunk)
                    total = dot(low_ref[here, :], b_ref[:, to])
                    for k in range(len(block)):
                        w = ws[at * len(block) + k][...]
                        total = total + dot(h_ref[here, k * units : (k + 1) * units], w)
                    outs[o][mm(m, chunk), to] = total.astype(BF16)

    smem = pl.BlockSpec(memory_space=pltpu.SMEM)
    vmem = pl.BlockSpec(memory_space=VM)
    return pl.pallas_call(
        kernel,
        in_specs=[smem] + [vmem] * (3 + len(flat)),
        out_specs=[vmem, vmem],
        out_shape=[jax.ShapeDtypeStruct((half, b.shape[1]), BF16)] * 2,
        compiler_params=PARAMS,
        cost_estimate=COST,
        name="project_down",
    )(order, hidden, low, b, *flat)


def assemble(pieces, places, shape):
    rows, columns = pieces[0].shape

    def kernel(places_ref, *refs):
        parts, out, sems = refs[: len(pieces)], refs[-2], refs[-1]
        copies = [
            pltpu.make_async_copy(
                parts[i],
                out.at[mm(places_ref[2 * i], rows), mm(places_ref[2 * i + 1], columns)],
                sems.at[i],
            )
            for i in range(len(pieces))
        ]
        for copy in copies:
            copy.start()
        for copy in copies:
            copy.wait()

    hbm = pl.BlockSpec(memory_space=pl.ANY)
    return pl.pallas_call(
        kernel,
        in_specs=[pl.BlockSpec(memory_space=pltpu.SMEM)] + [hbm] * len(pieces),
        out_specs=hbm,
        out_shape=jax.ShapeDtypeStruct(shape, BF16),
        scratch_shapes=[pltpu.SemaphoreType.DMA((len(pieces),))],
        compiler_params=PARAMS,
        cost_estimate=COST,
        name="assemble",
    )(places, *pieces)


def make_body(R, T):
    Z, ZH, Y = R // 2, R // 4, T // 2

    def move(f):
        pairs = []
        for r in range(R):
            for t in range(T):
                z, x, y, c = f(r // 2, r % 2, t // 2, t % 2)
                pairs.append((r * T + t, (z * 2 + x) * T + y * 2 + c))
        return pairs

    def send(value, pairs, after=()):
        if after:
            value = lax.optimization_barrier((value, *after))[0]
        return lax.ppermute(value, AXES, pairs)

    to_core = move(lambda z, x, y, c: (z, x, y, 1 - c))
    to_x = move(lambda z, x, y, c: (z, 1 - x, y, c))
    to_xz = {}
    for i in (0, 1):
        for j in (0, 1):
            to_xz[(i, j)] = move(lambda z, x, y, c, i=i, j=j: (z ^ j, x ^ i, y, c))
    z_up = move(lambda z, x, y, c: ((z + 1) % Z, x, y, c))
    z_down = move(lambda z, x, y, c: ((z - 1) % Z, x, y, c))
    from_y = {k: move(lambda z, x, y, c, k=k: (z, x, (y - k) % Y, c)) for k in range(1, Y)}
    from_zh = {
        k: move(lambda z, x, y, c, k=k: ((z - 2 * k) % Z, x, y, c)) for k in range(1, ZH)
    }
    near = [(0, 0), (1, 0), (0, 1), (1, 1)]
    others = near[1:]

    def ring(own, halve, after=()):
        got, left, right = {0: (own,)}, own, own
        if after:
            left = right = lax.optimization_barrier((own, *after))[0]
        for k in range(1, Z // 2):
            left, right = send(left, z_up), send(right, z_down)
            got[Z - k], got[k] = (left,), (right,)
        first, second = halve(left)[0], halve(right)[1]
        got[Z // 2] = (send(first, z_up), send(second, z_down))
        return got

    def body(
        tokens, lengths, request_adapter, w_qkv, w_out, w_gate, w_up, w_down,
        a_qkv, b_qkv, a_out, b_out, a_gate, b_gate, a_up, b_up, a_down, b_down,
    ):
        r, t = lax.axis_index("req"), lax.axis_index("tp")
        z, x, y, c = r // 2, r % 2, t // 2, t % 2
        zh, zl = z // 2, z % 2
        slots, width = tokens.shape
        piece = slots // T
        block = width // R
        local = w_qkv.shape[2]
        rank_all = a_qkv.shape[1]
        quarter = w_gate.shape[1] // 4
        span = width // ZH

        def cut(array, start, size, axis):
            return lax.dynamic_slice_in_dim(array, start, size, axis)

        def ints(values):
            return jnp.stack([jnp.asarray(v, jnp.int32) for v in values])

        def columns_halved(w):
            return w[:, : w.shape[1] // 2], w[:, w.shape[1] // 2 :]

        def rows_halved(w):
            return w[: w.shape[0] // 2], w[w.shape[0] // 2 :]

        qkv_got = ring(w_qkv.reshape(block, 3 * local), columns_halved)
        qkv_swapped = {}
        for k in [0, *[k for k in range(1, Z) if k != Z // 2], Z // 2]:
            qkv_swapped[k] = tuple(send(w, to_x) for w in qkv_got[k])
        qkv_weights = [w for k in range(Z) for w in (qkv_got[k], qkv_swapped[k])]
        order = ints([((z + k) % Z) * 2 + (x ^ i) for k in range(Z) for i in (0, 1)])

        out_got = ring(w_out, rows_halved, after=[qkv_got[1][0], qkv_got[Z - 1][0]])
        out_swapped = {k: tuple(send(w, to_x) for w in out_got[k]) for k in range(Z)}
        out_weights = [w for k in range(Z) for w in (out_got[k], out_swapped[k])]

        mine = (zl * 2 + x) * quarter
        gu, down = {}, {}
        for i, j in near:
            at = ((zl ^ j) * 2 + (x ^ i)) * quarter
            pair = [cut(w, at, quarter, 1) for w in (w_gate, w_up)]
            gu[(i, j, 0, 0)] = jnp.concatenate(pair, axis=1)
            down[(i, j, 0, 0)] = cut(w_down, at, quarter, 0)
        b_own = jnp.concatenate(
            [cut(b_gate, mine, quarter, 1), cut(b_up, mine, quarter, 1)], axis=1
        )
        a_down_own = cut(a_down, mine, quarter, 0)
        for o in others:
            gu[(*o, 0, 0)] = send(gu[(*o, 0, 0)], to_xz[o])
        for o in others:
            down[(*o, 0, 0)] = send(down[(*o, 0, 0)], to_xz[o])
        b_gu, a_dn = [b_own], [a_down_own]
        for k in range(1, Y):
            b_gu.append(send(b_own, from_y[k]))
            a_dn.append(send(a_down_own, from_y[k]))
        for held in (gu, down):
            for k in range(1, Y):
                for o in near:
                    held[(*o, 0, k)] = send(held[(*o, 0, 0)], from_y[k])
            for h in range(1, ZH):
                for o in near:
                    held[(*o, h, 0)] = send(held[(*o, 0, 0)], from_zh[h])
                    for k in range(1, Y):
                        held[(*o, h, k)] = send(held[(*o, h, 0)], from_y[k])

        request_of, position, adapter = slot_layout(lengths[0], request_adapter[0], slots)
        near_adapters = [adapter] + [send(adapter, to_xz[o]) for o in others]
        cosine, sine = rope_tables(position)
        normed = layer_norm(tokens.astype(F32))
        column_adapter = jnp.arange(rank_all, dtype=jnp.int32) // RANK
        chosen = adapter[:, None] == column_adapter[None, :]
        low = jnp.where(chosen, dot(normed, a_qkv), F32(0.0)).astype(BF16)
        qkv = project_qkv(
            normed, low, b_qkv.reshape(rank_all, 3 * local), cosine, sine, qkv_weights, order
        )
        attn = attend(qkv, request_of)
        row_order = ints([((y - k) % Y) * 2 + s for s in (c, 1 - c) for k in range(Y)])
        sums = []
        for keep, give in project_out(
            attn, adapter, a_out, b_out, out_weights, order, row_order, 2
        ):
            came = send(give, to_core)
            parts = [keep, came]
            for k in range(1, Y):
                rows = slice(k * piece, (k + 1) * piece)
                pair = (keep[rows].astype(F32) + came[rows].astype(F32)).astype(BF16)
                parts.append(send(pair, from_y[k]))
            sums.append(parts)
        hidden_state, normed2 = residual_norm(tokens, ints([t]), order, sums)

        rows = [normed2] + [send(normed2, to_xz[o]) for o in others]
        rows = rows + [send(row, to_core) for row in rows]
        adapters = jnp.stack(near_adapters)
        adapters = jnp.concatenate(
            [cut(adapters, (y * 2 + (c ^ s)) * piece, piece, 1).reshape(-1) for s in (0, 1)]
        )
        keys = [(*o, h) for h in range(ZH) for o in near]
        gu_order = ints([((zh + h) % ZH) * 4 + (zl ^ j) * 2 + (x ^ i) for i, j, h in keys])
        sets = [([gu[(*key, k)] for key in keys], b_gu[k], a_dn[k]) for k in range(Y)]
        hidden, low_down = gated(rows, adapters, a_gate, a_up, sets, gu_order)
        down_order = ints([(zl ^ j) * 2 + (x ^ i) for i, j in near])
        pieces, places = [], []
        for h in range(ZH):
            at = ((zh + h) % ZH) * span
            blocks = [[down[(*o, h, k)] for k in range(Y)] for o in near]
            keep, give = project_down(hidden, low_down, cut(b_down, at, span, 1), blocks, down_order)
            came = send(give, to_core)
            total = cut(hidden_state, at, span, 1)
            total = total + keep[:piece].astype(F32) + came[:piece].astype(F32)
            for n, o in enumerate(others):
                part = slice((n + 1) * piece, (n + 2) * piece)
                pair = (keep[part].astype(F32) + came[part].astype(F32)).astype(BF16)
                total = total + send(pair, to_xz[o]).astype(F32)
            done = total.astype(BF16)
            for k in range(Y):
                here = done if k == 0 else send(done, from_y[k])
                for s, got in ((0, here), (1, send(here, to_core))):
                    pieces.append(got)
                    places += [((y + k) % Y) * 2 + (c ^ s), (zh + h) % ZH]
        return assemble(pieces, ints(places), tokens.shape)

    return body


def solution(mesh):
    in_specs = (
        P("req", None),
        P("req", None),
        P("req", None),
        P("req", None, "tp"),
        P("tp", "req"),
        P("req", "tp"),
        P("req", "tp"),
        P("tp", "req"),
        P(),
        P(None, None, "tp"),
        P("tp", None),
        P(),
        P(),
        P(None, "tp"),
        P(),
        P(None, "tp"),
        P("tp", None),
        P(),
    )
    return jax.shard_map(
        make_body(mesh.shape["req"], mesh.shape["tp"]),
        mesh=mesh, in_specs=in_specs, out_specs=P("req", None), check_vma=False,
    )
```

```python
import functools
import math

import jax
import jax.numpy as jnp
from jax import lax
from jax.experimental import pallas as pl
from jax.experimental.pallas import tpu as pltpu
from jax.sharding import PartitionSpec as P

HD = 128
RANK = 16
AXES = ("req", "tp")
epsilon = 1e-05
rope_base = 10000.0
F32 = jnp.float32
BF16 = jnp.bfloat16
VM = pltpu.VMEM
PARAMS = pltpu.CompilerParams(vmem_limit_bytes=56 * 2**20)
COST = pl.CostEstimate(flops=1000, bytes_accessed=1000, transcendentals=0)


def dot(a, b):
    return jnp.dot(a, b, preferred_element_type=F32)


def layer_norm(values):
    row_mean = jnp.mean(values, axis=-1, keepdims=True)
    centred = values - row_mean
    spread = jnp.mean(centred * centred, axis=-1, keepdims=True)
    return (centred * lax.rsqrt(spread + epsilon)).astype(BF16)


def slot_layout(lengths_row, adapters_row, slot_count):
    request_ends = jnp.cumsum(lengths_row)
    request_starts = request_ends - lengths_row
    slot_index = jnp.arange(slot_count, dtype=jnp.int32)
    request_of = jnp.sum((slot_index[:, None] >= request_ends[None, :]).astype(jnp.int32), axis=1)
    member = request_of[:, None] == jnp.arange(lengths_row.shape[0], dtype=jnp.int32)[None, :]
    position = slot_index - jnp.sum(jnp.where(member, request_starts[None, :], 0), axis=1)
    adapter = jnp.sum(jnp.where(member, adapters_row[None, :], 0), axis=1)
    return (request_of, position, adapter)


def rope_tables(position):
    half = HD // 2
    frequency = jnp.exp(-math.log(rope_base) * 2.0 * jnp.arange(half, dtype=F32) / HD)
    angles = position.astype(F32)[:, None] * frequency[None, :]
    cosine, sine = jnp.cos(angles), jnp.sin(angles)
    return jnp.concatenate([cosine, cosine], 1), jnp.concatenate([-sine, sine], 1)


def masked(inner, adapter_column):
    rank = lax.broadcasted_iota(jnp.int32, inner.shape, 1) // RANK
    return jnp.where(adapter_column == rank, inner, F32(0.0)).astype(BF16)


def whole(array):
    return pl.BlockSpec(array.shape, lambda *_: (0,) * array.ndim, pipeline_mode=pl.Buffered(1))


def mm(start, size):
    return pl.ds(pl.multiple_of(start * size, size), size)


def dma(source, target, semaphore):
    return pltpu.make_async_copy(source, target, semaphore)


def run_all(copies):
    for copy in copies:
        copy.start()
    for copy in copies:
        copy.wait()


SMEM_SPEC = pl.BlockSpec(memory_space=pltpu.SMEM)
VMEM_SPEC = pl.BlockSpec(memory_space=VM)
HBM_SPEC = pl.BlockSpec(memory_space=pl.ANY)


def project_qkv(own, pieces, adapter, a, b, cosine, sine, weights, places):
    slots, width = own.shape
    total_rows, columns, rank = 2 * slots, b.shape[1], b.shape[0]
    piece, size, tile = pieces[0].shape[0], width // len(weights), columns // 3
    n_pieces, n_weights = len(pieces), len(weights)
    chunk = total_rows // 4
    column = adapter[:, None]

    def kernel(at_ref, adapter_ref, a_ref, cos_ref, sin_ref, own_ref, b_ref, *refs):
        p_in, w_in, rest = refs[:n_pieces], refs[n_pieces : n_pieces + n_weights], refs[-7:]
        out, x, w, bb, low, x_sem, w_sem = rest

        def weight_copies(step, slot):
            to = pl.ds(step * tile, tile)
            for i in range(n_weights):
                yield dma(
                    w_in[i].at[:, to],
                    w.at[slot, mm(at_ref[1 + n_pieces + i], size), :],
                    w_sem.at[slot, i],
                )
            yield dma(b_ref.at[:, to], bb.at[slot], w_sem.at[slot, n_weights])

        x_copies = [dma(own_ref, x.at[mm(at_ref[0], slots), :], x_sem.at[n_pieces])]
        for i in range(n_pieces):
            x_copies.append(dma(p_in[i], x.at[mm(at_ref[1 + i], piece), :], x_sem.at[i]))
        for copy in x_copies:
            copy.start()
        for copy in weight_copies(0, 0):
            copy.start()
        for copy in x_copies:
            copy.wait()
        for step in range(3):
            slot = step % 2
            if step < 2:
                for copy in weight_copies(step + 1, 1 - slot):
                    copy.start()
            for copy in weight_copies(step, slot):
                copy.wait()

            @pl.loop(0, total_rows // chunk)
            def _(m):
                at = mm(m, chunk)
                xs = x[at, :]
                if step == 0:
                    low[at, :] = masked(dot(xs, a_ref[...]), adapter_ref[at, :])
                total = dot(xs, w[slot]) + dot(low[at, :], bb[slot])
                for h in range(tile // HD):
                    v = total[:, h * HD : (h + 1) * HD]
                    if step < 2:
                        v = v * cos_ref[at, :] + pltpu.roll(v, HD // 2, 1) * sin_ref[at, :]
                    start = step * tile + h * HD
                    out[at, start : start + HD] = v.astype(BF16)

    return pl.pallas_call(
        kernel,
        in_specs=[SMEM_SPEC] + [VMEM_SPEC] * 4 + [HBM_SPEC] * (2 + n_pieces + n_weights),
        out_specs=VMEM_SPEC,
        out_shape=jax.ShapeDtypeStruct((total_rows, columns), BF16),
        scratch_shapes=[
            VM((total_rows, width), BF16),
            VM((2, width, tile), BF16),
            VM((2, rank, tile), BF16),
            VM((total_rows, rank), BF16),
            pltpu.SemaphoreType.DMA((n_pieces + 1,)),
            pltpu.SemaphoreType.DMA((2, n_weights + 1)),
        ],
        compiler_params=PARAMS,
        cost_estimate=COST,
        name="project_qkv",
    )(places, column, a, cosine, sine, own, b, *pieces, *weights)


def attend(qkv, request_of):
    indices, slots = request_of.shape
    heads = qkv.shape[1] // 3 // HD
    rows = 256 if slots % 256 == 0 else slots
    column, line = request_of[:, :, None], request_of[:, None, :]

    def kernel(q, k, v, column_ref, line_ref, out):
        for at in range(0, slots, rows):
            seen = at + rows
            s = lax.dot_general(
                q[at:seen], k[:seen], (((1,), (1,)), ((), ())), preferred_element_type=F32
            )
            s = s * (1.0 / math.sqrt(HD))
            here = at + lax.broadcasted_iota(jnp.int32, s.shape, 0)
            there = lax.broadcasted_iota(jnp.int32, s.shape, 1)
            allowed = (column_ref[0, at:seen] == line_ref[0, :, :seen]) & (here >= there)
            s = jnp.where(allowed, s, F32(-1e30))
            e = jnp.exp(s - jnp.max(s, axis=1, keepdims=True))
            weights = (e * (1.0 / jnp.sum(e, axis=1, keepdims=True))).astype(BF16)
            out[at:seen] = dot(weights, v[:seen]).astype(BF16)

    return pl.pallas_call(
        kernel,
        grid=(indices, heads),
        in_specs=[
            pl.BlockSpec((slots, HD), lambda i, h: (i, h)),
            pl.BlockSpec((slots, HD), lambda i, h: (i, heads + h)),
            pl.BlockSpec((slots, HD), lambda i, h: (i, 2 * heads + h)),
            pl.BlockSpec((1, slots, 1), lambda i, h: (i, 0, 0)),
            pl.BlockSpec((1, 1, slots), lambda i, h: (i, 0, 0)),
        ],
        out_specs=pl.BlockSpec((slots, HD), lambda i, h: (i, h)),
        out_shape=jax.ShapeDtypeStruct((indices * slots, heads * HD), BF16),
        compiler_params=PARAMS,
        cost_estimate=COST,
        name="attend",
    )(qkv, qkv, qkv, column, line)


def project_out(attn, adapter, a, b, weights, order, scalars, T, chunks):
    total_rows, depth = attn.shape
    width = b.shape[1]
    n, slots, piece = len(weights), total_rows // 2, total_rows // 2 // T
    size = width // n // 2
    flat = [p for w in weights for p in w]
    column = adapter[:, None]
    half = total_rows // 2
    shape = jax.ShapeDtypeStruct((half, width // chunks), BF16)

    def kernel(order_ref, at_ref, attn_ref, adapter_ref, a_ref, b_ref, *refs):
        ws, outs = refs[: len(flat)], refs[len(flat) : -2]
        rows, low = refs[-2:]
        x, c = at_ref[0], at_ref[1]
        mine = a_ref[mm(x, depth), :]
        for s in range(2):
            side = c if s == 0 else 1 - c
            for xa in range(2):
                for ya in range(T // 2):
                    here = mm(xa * T + ya * 2 + side, piece)
                    to = s * half + (xa * (T // 2) + ya) * piece
                    part = attn_ref[here, :]
                    rows[to : to + piece] = part
                    low[to : to + piece] = masked(dot(part, mine), adapter_ref[here, :])
        it = iter(ws)
        for k, w in enumerate(weights):
            blocks = []
            for p in w:
                ref = next(it)
                for start in range(0, p.shape[1], size):
                    blocks.append((ref, start))
            chunk, place = divmod(k, n // chunks)
            for i, (ref, start) in enumerate(blocks):
                there = mm(order_ref[2 * k + i], size)
                to = mm(place * 2 + (x ^ i), size)
                for s in range(2):
                    these = slice(s * half, (s + 1) * half)
                    total = dot(rows[these], ref[:, start : start + size])
                    total = total + dot(low[these], b_ref[:, there])
                    outs[2 * chunk + s][:, to] = total.astype(BF16)

    out = pl.pallas_call(
        kernel,
        in_specs=[SMEM_SPEC, SMEM_SPEC] + [VMEM_SPEC] * (4 + len(flat)),
        out_specs=[VMEM_SPEC] * (2 * chunks),
        out_shape=[shape] * (2 * chunks),
        scratch_shapes=[VM(attn.shape, BF16), VM((total_rows, a.shape[1]), BF16)],
        compiler_params=PARAMS,
        cost_estimate=COST,
        name="project_out",
    )(order, scalars, attn, column, a, b, *flat)
    return [(out[2 * i], out[2 * i + 1]) for i in range(chunks)]


def residual_norm(tokens, row, order, chunks, T):
    slots, width = tokens.shape
    n = order.shape[0]
    piece, size, per = slots // T, width // n, n // len(chunks)

    def kernel(row_ref, order_ref, tok_ref, *refs):
        parts, hidden, normed = refs[:-2], refs[-2], refs[-1]
        for c, part in enumerate(parts):
            total = part[:piece].astype(F32)
            for k in range(1, part.shape[0] // piece):
                total = total + part[k * piece : (k + 1) * piece].astype(F32)
            for place in range(per):
                to = mm(order_ref[c * per + place], size)
                more = total[:, place * size : (place + 1) * size]
                hidden[:, to] = tok_ref[:, to].astype(F32) + more
        normed[...] = layer_norm(hidden[...])

    return pl.pallas_call(
        kernel,
        grid_spec=pltpu.PrefetchScalarGridSpec(
            num_scalar_prefetch=2,
            grid=(1,),
            in_specs=[
                pl.BlockSpec((piece, width), lambda n, r, o: (r[0], 0)),
                *[pl.BlockSpec(p.shape, lambda n, r, o: (0, 0)) for p in chunks],
            ],
            out_specs=[pl.BlockSpec((piece, width), lambda n, r, o: (0, 0))] * 2,
        ),
        out_shape=[
            jax.ShapeDtypeStruct((piece, width), F32),
            jax.ShapeDtypeStruct((piece, width), BF16),
        ],
        compiler_params=PARAMS,
        cost_estimate=COST,
        name="residual_norm",
    )(row, order, tokens, *chunks)


def gated(rows, adapters, a_gate, a_up, sets, places):
    width = rows[0].shape[1]
    half = rows[0].shape[0]
    total_rows = half * len(rows)
    units = sets[0][1].shape[1] // 2
    tile = min(256, units)
    tiles = units // tile
    rank = a_gate.shape[1]
    column = adapters[:, None]
    flat = [w for s in sets for w in s[0]]
    first = [sum(len(s[0]) for s in sets[:k]) for k in range(len(sets) + 1)]
    bs = [s[1] for s in sets]
    downs = [s[2] for s in sets]
    n_rows, n_sets = len(rows), len(sets)
    most = max(len(s[0]) for s in sets)
    steps = n_sets * tiles
    chunk = total_rows // 4
    hidden_width = n_sets * units

    def kernel(place_ref, adapter_ref, ag_ref, au_ref, *refs):
        it = iter(refs)
        take = lambda k: [next(it) for _ in range(k)]
        x_in, w_in, b_in, d_in = take(n_rows), take(len(flat)), take(n_sets), take(n_sets)
        hidden, x, w, bb, lg, lu, ld, x_sem, w_sem, b_sem = take(10)

        def weight_copies(step, slot):
            s, t = divmod(step, tiles)
            for g in range(2):
                for i in range(first[s], first[s + 1]):
                    yield dma(
                        w_in[i].at[:, pl.ds(g * units + t * tile, tile)],
                        w.at[slot, g, mm(place_ref[i], flat[i].shape[0]), :],
                        w_sem.at[slot, g, i - first[s]],
                    )
                yield dma(
                    b_in[s].at[:, pl.ds(g * units + t * tile, tile)],
                    bb.at[slot, g],
                    b_sem.at[slot, g],
                )

        x_copies = [dma(x_in[i], x.at[pl.ds(i * half, half), :], x_sem.at[i]) for i in range(n_rows)]
        for copy in x_copies:
            copy.start()
        for copy in weight_copies(0, 0):
            copy.start()
        for copy in x_copies:
            copy.wait()
        for step in range(steps):
            slot = step % 2
            if step + 1 < steps:
                for copy in weight_copies(step + 1, 1 - slot):
                    copy.start()
            for copy in weight_copies(step, slot):
                copy.wait()
            s, t = divmod(step, tiles)

            @pl.loop(0, total_rows // chunk)
            def _(m):
                at = mm(m, chunk)
                xs = x[at, :]
                if step == 0:
                    lg[at, :] = masked(dot(xs, ag_ref[...]), adapter_ref[at, :])
                    lu[at, :] = masked(dot(xs, au_ref[...]), adapter_ref[at, :])
                gate = dot(xs, w[slot, 0]) + dot(lg[at, :], bb[slot, 0])
                up = dot(xs, w[slot, 1]) + dot(lu[at, :], bb[slot, 1])
                h = (gate / (1.0 + jnp.exp(-gate)) * up).astype(BF16)
                hidden[at, step * tile : (step + 1) * tile] = h
                more = dot(h, d_in[s][t * tile : (t + 1) * tile, :])
                if step > 0:
                    more = more + ld[at, :]
                if step < steps - 1:
                    ld[at, :] = more
                else:
                    hidden[at, hidden_width:] = masked(more, adapter_ref[at, :])

    return pl.pallas_call(
        kernel,
        in_specs=[SMEM_SPEC] + [VMEM_SPEC] * 3
        + [HBM_SPEC] * (n_rows + len(flat) + n_sets)
        + [VMEM_SPEC] * n_sets,
        out_specs=VMEM_SPEC,
        out_shape=jax.ShapeDtypeStruct((total_rows, hidden_width + rank), BF16),
        scratch_shapes=[
            VM((total_rows, width), BF16),
            VM((2, 2, width, tile), BF16),
            VM((2, 2, rank, tile), BF16),
            VM((total_rows, rank), BF16),
            VM((total_rows, rank), BF16),
            VM((total_rows, rank), F32),
            pltpu.SemaphoreType.DMA((n_rows,)),
            pltpu.SemaphoreType.DMA((2, 2, most)),
            pltpu.SemaphoreType.DMA((2, 2)),
        ],
        compiler_params=PARAMS,
        cost_estimate=COST,
        name="gated",
    )(places, column, a_gate, a_up, *rows, *flat, *bs, *downs)


def project_down(hidden, b, sets, units, scalars):
    total_rows, depth = hidden.shape
    half = total_rows // 2
    rank = b.shape[0]
    size = sets[0].shape[1]
    n = 4
    n_sets = len(sets)
    chunk = half // 2

    def kernel(at_ref, h_ref, b_ref, *refs):
        w_in, outs, w, sems = refs[:n_sets], refs[n_sets : n_sets + 2], refs[-2], refs[-1]
        copies = [
            dma(
                b_ref.at[:, mm(at_ref[0], n * size)],
                w.at[n_sets * units : n_sets * units + rank, :],
                sems.at[n_sets * n],
            )
        ]
        for at in range(n):
            for k in range(n_sets):
                copies.append(
                    dma(
                        w_in[k].at[mm(at_ref[1 + k] * n + at, units), :],
                        w.at[k * units : (k + 1) * units, at * size : (at + 1) * size],
                        sems.at[k * n + at],
                    )
                )
        run_all(copies)
        for o in range(2):

            @pl.loop(0, half // chunk)
            def _(m):
                hs = h_ref[mm(m + o * (half // chunk), chunk), :]
                for at in range(n):
                    to = slice(at * size, (at + 1) * size)
                    outs[o][mm(m, chunk), to] = dot(hs, w[:, to]).astype(BF16)

    return pl.pallas_call(
        kernel,
        in_specs=[SMEM_SPEC, VMEM_SPEC] + [HBM_SPEC] * (1 + n_sets),
        out_specs=[VMEM_SPEC] * 2,
        out_shape=[jax.ShapeDtypeStruct((half, n * size), BF16)] * 2,
        scratch_shapes=[
            VM((depth, n * size), BF16),
            pltpu.SemaphoreType.DMA((n_sets * n + 1,)),
        ],
        compiler_params=PARAMS,
        cost_estimate=COST,
        name="project_down",
    )(scalars, hidden, b, *sets)


def assemble(pieces, places, shape):
    rows, columns = pieces[0].shape

    def kernel(places_ref, *refs):
        out = refs[-1]
        for i in range(len(pieces)):
            to = mm(places_ref[2 * i], rows), mm(places_ref[2 * i + 1], columns)
            out[to] = refs[i][...]

    return pl.pallas_call(
        kernel,
        in_specs=[SMEM_SPEC] + [VMEM_SPEC] * len(pieces),
        out_specs=VMEM_SPEC,
        out_shape=jax.ShapeDtypeStruct(shape, BF16),
        compiler_params=PARAMS,
        cost_estimate=COST,
        name="assemble",
    )(places, *pieces)


def make_body(R, T):
    Z, ZH, Y = R // 2, R // 4, T // 2

    def flat(z, x, y, c):
        return (z * 2 + x) * T + y * 2 + c

    def move(f):
        every = [(r // 2, r % 2, t // 2, t % 2) for r in range(R) for t in range(T)]
        return [(flat(*d), flat(*f(*d))) for d in every]

    def wait_for(value, after):
        return lax.optimization_barrier((value, *after))[0] if after else value

    def send(value, pairs, after=()):
        return lax.ppermute(wait_for(value, after), AXES, pairs)

    to_core = move(lambda z, x, y, c: (z, x, y, 1 - c))
    to_x = move(lambda z, x, y, c: (z, 1 - x, y, c))
    z_up = move(lambda z, x, y, c: ((z + 1) % Z, x, y, c))
    z_down = move(lambda z, x, y, c: ((z - 1) % Z, x, y, c))
    from_y = {k: move(lambda z, x, y, c, k=k: (z, x, (y - k) % Y, c)) for k in range(1, Y)}
    same_xzl = [[zh * 4 + b for b in range(4)] for zh in range(ZH)]
    same_zh = [[zh * 4 + b for zh in range(ZH)] for b in range(4)]
    same_xy = [
        [flat(z, x, y, c) for x in (0, 1) for y in range(Y)] for z in range(Z) for c in (0, 1)
    ]

    def spread(value, axes, groups, after=()):
        return lax.all_to_all(
            wait_for(value, after), axes, 0, 0, axis_index_groups=groups, tiled=True
        )

    def gather_zh(value, after=()):
        return lax.all_gather(
            wait_for(value, after), "req", axis=0, axis_index_groups=same_zh, tiled=True
        )

    def body(
        tokens, lengths, request_adapter, w_qkv, w_out, w_gate, w_up, w_down,
        a_qkv, b_qkv, a_out, b_out, a_gate, b_gate, a_up, b_up, a_down, b_down,
    ):
        r, t = lax.axis_index("req"), lax.axis_index("tp")
        z, x, y, c = r // 2, r % 2, t // 2, t % 2
        zh, zl = z // 2, z % 2
        slots, width = tokens.shape
        piece = slots // T
        block = width // R
        local = w_qkv.shape[2] // 2
        rank = a_qkv.shape[1]
        quarter = w_gate.shape[1] // 4
        span = width // ZH

        def cut(array, start, size, axis):
            return lax.dynamic_slice_in_dim(array, start, size, axis)

        def ints(values):
            return jnp.stack([jnp.asarray(v, jnp.int32) for v in values])

        both = jnp.concatenate([lengths, request_adapter], axis=1)
        both = lax.all_gather(both, "req", axis=0, axis_index_groups=same_xzl, tiled=True)
        count = lengths.shape[1]
        request_of, position, adapter = jax.vmap(lambda l, a: slot_layout(l, a, slots))(
            both[:, :count], both[:, count:]
        )
        here = lambda v: cut(v, zl * 2, 2, 0)
        cosine, sine = rope_tables(here(position).reshape(-1))

        def heads_of(w, which):
            return cut(w, which * local, local, 2).reshape(w.shape[0], 3 * local)

        qkv = {(0, 0): heads_of(w_qkv, x)}
        qkv[(0, 1)] = send(heads_of(w_qkv, 1 - x), to_x)
        normed = layer_norm(tokens.astype(F32))
        quarter_x = send(cut(normed, t * piece, piece, 0), to_x)
        for i in (0, 1):
            left = right = qkv[(0, i)]
            for k in range(1, Z // 2):
                left, right = send(left, z_up), send(right, z_down)
                qkv[(Z - k, i)], qkv[(k, i)] = left, right
        gu = jnp.concatenate([w_gate.reshape(block, 4, quarter), w_up.reshape(block, 4, quarter)], 2)
        gu = gu.transpose(1, 0, 2).reshape(4 * block, 2 * quarter)
        gu = spread(gu, "req", same_xzl, [qkv[(0, 1)]])
        qkv[(Z // 2, 0)] = send(qkv[(Z // 2 + 1, 0)], z_up)
        qkv[(Z // 2, 1)] = send(qkv[(Z // 2 - 1, 1)], z_down)
        keys = [(k, i) for k in range(Z) for i in (0, 1)]
        order = [((z + k) % Z) * 2 + (x ^ i) for k, i in keys]
        quarters, at = [], []
        for k in range(Y):
            came = quarter_x if k == 0 else send(quarter_x, from_y[k])
            quarters += [came, send(came, to_core)]
            at += [(1 - x) * T + ((y + k) % Y) * 2 + s for s in (c, 1 - c)]

        own = cut(w_out, x * local, local, 0)
        other = send(cut(w_out, (1 - x) * local, local, 0), to_x, [quarter_x])
        left = right = jnp.concatenate([own, other], axis=1)
        late = [qkv[(Z // 2, 0)], qkv[(Z // 2, 1)]]
        out = {0: (left,)}
        for k in range(1, Z // 2):
            left, right = send(left, z_up, late), send(right, z_down, late)
            out[Z - k], out[k] = (left,), (right,)
        out[Z // 2] = (send(left[:, :block], z_up), send(right[:, block:], z_down))

        gu_all = gather_zh(gu, [qkv[(1, 1)], qkv[(Z - 1, 1)]])
        down = spread(w_down, "req", same_xzl, [quarter_x, gu])
        down_all = gather_zh(down)
        mine = (zl * 2 + x) * quarter
        b_own = jnp.concatenate(
            [cut(b_gate, mine, quarter, 1), cut(b_up, mine, quarter, 1)], axis=1
        )
        a_down_own = cut(a_down, mine, quarter, 0)
        sets = [([gu_all], b_own, a_down_own)]
        places = [0]
        down_sets = [[(down, 0)]] + [[(down_all, (zh + h) % ZH)] for h in range(1, ZH)]
        for k in range(1, Y):
            first = send(gu, from_y[k])
            ends = send(b_own, from_y[k]), send(a_down_own, from_y[k])
            down_sets[0].append((send(down, from_y[k]), 0))
            relayed = [first]
            places.append(zh)
            for h in range(1, ZH):
                there = (zh + h) % ZH
                relayed.append(send(cut(gu_all, there * gu.shape[0], gu.shape[0], 0), from_y[k]))
                places.append(there)
                part = cut(down_all, there * down.shape[0], down.shape[0], 0)
                down_sets[h].append((send(part, from_y[k]), 0))
            sets.append((relayed, *ends))

        two = here(adapter).reshape(-1)
        b_heads = heads_of(b_qkv, x)
        joined = project_qkv(
            normed, quarters, two, a_qkv, b_heads, cosine, sine,
            [qkv[key] for key in keys], ints([x, *at, *order]),
        )
        attn = attend(joined, here(request_of))
        terms = []
        for keep, give in project_out(
            attn, two, a_out, b_out, [out[k] for k in range(Z)], ints(order), ints([x, c]), T, 2
        ):
            pair = keep.astype(F32) + send(give, to_core).astype(F32)
            terms.append(spread(pair.astype(BF16), AXES, same_xy))
        z_order = ints([(z + k) % Z for k in range(Z)])
        hidden_state, normed2 = residual_norm(tokens, ints([t]), z_order, terms, T)

        rows = spread(jnp.concatenate([normed2] * 4, axis=0), "req", same_xzl)
        rows = [rows, send(rows, to_core)]
        adapters = jnp.concatenate(
            [cut(adapter, (y * 2 + (c ^ s)) * piece, piece, 1).reshape(-1) for s in (0, 1)]
        )
        hidden = gated(rows, adapters, a_gate, a_up, sets, ints(places))
        pieces, places = [], []
        for h in range(ZH):
            there = (zh + h) % ZH
            keep, give = project_down(
                hidden, b_down, [w for w, _ in down_sets[h]], quarter,
                ints([there] + [p for _, p in down_sets[h]]),
            )
            pair = keep.astype(F32) + send(give, to_core).astype(F32)
            came = spread(pair.astype(BF16), "req", same_xzl).astype(F32)
            total = cut(hidden_state, there * span, span, 1)
            for b in range(4):
                total = total + came[b * piece : (b + 1) * piece]
            done = total.astype(BF16)
            for k in range(Y):
                there_y = done if k == 0 else send(done, from_y[k])
                for s, got in ((0, there_y), (1, send(there_y, to_core))):
                    pieces.append(got)
                    places += [((y + k) % Y) * 2 + (c ^ s), there]
        return assemble(pieces, ints(places), tokens.shape)

    return body


def solution(mesh):
    in_specs = (
        P("req", None),
        P("req", None),
        P("req", None),
        P("req", None, "tp"),
        P("tp", "req"),
        P("req", "tp"),
        P("req", "tp"),
        P("tp", "req"),
        P(),
        P(None, None, "tp"),
        P("tp", None),
        P(),
        P(),
        P(None, "tp"),
        P(),
        P(None, "tp"),
        P("tp", None),
        P(),
    )
    return jax.shard_map(
        make_body(mesh.shape["req"], mesh.shape["tp"]),
        mesh=mesh, in_specs=in_specs, out_specs=P("req", None), check_vma=False,
    )
```

```python
import math

import jax
import jax.numpy as jnp
from jax import lax
from jax.experimental import pallas as pl
from jax.experimental.pallas import tpu as pltpu
from jax.sharding import PartitionSpec as P

HD = 128
RANK = 16
AXES = ("req", "tp")
epsilon = 1e-05
rope_base = 10000.0
F32 = jnp.float32
BF16 = jnp.bfloat16
VM = pltpu.VMEM
PARAMS = pltpu.CompilerParams(vmem_limit_bytes=56 * 2**20)
COST = pl.CostEstimate(flops=1000, bytes_accessed=1000, transcendentals=0)


def dot(a, b):
    return jnp.dot(a, b, preferred_element_type=F32)


def layer_norm(values):
    row_mean = jnp.mean(values, axis=-1, keepdims=True)
    centred = values - row_mean
    spread = jnp.mean(centred * centred, axis=-1, keepdims=True)
    return (centred * lax.rsqrt(spread + epsilon)).astype(BF16)


def masked(inner, adapter_column):
    rank = lax.broadcasted_iota(jnp.int32, inner.shape, 1) // RANK
    return jnp.where(adapter_column == rank, inner, F32(0.0)).astype(BF16)


def whole(array):
    return pl.BlockSpec(array.shape, lambda *_: (0,) * array.ndim, pipeline_mode=pl.Buffered(1))


def mm(start, size):
    return pl.ds(pl.multiple_of(start * size, size), size)


def dma(source, target, semaphore):
    return pltpu.make_async_copy(source, target, semaphore)


def run_all(copies):
    for copy in copies:
        copy.start()
    for copy in copies:
        copy.wait()


SMEM_SPEC = pl.BlockSpec(memory_space=pltpu.SMEM)
VMEM_SPEC = pl.BlockSpec(memory_space=VM)
HBM_SPEC = pl.BlockSpec(memory_space=pl.ANY)


def split_heads(w_qkv, w_out, x):
    rows, _, columns = w_qkv.shape
    local = columns // 2
    width = w_out.shape[1]

    def kernel(x_ref, qkv_ref, out_ref, *outs):
        for which in range(2):
            at = mm(x_ref[0] ^ which, local)
            for i in range(3):
                outs[which][:, i * local : (i + 1) * local] = qkv_ref[:, i, at]
            outs[2 + which][...] = out_ref[at, :]

    return pl.pallas_call(
        kernel,
        in_specs=[SMEM_SPEC, VMEM_SPEC, VMEM_SPEC],
        out_specs=[VMEM_SPEC] * 4,
        out_shape=[jax.ShapeDtypeStruct((rows, 3 * local), BF16)] * 2
        + [jax.ShapeDtypeStruct((local, width), BF16)] * 2,
        compiler_params=PARAMS,
        cost_estimate=COST,
        name="split_heads",
    )(x, w_qkv, w_out)


def norm_rows(tokens, row, T):
    slots, width = tokens.shape
    piece = slots // T

    def kernel(row_ref, tok_ref, out, part):
        i = pl.program_id(0)
        normed = layer_norm(tok_ref[...].astype(F32))
        out[...] = normed

        @pl.when(i == row_ref[0])
        def _():
            part[...] = normed

    return pl.pallas_call(
        kernel,
        grid_spec=pltpu.PrefetchScalarGridSpec(
            num_scalar_prefetch=1,
            grid=(T,),
            in_specs=[pl.BlockSpec((piece, width), lambda i, r: (i, 0))],
            out_specs=[
                pl.BlockSpec((piece, width), lambda i, r: (i, 0)),
                pl.BlockSpec((piece, width), lambda i, r: (0, 0)),
            ],
        ),
        out_shape=[
            jax.ShapeDtypeStruct((slots, width), BF16),
            jax.ShapeDtypeStruct((piece, width), BF16),
        ],
        compiler_params=PARAMS,
        cost_estimate=COST,
        name="norm_rows",
    )(row, tokens)


def pack(gate, up, b):
    rows, columns = gate.shape
    quarter = columns // 4

    def spec(which):
        return pl.BlockSpec((rows, quarter), lambda i, o: (0, o[0] ^ (i * 2 + which)))

    def kernel(b_ref, g0, u0, g1, u1, keep, give):
        keep[0, :, :quarter], keep[0, :, quarter:] = g0[...], u0[...]
        give[0, :, :quarter], give[0, :, quarter:] = g1[...], u1[...]

    out = pl.BlockSpec((1, rows, 2 * quarter), lambda i, o: (i, 0, 0))
    return pl.pallas_call(
        kernel,
        grid_spec=pltpu.PrefetchScalarGridSpec(
            num_scalar_prefetch=1,
            grid=(2,),
            in_specs=[spec(0), spec(0), spec(1), spec(1)],
            out_specs=[out, out],
        ),
        out_shape=[jax.ShapeDtypeStruct((2, rows, 2 * quarter), BF16)] * 2,
        compiler_params=PARAMS,
        cost_estimate=COST,
        name="pack",
    )(b, gate, up, gate, up)


def join(own, came, x):
    rows, columns = own.shape[1:]
    spec = pl.BlockSpec((1, rows, columns), lambda i: (i, 0, 0))
    shape = jax.ShapeDtypeStruct((2 * rows, columns), BF16)

    def kernel(x_ref, own_ref, came_ref, near, give):
        @pl.when(pl.program_id(0) == 0)
        def _():
            near[mm(x_ref[0], rows), :] = own_ref[0]
            near[mm(1 - x_ref[0], rows), :] = came_ref[0]

        @pl.when(pl.program_id(0) == 1)
        def _():
            give[mm(x_ref[0], rows), :] = own_ref[0]
            give[mm(1 - x_ref[0], rows), :] = came_ref[0]

    return pl.pallas_call(
        kernel,
        grid=(2,),
        in_specs=[SMEM_SPEC, spec, spec],
        out_specs=[pl.BlockSpec((2 * rows, columns), lambda i: (0, 0))] * 2,
        out_shape=[shape, shape],
        compiler_params=PARAMS,
        cost_estimate=COST,
        name="join",
    )(x, own, came)


def tables(lengths, adapters, scalars, slots, T):
    count = lengths.shape[1]
    piece = slots // T
    half = HD // 2

    def kernel(len_ref, ad_ref, at_ref, column, line, two, cosine, sine, rows):
        def layout(index, slot, wants):
            end = jnp.int32(0)
            request, start = jnp.zeros(slot.shape, jnp.int32), jnp.zeros(slot.shape, jnp.int32)
            adapter = jnp.full(slot.shape, ad_ref[index, 0], jnp.int32)
            for k in range(count):
                end = end + len_ref[index, k]
                past = slot >= end
                request = request + past.astype(jnp.int32)
                if wants and k + 1 < count:
                    start = jnp.where(past, end, start)
                    adapter = jnp.where(past, ad_ref[index, k + 1], adapter)
            return request, slot - start, adapter

        lane = lax.broadcasted_iota(jnp.int32, (1, HD), 1)
        frequency = jnp.exp((lane % half).astype(F32) * F32(-math.log(rope_base) * 2.0 / HD))
        for i in range(2):
            index = at_ref[0] * 2 + i
            down = lax.broadcasted_iota(jnp.int32, (slots, 1), 0)
            request, position, adapter = layout(index, down, True)
            column[i] = request
            line[i] = layout(index, lax.broadcasted_iota(jnp.int32, (1, slots), 1), False)[0]
            here = slice(i * slots, (i + 1) * slots)
            two[here] = adapter
            angles = position.astype(F32) * frequency
            cosine[here] = jnp.cos(angles)
            sine[here] = jnp.where(lane < half, -jnp.sin(angles), jnp.sin(angles))
        for s in range(2):
            first = (at_ref[1] * 2 + (at_ref[2] ^ s)) * piece
            slot = first + lax.broadcasted_iota(jnp.int32, (piece, 1), 0)
            for b in range(4):
                to = (s * 4 + b) * piece
                rows[to : to + piece] = layout(at_ref[3] ^ b, slot, True)[2]

    table = jax.ShapeDtypeStruct((2 * slots, HD), F32)
    return pl.pallas_call(
        kernel,
        in_specs=[SMEM_SPEC] * 3,
        out_specs=[VMEM_SPEC] * 6,
        out_shape=[
            jax.ShapeDtypeStruct((2, slots, 1), jnp.int32),
            jax.ShapeDtypeStruct((2, 1, slots), jnp.int32),
            jax.ShapeDtypeStruct((2 * slots, 1), jnp.int32),
            table,
            table,
            jax.ShapeDtypeStruct((8 * piece, 1), jnp.int32),
        ],
        compiler_params=PARAMS,
        cost_estimate=COST,
        name="tables",
    )(lengths, adapters, scalars)


def finish(hidden_state, terms, at):
    piece, columns = terms[0].shape
    spec = pl.BlockSpec((piece, columns), lambda i, a: (0, 0))

    def kernel(at_ref, hidden_ref, *refs):
        total = hidden_ref[...]
        for ref in refs[:-1]:
            total = total + ref[...].astype(F32)
        refs[-1][...] = total.astype(BF16)

    return pl.pallas_call(
        kernel,
        grid_spec=pltpu.PrefetchScalarGridSpec(
            num_scalar_prefetch=1,
            grid=(1,),
            in_specs=[pl.BlockSpec((piece, columns), lambda i, a: (0, a[0]))] + [spec] * len(terms),
            out_specs=spec,
        ),
        out_shape=jax.ShapeDtypeStruct((piece, columns), BF16),
        compiler_params=PARAMS,
        cost_estimate=COST,
        name="finish",
    )(at, hidden_state, *terms)


def project_qkv(own, pieces, adapter, a, b, cosine, sine, weights, places):
    slots, width = own.shape
    total_rows, columns, rank = 2 * slots, b.shape[1], b.shape[0]
    piece, size, tile = pieces[0].shape[0], width // len(weights), columns // 3
    n_pieces, n_weights = len(pieces), len(weights)
    chunk = total_rows // 4
    column = adapter

    def kernel(at_ref, adapter_ref, a_ref, cos_ref, sin_ref, own_ref, b_ref, *refs):
        p_in, w_in, rest = refs[:n_pieces], refs[n_pieces : n_pieces + n_weights], refs[-7:]
        out, x, w, bb, low, x_sem, w_sem = rest

        def weight_copies(step, slot):
            to = pl.ds(step * tile, tile)
            for i in range(n_weights):
                yield dma(
                    w_in[i].at[:, to],
                    w.at[slot, mm(at_ref[1 + n_pieces + i], size), :],
                    w_sem.at[slot, i],
                )
            yield dma(b_ref.at[:, to], bb.at[slot], w_sem.at[slot, n_weights])

        x_copies = [dma(own_ref, x.at[mm(at_ref[0], slots), :], x_sem.at[n_pieces])]
        for i in range(n_pieces):
            x_copies.append(dma(p_in[i], x.at[mm(at_ref[1 + i], piece), :], x_sem.at[i]))
        for copy in x_copies:
            copy.start()
        for copy in weight_copies(0, 0):
            copy.start()
        for copy in x_copies:
            copy.wait()
        for step in range(3):
            slot = step % 2
            if step < 2:
                for copy in weight_copies(step + 1, 1 - slot):
                    copy.start()
            for copy in weight_copies(step, slot):
                copy.wait()

            @pl.loop(0, total_rows // chunk)
            def _(m):
                at = mm(m, chunk)
                xs = x[at, :]
                if step == 0:
                    low[at, :] = masked(dot(xs, a_ref[...]), adapter_ref[at, :])
                total = dot(xs, w[slot]) + dot(low[at, :], bb[slot])
                for h in range(tile // HD):
                    v = total[:, h * HD : (h + 1) * HD]
                    if step < 2:
                        v = v * cos_ref[at, :] + pltpu.roll(v, HD // 2, 1) * sin_ref[at, :]
                    start = step * tile + h * HD
                    out[at, start : start + HD] = v.astype(BF16)

    return pl.pallas_call(
        kernel,
        in_specs=[SMEM_SPEC] + [VMEM_SPEC] * 4 + [HBM_SPEC] * (2 + n_pieces + n_weights),
        out_specs=VMEM_SPEC,
        out_shape=jax.ShapeDtypeStruct((total_rows, columns), BF16),
        scratch_shapes=[
            VM((total_rows, width), BF16),
            VM((2, width, tile), BF16),
            VM((2, rank, tile), BF16),
            VM((total_rows, rank), BF16),
            pltpu.SemaphoreType.DMA((n_pieces + 1,)),
            pltpu.SemaphoreType.DMA((2, n_weights + 1)),
        ],
        compiler_params=PARAMS,
        cost_estimate=COST,
        name="project_qkv",
    )(places, column, a, cosine, sine, own, b, *pieces, *weights)


def attend(qkv, column, line):
    indices, slots = column.shape[:2]
    heads = qkv.shape[1] // 3 // HD
    rows = 256 if slots % 256 == 0 else slots

    def kernel(q, k, v, column_ref, line_ref, out):
        for at in range(0, slots, rows):
            seen = at + rows
            s = lax.dot_general(
                q[at:seen], k[:seen], (((1,), (1,)), ((), ())), preferred_element_type=F32
            )
            s = s * (1.0 / math.sqrt(HD))
            here = at + lax.broadcasted_iota(jnp.int32, s.shape, 0)
            there = lax.broadcasted_iota(jnp.int32, s.shape, 1)
            allowed = (column_ref[0, at:seen] == line_ref[0, :, :seen]) & (here >= there)
            s = jnp.where(allowed, s, F32(-1e30))
            e = jnp.exp(s - jnp.max(s, axis=1, keepdims=True))
            weights = (e * (1.0 / jnp.sum(e, axis=1, keepdims=True))).astype(BF16)
            out[at:seen] = dot(weights, v[:seen]).astype(BF16)

    return pl.pallas_call(
        kernel,
        grid=(indices, heads),
        in_specs=[
            pl.BlockSpec((slots, HD), lambda i, h: (i, h)),
            pl.BlockSpec((slots, HD), lambda i, h: (i, heads + h)),
            pl.BlockSpec((slots, HD), lambda i, h: (i, 2 * heads + h)),
            pl.BlockSpec((1, slots, 1), lambda i, h: (i, 0, 0)),
            pl.BlockSpec((1, 1, slots), lambda i, h: (i, 0, 0)),
        ],
        out_specs=pl.BlockSpec((slots, HD), lambda i, h: (i, h)),
        out_shape=jax.ShapeDtypeStruct((indices * slots, heads * HD), BF16),
        compiler_params=PARAMS,
        cost_estimate=COST,
        name="attend",
    )(qkv, qkv, qkv, column, line)


def project_out(attn, adapter, a, b, weights, order, scalars, T, came=None):
    total_rows, depth = attn.shape
    n, slots, piece, Y = len(weights), total_rows // 2, total_rows // 2 // T, T // 2
    flat = [p for w in weights for p in w]
    size = sum(p.shape[1] for p in flat) // n // 2
    half, columns = total_rows // 2, n * 2 * size
    extra = [] if came is None else [came]

    def kernel(order_ref, at_ref, attn_ref, adapter_ref, a_ref, b_ref, *refs):
        ws, outs, rows, low = refs[: len(flat)], refs[len(flat) + len(extra) : -2], *refs[-2:]
        x, y, c = at_ref[0], at_ref[1], at_ref[2]
        mine = a_ref[mm(x, depth), :]
        for i in range(2):
            for k in range(Y):
                here = mm((x ^ i) * T + lax.rem(y + Y - k, Y) * 2 + c, piece)
                to = (i * Y + k) * piece
                part = attn_ref[here, :]
                rows[to : to + piece] = part
                low[to : to + piece] = masked(dot(part, mine), adapter_ref[here, :])
        it = iter(ws)
        for k, w in enumerate(weights):
            blocks = []
            for p in w:
                ref = next(it)
                for start in range(0, p.shape[1], size):
                    blocks.append((ref, start))
            for i, (ref, start) in enumerate(blocks):
                there = mm(order_ref[2 * k + i], size)
                to = mm(k * 2 + (x ^ i), size)
                total = dot(rows[...], ref[:, start : start + size]) + dot(low[...], b_ref[:, there])
                if came is None:
                    outs[0][:, to] = total.astype(BF16)
                else:
                    total = (total + refs[len(flat)][:, to].astype(F32)).astype(BF16)
                    for p in range(2 * Y):
                        outs[p][:, to] = total[p * piece : (p + 1) * piece]

    shapes = [jax.ShapeDtypeStruct((half, columns), BF16)]
    if came is not None:
        shapes = [jax.ShapeDtypeStruct((piece, columns), BF16)] * (2 * Y)
    out = pl.pallas_call(
        kernel,
        in_specs=[SMEM_SPEC, SMEM_SPEC] + [VMEM_SPEC] * (4 + len(flat) + len(extra)),
        out_specs=[VMEM_SPEC] * len(shapes),
        out_shape=shapes,
        scratch_shapes=[VM((half, depth), BF16), VM((half, a.shape[1]), BF16)],
        compiler_params=PARAMS,
        cost_estimate=COST,
        name="project_out",
    )(order, scalars, attn, adapter, a, b, *flat, *extra)
    return out[0] if came is None else out


def residual_norm(tokens, row, order, chunks):
    width = tokens.shape[1]
    n = order.shape[0]
    piece, size, per = chunks[0][0].shape[0], width // n, n // len(chunks)
    flat = [term for chunk in chunks for term in chunk]

    def kernel(row_ref, order_ref, tok_ref, *refs):
        it, hidden, normed = iter(refs[:-2]), refs[-2], refs[-1]
        for c, chunk in enumerate(chunks):
            total = next(it)[...].astype(F32)
            for _ in chunk[1:]:
                total = total + next(it)[...].astype(F32)
            for place in range(per):
                to = mm(order_ref[c * per + place], size)
                more = total[:, place * size : (place + 1) * size]
                hidden[:, to] = tok_ref[:, to].astype(F32) + more
        normed[...] = layer_norm(hidden[...])

    return pl.pallas_call(
        kernel,
        grid_spec=pltpu.PrefetchScalarGridSpec(
            num_scalar_prefetch=2,
            grid=(1,),
            in_specs=[
                pl.BlockSpec((piece, width), lambda n, r, o: (r[0], 0)),
                *[pl.BlockSpec(p.shape, lambda n, r, o: (0, 0)) for p in flat],
            ],
            out_specs=[pl.BlockSpec((piece, width), lambda n, r, o: (0, 0))] * 2,
        ),
        out_shape=[
            jax.ShapeDtypeStruct((piece, width), F32),
            jax.ShapeDtypeStruct((piece, width), BF16),
        ],
        compiler_params=PARAMS,
        cost_estimate=COST,
        name="residual_norm",
    )(row, order, tokens, *flat)


def gated(rows, adapters, a_gate, a_up, sets, places):
    width = rows[0].shape[1]
    total_rows = sum(row.shape[0] for row in rows)
    units = sets[0][1].shape[1] // 2
    tile = min(256, units)
    tiles = units // tile
    rank = a_gate.shape[1]
    column = adapters
    flat = [w for s in sets for w in s[0]]
    first = [sum(len(s[0]) for s in sets[:k]) for k in range(len(sets) + 1)]
    bs = [s[1] for s in sets]
    downs = [s[2] for s in sets]
    n_rows, n_sets = len(rows), len(sets)
    most = max(len(s[0]) for s in sets)
    steps = n_sets * tiles
    chunk = total_rows // 4
    hidden_width = n_sets * units

    def kernel(place_ref, adapter_ref, ag_ref, au_ref, *refs):
        it = iter(refs)
        take = lambda k: [next(it) for _ in range(k)]
        x_in, w_in, b_in, d_in = take(n_rows), take(len(flat)), take(n_sets), take(n_sets)
        hidden, x, w, bb, lg, lu, ld, x_sem, w_sem, b_sem = take(10)

        def weight_copies(step, slot):
            s, t = divmod(step, tiles)
            for g in range(2):
                for i in range(first[s], first[s + 1]):
                    yield dma(
                        w_in[i].at[:, pl.ds(g * units + t * tile, tile)],
                        w.at[slot, g, mm(place_ref[i], flat[i].shape[0]), :],
                        w_sem.at[slot, g, i - first[s]],
                    )
                yield dma(
                    b_in[s].at[:, pl.ds(g * units + t * tile, tile)],
                    bb.at[slot, g],
                    b_sem.at[slot, g],
                )

        x_copies, start = [], 0
        for i in range(n_rows):
            x_copies.append(dma(x_in[i], x.at[pl.ds(start, rows[i].shape[0]), :], x_sem.at[i]))
            start += rows[i].shape[0]
        for copy in x_copies:
            copy.start()
        for copy in weight_copies(0, 0):
            copy.start()
        for copy in x_copies:
            copy.wait()
        for step in range(steps):
            slot = step % 2
            if step + 1 < steps:
                for copy in weight_copies(step + 1, 1 - slot):
                    copy.start()
            for copy in weight_copies(step, slot):
                copy.wait()
            s, t = divmod(step, tiles)

            @pl.loop(0, total_rows // chunk)
            def _(m):
                at = mm(m, chunk)
                xs = x[at, :]
                if step == 0:
                    lg[at, :] = masked(dot(xs, ag_ref[...]), adapter_ref[at, :])
                    lu[at, :] = masked(dot(xs, au_ref[...]), adapter_ref[at, :])
                gate = dot(xs, w[slot, 0]) + dot(lg[at, :], bb[slot, 0])
                up = dot(xs, w[slot, 1]) + dot(lu[at, :], bb[slot, 1])
                h = (gate / (1.0 + jnp.exp(-gate)) * up).astype(BF16)
                hidden[at, step * tile : (step + 1) * tile] = h
                more = dot(h, d_in[s][t * tile : (t + 1) * tile, :])
                if step > 0:
                    more = more + ld[at, :]
                if step < steps - 1:
                    ld[at, :] = more
                else:
                    hidden[at, hidden_width:] = masked(more, adapter_ref[at, :])

    return pl.pallas_call(
        kernel,
        in_specs=[SMEM_SPEC] + [VMEM_SPEC] * 3
        + [HBM_SPEC] * (n_rows + len(flat) + n_sets)
        + [VMEM_SPEC] * n_sets,
        out_specs=VMEM_SPEC,
        out_shape=jax.ShapeDtypeStruct((total_rows, hidden_width + rank), BF16),
        scratch_shapes=[
            VM((total_rows, width), BF16),
            VM((2, 2, width, tile), BF16),
            VM((2, 2, rank, tile), BF16),
            VM((total_rows, rank), BF16),
            VM((total_rows, rank), BF16),
            VM((total_rows, rank), F32),
            pltpu.SemaphoreType.DMA((n_rows,)),
            pltpu.SemaphoreType.DMA((2, 2, most)),
            pltpu.SemaphoreType.DMA((2, 2)),
        ],
        compiler_params=PARAMS,
        cost_estimate=COST,
        name="gated",
    )(places, column, a_gate, a_up, *rows, *flat, *bs, *downs)


def project_down(hidden, b, sets, units, at, which, came=None):
    half, depth = hidden.shape[0] // 2, hidden.shape[1]
    piece, rank = half // 4, b.shape[0]
    size = sets[0][0].shape[1]
    flat = [w for group in sets for w in group]
    n, n_sets, n_weights = 4, len(sets), len(flat)
    extra = [] if came is None else [came]

    def kernel(at_ref, h_ref, *refs):
        refs = list(refs)
        came_ref = refs.pop(0) if extra else None
        b_ref, w_in, outs, w, sems = refs[0], refs[1 : 1 + n_weights], refs[1 + n_weights : -2], *refs[-2:]
        copies = [
            dma(
                b_ref.at[:, mm(at_ref[0], n * size)],
                w.at[n_sets * units : n_sets * units + rank, :],
                sems.at[n_sets * n],
            )
        ]
        it = iter(w_in)
        for k, group in enumerate(sets):
            place = 0
            for array in group:
                ref = next(it)
                for i in range(array.shape[0] // units):
                    copies.append(
                        dma(
                            ref.at[pl.ds(i * units, units), :],
                            w.at[k * units : (k + 1) * units, place * size : (place + 1) * size],
                            sems.at[k * n + place],
                        )
                    )
                    place += 1
        run_all(copies)
        for m in range(2):
            here = slice(m * 2 * piece, (m + 1) * 2 * piece)
            total = dot(h_ref[here, :], w[...])
            if came is None:
                outs[0][here, :] = total.astype(BF16)
            else:
                total = (total + came_ref[here, :].astype(F32)).astype(BF16)
                outs[2 * m][...], outs[2 * m + 1][...] = total[:piece], total[piece:]

    shapes = [jax.ShapeDtypeStruct((half, n * size), BF16)]
    if came is not None:
        shapes = [jax.ShapeDtypeStruct((piece, n * size), BF16)] * 4
    out = pl.pallas_call(
        kernel,
        grid=(1,),
        in_specs=[SMEM_SPEC, pl.BlockSpec((half, depth), lambda i: (which, 0))]
        + [VMEM_SPEC] * len(extra)
        + [HBM_SPEC] * (1 + n_weights),
        out_specs=[VMEM_SPEC] * len(shapes),
        out_shape=shapes,
        scratch_shapes=[
            VM((depth, n * size), BF16),
            pltpu.SemaphoreType.DMA((n_sets * n + 1,)),
        ],
        compiler_params=PARAMS,
        cost_estimate=COST,
        name="project_down",
    )(at, hidden, *extra, b, *flat)
    return out[0] if came is None else out


def assemble(pieces, places, shape):
    rows, columns = pieces[0].shape

    def kernel(places_ref, *refs):
        out = refs[-1]
        for i in range(len(pieces)):
            to = mm(places_ref[2 * i], rows), mm(places_ref[2 * i + 1], columns)
            out[to] = refs[i][...]

    return pl.pallas_call(
        kernel,
        in_specs=[SMEM_SPEC] + [VMEM_SPEC] * len(pieces),
        out_specs=VMEM_SPEC,
        out_shape=jax.ShapeDtypeStruct(shape, BF16),
        compiler_params=PARAMS,
        cost_estimate=COST,
        name="assemble",
    )(places, *pieces)


@jax.tree_util.register_pytree_node_class
class Live:
    def __init__(self, **arrays):
        self.__dict__.update(arrays)

    def tree_flatten(self):
        names = tuple(sorted(self.__dict__))
        return [self.__dict__[name] for name in names], names

    @classmethod
    def tree_unflatten(cls, names, arrays):
        return cls(**dict(zip(names, arrays)))

    @property
    def pop(self):
        return Pop(self)

    @property
    def drop(self):
        return Drop(self)


class Pop:
    def __init__(self, live):
        self.__dict__.update(live=live)

    def __getattr__(self, name):
        return self.live.__dict__.pop(name)


class Drop(Pop):
    def __getattr__(self, name):
        self.live.__dict__.pop(name)
        return self


def make_body(R, T):
    Z, ZH, Y = R // 2, R // 4, T // 2

    def flat(z, x, y, c):
        return (z * 2 + x) * T + y * 2 + c

    def move(f):
        every = [(r // 2, r % 2, t // 2, t % 2) for r in range(R) for t in range(T)]
        return [(flat(*d), flat(*f(*d))) for d in every]

    def send(value, pairs):
        return lax.ppermute(value, AXES, pairs)

    to_core = move(lambda z, x, y, c: (z, x, y, 1 - c))
    to_x = move(lambda z, x, y, c: (z, 1 - x, y, c))
    z_up = move(lambda z, x, y, c: ((z + 1) % Z, x, y, c))
    z_down = move(lambda z, x, y, c: ((z - 1) % Z, x, y, c))
    from_y = {k: move(lambda z, x, y, c, k=k: (z, x, (y - k) % Y, c)) for k in range(1, Y)}
    same_xzl = [[zh * 4 + b for b in range(4)] for zh in range(ZH)]
    same_zh = [[zh * 4 + b for zh in range(ZH)] for b in range(4)]
    to_xy = {
        (i, k): move(lambda z, x, y, c, i=i, k=k: (z, x ^ i, (y - k) % Y, c))
        for i in (0, 1)
        for k in range(Y)
    }
    to_xzl = {
        (i, j): move(lambda z, x, y, c, i=i, j=j: (z ^ j, x ^ i, y, c))
        for j in (0, 1)
        for i in (0, 1)
    }

    from_zh = {
        k: move(lambda z, x, y, c, k=k: ((z - 2 * k) % Z, x, y, c)) for k in range(1, ZH)
    }
    to_zl = move(lambda z, x, y, c: (z ^ 1, x, y, c))

    def spread(value, axes, groups):
        return lax.all_to_all(value, axes, 0, 0, axis_index_groups=groups, tiled=True)

    def fence(live):
        return lax.optimization_barrier(live)

    def body(
        tokens, lengths, request_adapter, w_qkv, w_out, w_gate, w_up, w_down,
        a_qkv, b_qkv, a_out, b_out, a_gate, b_gate, a_up, b_up, a_down, b_down,
    ):
        r, t = lax.axis_index("req"), lax.axis_index("tp")
        z, x, y, c = r // 2, r % 2, t // 2, t % 2
        zh, zl = z // 2, z % 2
        slots, width = tokens.shape
        piece = slots // T
        block = width // R
        local = w_qkv.shape[2] // 2
        rank = a_qkv.shape[1]
        quarter = w_gate.shape[1] // 4
        span = width // ZH
        count = lengths.shape[1]
        far_y, far_zh, opposite = range(1, Y), range(1, ZH), Z // 2

        def cut(array, start, size, axis):
            return lax.dynamic_slice_in_dim(array, start, size, axis)

        def ints(values):
            return jnp.stack([jnp.asarray(v, jnp.int32) for v in values])

        L = Live(
            tokens=tokens, both=jnp.concatenate([lengths, request_adapter], axis=1), w_gate=w_gate,
            w_up=w_up, w_down=w_down, a_qkv=a_qkv, a_out=a_out, b_out=b_out, a_gate=a_gate,
            a_up=a_up, b_down=b_down, b_qkv=b_qkv, b_gate=b_gate, b_up=b_up, a_down=a_down,
        )
        keys = [(k, i) for k in range(Z) for i in (0, 1)]
        order = [((z + k) % Z) * 2 + (x ^ i) for k, i in keys]
        there = [(zh + h) % ZH for h in range(ZH)]
        at = [(1 - x) * T + ((y + k) % Y) * 2 + s for s in (c, 1 - c) for k in range(Y)]
        far_places = [h * 4 + (zl ^ j) * 2 + q for h in there[1:] for j in (0, 1) for q in (0, 1)]
        places = ([zh * 2 + zl, zh * 2 + 1 - zl] + far_places) * Y
        L.ints = Live(
            t=ints([t]), order=[ints(order[:Z]), ints(order[Z:])], qkv=ints([x, *at, *order]),
            xyc=[ints([x, y, c]), ints([x, y, 1 - c])],
            zyc=ints([zl, y, c, zl * 2 + x]), z=ints([(z + k) % Z for k in range(Z)]),
            gated=ints(places), span=[ints([h]) for h in there], b=ints([zl * 2 + x]),
        )
        mine = (zl * 2 + x) * quarter
        L.split = split_heads(w_qkv, w_out, ints([x]))
        L = fence(L)

        def ring_start(own):
            left = right = own
            got = {0: own}
            for k in range(1, opposite):
                left, right = send(left, z_up), send(right, z_down)
                got[Z - k], got[k] = left, right
            return got

        head, other_head, own_out, other_out = L.pop.split
        L.first = send(other_head, to_x)
        L.ring = [ring_start(head)]
        L.out = send(other_out, to_x)
        L.both = spread(jnp.concatenate([L.both] * 4, axis=0), "req", same_xzl)
        L.normed, L.mine = norm_rows(L.tokens, L.ints.t, T)
        L.b = jnp.concatenate(
            [cut(L.pop.b_gate, mine, quarter, 1), cut(L.pop.b_up, mine, quarter, 1)], axis=1
        )
        L.a_down = cut(L.a_down, mine, quarter, 0)
        L.b_heads = cut(L.pop.b_qkv, x * local, local, 2).reshape(rank, 3 * local)
        L.own_out = own_out
        L = fence(L)

        L.ring.append(ring_start(L.pop.first))
        L.quarter = send(L.pop.mine, to_x)
        L.b_far = [send(L.b, from_y[k]) for k in far_y]
        L.gu, L.gu_give = pack(L.pop.w_gate, L.pop.w_up, L.ints.b)
        L.out = jnp.concatenate([L.pop.own_out, L.out], axis=1)
        L = fence(L)

        L.ring[0][opposite] = send(L.ring[0][opposite + 1], z_up)
        L.ring[1][opposite] = send(L.ring[1][opposite - 1], z_down)
        L.quarters = [L.quarter] + [send(L.quarter, from_y[k]) for k in far_y]
        L.out = ring_start(L.out)
        L.gu_came = send(L.pop.gu_give, to_x)
        both = L.pop.both
        L.tables = tables(both[:, :count], both[:, count:], L.ints.zyc, slots, T)
        L = fence(L)
        L.quarters = L.quarters + [send(q, to_core) for q in L.quarters]
        L.for_out = [L.out[opposite + 1][:, :block], L.out[opposite - 1][:, block:]]
        L.near, L.give = join(L.pop.gu, L.pop.gu_came, L.ints.xyc[0])
        L = fence(L)

        one, two = L.pop.for_out
        L.far_out = [send(one, z_up), send(two, z_down)]
        L.far = send(L.pop.give, to_zl)
        L.y = [[send(L.near, from_y[k]) for k in far_y]]
        column, line, adapter, cosine, sine, adapters = L.tables
        L.joined = project_qkv(
            L.pop.normed, L.pop.quarters, adapter, L.pop.a_qkv, L.pop.b_heads, cosine,
            sine, [L.ring[i][k] for k, i in keys], L.ints.qkv,
        )
        L.pop.ring
        L = fence(L)

        def over_zh(w):
            return [send(w, from_zh[h]) for h in far_zh]

        rows = L.near.shape[0] // 2
        L.for_zh = [w[q * rows : (q + 1) * rows] for w in (L.near, L.far) for q in (0, 1)]
        L.y.append([send(L.far, from_y[k]) for k in far_y])
        L.zh = [over_zh(L.for_zh[0])]
        L.a_far = [send(L.a_down, from_y[k]) for k in far_y]
        column, line, adapter, cosine, sine, adapters = L.pop.tables
        L.attn = attend(L.pop.joined, column, line)
        blocks = [(L.out[k],) if k != opposite else tuple(L.far_out) for k in range(Z)]
        L.blocks = [blocks[:opposite], blocks[opposite:]]
        L.adapter, L.adapters = adapter, adapters
        L.pop.out, L.pop.far_out, L.pop.quarter
        L.down = spread(L.pop.w_down, "req", same_xzl)
        L = fence(L)

        def out_of(L, chunk, core, came=None):
            return project_out(
                L.attn, L.adapter, L.a_out, L.b_out, L.blocks[chunk],
                L.ints.order[chunk], L.ints.xyc[core], T, came,
            )

        L.zh += [over_zh(L.for_zh[1]), over_zh(L.for_zh[2])]
        came = [send(out_of(L, chunk, 1), to_core) for chunk in (0, 1)]
        L.sums = []
        for chunk in (0, 1):
            parts = out_of(L, chunk, 0, came[chunk])
            terms = [parts[0]]
            for i in (0, 1):
                for k in range(Y):
                    if i or k:
                        terms.append(send(parts[i * Y + k], to_xy[(i, k)]))
            L.sums.append(terms)
        L = fence(L)
        L.hidden_state, L.normed2 = residual_norm(
            L.pop.tokens, L.ints.t, L.ints.z, L.pop.sums
        )
        L.drop.attn.adapter.a_out.b_out.blocks
        split = L.down.shape[0] // 2
        L.for_down = [L.down[:split], L.down[split:]]
        L = fence(L)

        def relay(parts):
            return [[[send(w, from_y[k]) for w in part] for k in far_y] for part in parts]

        own = L.pop.normed2
        L.rows = [own, send(own, to_x), send(own, to_zl)]
        L.core = [send(own, to_core)]
        L.zh_y = relay(L.zh[:2])
        L.zh.append(over_zh(L.for_zh[3]))
        L.cut = [L.rows[1][: piece // 2], L.rows[2][piece // 2 :]]
        L = fence(L)
        one, two = L.pop.cut
        L.core += [send(row, to_core) for row in L.rows[1:]]
        L.rows += [send(one, to_zl), send(two, to_x)]
        L.zh_y += relay(L.zh[2:])
        L.down_zh = [over_zh(L.for_down[0])]
        L = fence(L)
        L.rows += L.pop.core + [send(row, to_core) for row in L.rows[3:]]
        L = fence(L)

        L.down_zh.append(over_zh(L.for_down[1]))
        L.down_y = [send(L.down, from_y[k]) for k in far_y]
        L.down_zh_y = relay(L.down_zh[:1])
        zh_blocks = [part[h] for h in range(ZH - 1) for part in L.zh]
        sets = [([L.near, L.far, *zh_blocks], L.b, L.a_down)]
        for k in range(Y - 1):
            relayed = [part[k][h] for h in range(ZH - 1) for part in L.zh_y]
            sets.append(([L.y[0][k], L.y[1][k], *relayed], L.b_far[k], L.a_far[k]))
        L.hidden = gated(
            L.rows, L.adapters, L.pop.a_gate, L.pop.a_up, sets, L.ints.gated
        )
        L.drop.near.far.for_zh.zh.b.a_down.zh_y.y.b_far.a_far.rows
        L = fence(L)

        L.down_zh_y += relay(L.down_zh[1:])
        down_sets = [[[L.down]] + [[w] for w in L.down_y]]
        for h in range(ZH - 1):
            far = [[part[k][h] for part in L.down_zh_y] for k in range(Y - 1)]
            down_sets.append([[part[h] for part in L.down_zh]] + far)

        def down_of(h, which, came=None):
            return project_down(
                L.hidden, L.b_down, down_sets[h], quarter, L.ints.span[h], which, came
            )

        came = [send(down_of(h, 1), to_core) for h in range(ZH)]
        pieces, places = [], []
        for h in range(ZH):
            parts = down_of(h, 0, came[h])
            terms = [parts[0]]
            terms += [send(parts[j * 2 + i], to_xzl[(i, j)]) for j in (0, 1) for i in (0, 1) if i or j]
            done = finish(L.hidden_state, terms, L.ints.span[h])
            for k in range(Y):
                there_y = done if k == 0 else send(done, from_y[k])
                for s, got in ((0, there_y), (1, send(there_y, to_core))):
                    pieces.append(got)
                    places += [((y + k) % Y) * 2 + (c ^ s), there[h]]
        return assemble(pieces, ints(places), tokens.shape)

    return body


def solution(mesh):
    in_specs = (
        P("req", None),
        P("req", None),
        P("req", None),
        P("req", None, "tp"),
        P("tp", "req"),
        P("req", "tp"),
        P("req", "tp"),
        P("tp", "req"),
        P(),
        P(None, None, "tp"),
        P("tp", None),
        P(),
        P(),
        P(None, "tp"),
        P(),
        P(None, "tp"),
        P("tp", None),
        P(),
    )
    return jax.shard_map(
        make_body(mesh.shape["req"], mesh.shape["tp"]),
        mesh=mesh, in_specs=in_specs, out_specs=P("req", None), check_vma=False,
    )
```

```python
import math

import jax
import jax.numpy as jnp
from jax import lax
from jax.experimental import pallas as pl
from jax.experimental.pallas import tpu as pltpu
from jax.sharding import PartitionSpec as P

HD = 128
RANK = 16
AXES = ("req", "tp")
epsilon = 1e-05
rope_base = 10000.0
F32 = jnp.float32
BF16 = jnp.bfloat16
VM = pltpu.VMEM
PARAMS = pltpu.CompilerParams(vmem_limit_bytes=56 * 2**20)
COST = pl.CostEstimate(flops=1000, bytes_accessed=1000, transcendentals=0)


def dot(a, b):
    return jnp.dot(a, b, preferred_element_type=F32)


def layer_norm(values):
    row_mean = jnp.mean(values, axis=-1, keepdims=True)
    centred = values - row_mean
    spread = jnp.mean(centred * centred, axis=-1, keepdims=True)
    return (centred * lax.rsqrt(spread + epsilon)).astype(BF16)


def masked(inner, adapter_column):
    rank = lax.broadcasted_iota(jnp.int32, inner.shape, 1) // RANK
    return jnp.where(adapter_column == rank, inner, F32(0.0)).astype(BF16)


def whole(array):
    return pl.BlockSpec(array.shape, lambda *_: (0,) * array.ndim, pipeline_mode=pl.Buffered(1))


def mm(start, size):
    return pl.ds(pl.multiple_of(start * size, size), size)


def dma(source, target, semaphore):
    return pltpu.make_async_copy(source, target, semaphore)


SMEM_SPEC = pl.BlockSpec(memory_space=pltpu.SMEM)
VMEM_SPEC = pl.BlockSpec(memory_space=VM)
HBM_SPEC = pl.BlockSpec(memory_space=pl.ANY)


def norm_rows(tokens, row, T):
    slots, width = tokens.shape
    piece = slots // T

    def kernel(row_ref, tok_ref, out, part):
        i = pl.program_id(0)
        normed = layer_norm(tok_ref[...].astype(F32))
        out[...] = normed

        @pl.when(i == row_ref[0])
        def _():
            part[...] = normed

    return pl.pallas_call(
        kernel,
        grid_spec=pltpu.PrefetchScalarGridSpec(
            num_scalar_prefetch=1,
            grid=(T,),
            in_specs=[pl.BlockSpec((piece, width), lambda i, r: (i, 0))],
            out_specs=[
                pl.BlockSpec((piece, width), lambda i, r: (i, 0)),
                pl.BlockSpec((piece, width), lambda i, r: (0, 0)),
            ],
        ),
        out_shape=[
            jax.ShapeDtypeStruct((slots, width), BF16),
            jax.ShapeDtypeStruct((piece, width), BF16),
        ],
        compiler_params=PARAMS,
        cost_estimate=COST,
        name="norm_rows",
    )(row, tokens)


def pack(gate, up, b):
    rows, columns = gate.shape
    quarter = columns // 4

    def spec(which):
        return pl.BlockSpec((rows, quarter), lambda i, o: (0, o[0] ^ (i * 2 + which)))

    def kernel(b_ref, g0, u0, g1, u1, keep, give):
        keep[0, :, :quarter], keep[0, :, quarter:] = g0[...], u0[...]
        give[0, :, :quarter], give[0, :, quarter:] = g1[...], u1[...]

    out = pl.BlockSpec((1, rows, 2 * quarter), lambda i, o: (i, 0, 0))
    return pl.pallas_call(
        kernel,
        grid_spec=pltpu.PrefetchScalarGridSpec(
            num_scalar_prefetch=1,
            grid=(2,),
            in_specs=[spec(0), spec(0), spec(1), spec(1)],
            out_specs=[out, out],
        ),
        out_shape=[jax.ShapeDtypeStruct((2, rows, 2 * quarter), BF16)] * 2,
        compiler_params=PARAMS,
        cost_estimate=COST,
        name="pack",
    )(b, gate, up, gate, up)


def join(own, came, x):
    rows, columns = own.shape[1:]
    spec = pl.BlockSpec((1, rows, columns), lambda i: (i, 0, 0))
    shape = jax.ShapeDtypeStruct((2 * rows, columns), BF16)

    def kernel(x_ref, own_ref, came_ref, near, give):
        @pl.when(pl.program_id(0) == 0)
        def _():
            near[mm(x_ref[0], rows), :] = own_ref[0]
            near[mm(1 - x_ref[0], rows), :] = came_ref[0]

        @pl.when(pl.program_id(0) == 1)
        def _():
            give[mm(x_ref[0], rows), :] = own_ref[0]
            give[mm(1 - x_ref[0], rows), :] = came_ref[0]

    return pl.pallas_call(
        kernel,
        grid=(2,),
        in_specs=[SMEM_SPEC, spec, spec],
        out_specs=[pl.BlockSpec((2 * rows, columns), lambda i: (0, 0))] * 2,
        out_shape=[shape, shape],
        compiler_params=PARAMS,
        cost_estimate=COST,
        name="join",
    )(x, own, came)


def tables(lengths, adapters, scalars, slots, T):
    count = lengths.shape[1]
    piece = slots // T
    half = HD // 2

    def kernel(len_ref, ad_ref, at_ref, column, line, two, cosine, sine, rows):
        def layout(index, slot, wants):
            end = jnp.int32(0)
            request, start = jnp.zeros(slot.shape, jnp.int32), jnp.zeros(slot.shape, jnp.int32)
            adapter = jnp.full(slot.shape, ad_ref[index, 0], jnp.int32)
            for k in range(count):
                end = end + len_ref[index, k]
                past = slot >= end
                request = request + past.astype(jnp.int32)
                if wants and k + 1 < count:
                    start = jnp.where(past, end, start)
                    adapter = jnp.where(past, ad_ref[index, k + 1], adapter)
            return request, slot - start, adapter

        lane = lax.broadcasted_iota(jnp.int32, (1, HD), 1)
        frequency = jnp.exp((lane % half).astype(F32) * F32(-math.log(rope_base) * 2.0 / HD))
        for i in range(2):
            index = at_ref[0] * 2 + i
            down = lax.broadcasted_iota(jnp.int32, (slots, 1), 0)
            request, position, adapter = layout(index, down, True)
            column[i] = request
            line[i] = layout(index, lax.broadcasted_iota(jnp.int32, (1, slots), 1), False)[0]
            here = slice(i * slots, (i + 1) * slots)
            two[here] = adapter
            angles = position.astype(F32) * frequency
            cosine[here] = jnp.cos(angles)
            sine[here] = jnp.where(lane < half, -jnp.sin(angles), jnp.sin(angles))
        for s in range(2):
            first = (at_ref[1] * 2 + (at_ref[2] ^ s)) * piece
            slot = first + lax.broadcasted_iota(jnp.int32, (piece, 1), 0)
            for b in range(4):
                to = (s * 4 + b) * piece
                rows[to : to + piece] = layout(at_ref[3] ^ b, slot, True)[2]

    table = jax.ShapeDtypeStruct((2 * slots, HD), F32)
    return pl.pallas_call(
        kernel,
        in_specs=[SMEM_SPEC] * 3,
        out_specs=[VMEM_SPEC] * 6,
        out_shape=[
            jax.ShapeDtypeStruct((2, slots, 1), jnp.int32),
            jax.ShapeDtypeStruct((2, 1, slots), jnp.int32),
            jax.ShapeDtypeStruct((2 * slots, 1), jnp.int32),
            table,
            table,
            jax.ShapeDtypeStruct((8 * piece, 1), jnp.int32),
        ],
        compiler_params=PARAMS,
        cost_estimate=COST,
        name="tables",
    )(lengths, adapters, scalars)


def finish(hidden_state, terms, at):
    piece, columns = terms[0].shape
    spec = pl.BlockSpec((piece, columns), lambda i, a: (0, 0))

    def kernel(at_ref, hidden_ref, *refs):
        total = hidden_ref[...]
        for ref in refs[:-1]:
            total = total + ref[...].astype(F32)
        refs[-1][...] = total.astype(BF16)

    return pl.pallas_call(
        kernel,
        grid_spec=pltpu.PrefetchScalarGridSpec(
            num_scalar_prefetch=1,
            grid=(1,),
            in_specs=[pl.BlockSpec((piece, columns), lambda i, a: (0, a[0]))] + [spec] * len(terms),
            out_specs=spec,
        ),
        out_shape=jax.ShapeDtypeStruct((piece, columns), BF16),
        compiler_params=PARAMS,
        cost_estimate=COST,
        name="finish",
    )(at, hidden_state, *terms)


def project_qkv(own, pieces, adapter, a, b, cosine, sine, weights, places):
    slots, width = own.shape
    total_rows, columns, rank = 2 * slots, b.shape[1], b.shape[0]
    piece, size, tile = pieces[0].shape[0], width // len(weights), columns // 3
    n_pieces, n_weights = len(pieces), len(weights)
    chunk = total_rows // 2
    column = adapter

    def kernel(at_ref, adapter_ref, a_ref, cos_ref, sin_ref, own_ref, b_ref, *refs):
        p_in, w_in, rest = refs[:n_pieces], refs[n_pieces : n_pieces + n_weights], refs[-7:]
        out, x, w, bb, low, x_sem, w_sem = rest

        def weight_copies(step, slot):
            to = pl.ds(step * tile, tile)
            for i in range(n_weights):
                yield dma(
                    w_in[i].at[:, to],
                    w.at[slot, mm(at_ref[1 + n_pieces + i], size), :],
                    w_sem.at[slot, i],
                )
            yield dma(b_ref.at[:, to], bb.at[slot], w_sem.at[slot, n_weights])

        x_copies = [dma(own_ref, x.at[mm(at_ref[0], slots), :], x_sem.at[n_pieces])]
        for i in range(n_pieces):
            x_copies.append(dma(p_in[i], x.at[mm(at_ref[1 + i], piece), :], x_sem.at[i]))
        for copy in x_copies:
            copy.start()
        for copy in weight_copies(0, 0):
            copy.start()
        for copy in x_copies:
            copy.wait()
        for step in range(3):
            slot = step % 2
            if step < 2:
                for copy in weight_copies(step + 1, 1 - slot):
                    copy.start()
            for copy in weight_copies(step, slot):
                copy.wait()

            @pl.loop(0, total_rows // chunk)
            def _(m):
                at = mm(m, chunk)
                xs = x[at, :]
                if step == 0:
                    low[at, :] = masked(dot(xs, a_ref[...]), adapter_ref[at, :])
                total = dot(xs, w[slot]) + dot(low[at, :], bb[slot])
                for h in range(tile // HD):
                    v = total[:, h * HD : (h + 1) * HD]
                    if step < 2:
                        v = v * cos_ref[at, :] + pltpu.roll(v, HD // 2, 1) * sin_ref[at, :]
                    start = step * tile + h * HD
                    out[at, start : start + HD] = v.astype(BF16)

    return pl.pallas_call(
        kernel,
        in_specs=[SMEM_SPEC] + [VMEM_SPEC] * 4 + [HBM_SPEC] * (2 + n_pieces + n_weights),
        out_specs=VMEM_SPEC,
        out_shape=jax.ShapeDtypeStruct((total_rows, columns), BF16),
        scratch_shapes=[
            VM((total_rows, width), BF16),
            VM((2, width, tile), BF16),
            VM((2, rank, tile), BF16),
            VM((total_rows, rank), BF16),
            pltpu.SemaphoreType.DMA((n_pieces + 1,)),
            pltpu.SemaphoreType.DMA((2, n_weights + 1)),
        ],
        compiler_params=PARAMS,
        cost_estimate=COST,
        name="project_qkv",
    )(places, column, a, cosine, sine, own, b, *pieces, *weights)


def attend(qkv, column, line):
    indices, slots = column.shape[:2]
    heads = qkv.shape[1] // 3 // HD
    rows = 256 if slots % 256 == 0 else slots

    def kernel(q, k, v, column_ref, line_ref, out):
        for at in range(0, slots, rows):
            seen = at + rows
            s = lax.dot_general(
                q[at:seen], k[:seen], (((1,), (1,)), ((), ())), preferred_element_type=F32
            )
            s = s * (1.0 / math.sqrt(HD))
            here = at + lax.broadcasted_iota(jnp.int32, s.shape, 0)
            there = lax.broadcasted_iota(jnp.int32, s.shape, 1)
            allowed = (column_ref[0, at:seen] == line_ref[0, :, :seen]) & (here >= there)
            s = jnp.where(allowed, s, F32(-1e30))
            e = jnp.exp(s - jnp.max(s, axis=1, keepdims=True))
            weights = (e * (1.0 / jnp.sum(e, axis=1, keepdims=True))).astype(BF16)
            out[at:seen] = dot(weights, v[:seen]).astype(BF16)

    return pl.pallas_call(
        kernel,
        grid=(indices, heads),
        in_specs=[
            pl.BlockSpec((slots, HD), lambda i, h: (i, h)),
            pl.BlockSpec((slots, HD), lambda i, h: (i, heads + h)),
            pl.BlockSpec((slots, HD), lambda i, h: (i, 2 * heads + h)),
            pl.BlockSpec((1, slots, 1), lambda i, h: (i, 0, 0)),
            pl.BlockSpec((1, 1, slots), lambda i, h: (i, 0, 0)),
        ],
        out_specs=pl.BlockSpec((slots, HD), lambda i, h: (i, h)),
        out_shape=jax.ShapeDtypeStruct((indices * slots, heads * HD), BF16),
        compiler_params=PARAMS,
        cost_estimate=COST,
        name="attend",
    )(qkv, qkv, qkv, column, line)


def project_out(attn, adapter, a, b, weights, order, scalars, T, came=None):
    total_rows, depth = attn.shape
    n, slots, piece, Y = len(weights), total_rows // 2, total_rows // 2 // T, T // 2
    extra = list(came or [])
    flat = [p for w in weights for p in w]
    size = sum(p.shape[1] for p in flat) // n // 2
    half, columns = total_rows // 2, n * 2 * size
    per = n // max(1, len(extra))

    def kernel(order_ref, at_ref, attn_ref, adapter_ref, a_ref, b_ref, *refs):
        ws, outs, rows, low = refs[: len(flat)], refs[len(flat) + len(extra) : -2], *refs[-2:]
        x, y, c = at_ref[0], at_ref[1], at_ref[2]
        mine = a_ref[mm(x, depth), :]
        for i in range(2):
            for k in range(Y):
                here = mm((x ^ i) * T + lax.rem(y + Y - k, Y) * 2 + c, piece)
                to = (i * Y + k) * piece
                part = attn_ref[here, :]
                rows[to : to + piece] = part
                low[to : to + piece] = masked(dot(part, mine), adapter_ref[here, :])
        it = iter(ws)
        for k, w in enumerate(weights):
            blocks = []
            for p in w:
                ref = next(it)
                for start in range(0, p.shape[1], size):
                    blocks.append((ref, start))
            for i, (ref, start) in enumerate(blocks):
                there = mm(order_ref[2 * k + i], size)
                to = mm(k * 2 + (x ^ i), size)
                total = dot(rows[...], ref[:, start : start + size]) + dot(low[...], b_ref[:, there])
                if came is None:
                    outs[0][:, to] = total.astype(BF16)
                else:
                    from_core = refs[len(flat) + k // per][:, mm(k % per * 2 + (x ^ i), size)]
                    total = (total + from_core.astype(F32)).astype(BF16)
                    for p in range(2 * Y):
                        outs[p][:, to] = total[p * piece : (p + 1) * piece]

    shapes = [jax.ShapeDtypeStruct((half, columns), BF16)]
    if came is not None:
        shapes = [jax.ShapeDtypeStruct((piece, columns), BF16)] * (2 * Y)
    out = pl.pallas_call(
        kernel,
        in_specs=[SMEM_SPEC, SMEM_SPEC] + [VMEM_SPEC] * (4 + len(flat) + len(extra)),
        out_specs=[VMEM_SPEC] * len(shapes),
        out_shape=shapes,
        scratch_shapes=[VM((half, depth), BF16), VM((half, a.shape[1]), BF16)],
        compiler_params=PARAMS,
        cost_estimate=COST,
        name="project_out",
    )(order, scalars, attn, adapter, a, b, *flat, *extra)
    return out[0] if came is None else out


def residual_norm(tokens, row, order, chunks):
    width = tokens.shape[1]
    n = order.shape[0]
    piece, size, per = chunks[0][0].shape[0], width // n, n // len(chunks)
    flat = [term for chunk in chunks for term in chunk]

    def kernel(row_ref, order_ref, tok_ref, *refs):
        it, hidden, normed = iter(refs[:-2]), refs[-2], refs[-1]
        for c, chunk in enumerate(chunks):
            total = next(it)[...].astype(F32)
            for _ in chunk[1:]:
                total = total + next(it)[...].astype(F32)
            for place in range(per):
                to = mm(order_ref[c * per + place], size)
                more = total[:, place * size : (place + 1) * size]
                hidden[:, to] = tok_ref[:, to].astype(F32) + more
        normed[...] = layer_norm(hidden[...])

    return pl.pallas_call(
        kernel,
        grid_spec=pltpu.PrefetchScalarGridSpec(
            num_scalar_prefetch=2,
            grid=(1,),
            in_specs=[
                pl.BlockSpec((piece, width), lambda n, r, o: (r[0], 0)),
                *[pl.BlockSpec(p.shape, lambda n, r, o: (0, 0)) for p in flat],
            ],
            out_specs=[pl.BlockSpec((piece, width), lambda n, r, o: (0, 0))] * 2,
        ),
        out_shape=[
            jax.ShapeDtypeStruct((piece, width), F32),
            jax.ShapeDtypeStruct((piece, width), BF16),
        ],
        compiler_params=PARAMS,
        cost_estimate=COST,
        name="residual_norm",
    )(row, order, tokens, *flat)


def gated(rows, adapters, a_gate, a_up, sets, places, unit):
    width = rows[0].shape[1]
    total_rows = sum(row.shape[0] for row in rows)
    units = sets[0][1].shape[1] // 2
    tile = min(256, units)
    tiles = units // tile
    rank = a_gate.shape[1]
    column = adapters
    flat = [w for s in sets for w in s[0]]
    first = [sum(len(s[0]) for s in sets[:k]) for k in range(len(sets) + 1)]
    bs = [s[1] for s in sets]
    downs = [s[2] for s in sets]
    n_rows, n_sets = len(rows), len(sets)
    most = max(len(s[0]) for s in sets)
    steps = n_sets * tiles
    chunk = total_rows // 2
    hidden_width = n_sets * units

    def kernel(place_ref, adapter_ref, ag_ref, au_ref, *refs):
        it = iter(refs)
        take = lambda k: [next(it) for _ in range(k)]
        x_in, w_in, b_in, d_in = take(n_rows), take(len(flat)), take(n_sets), take(n_sets)
        hidden, x, w, bb, lg, lu, ld, x_sem, w_sem, b_sem = take(10)

        def weight_copies(step, slot):
            s, t = divmod(step, tiles)
            for g in range(2):
                for i in range(first[s], first[s + 1]):
                    yield dma(
                        w_in[i].at[:, pl.ds(g * units + t * tile, tile)],
                        w.at[slot, g, pl.ds(pl.multiple_of(place_ref[i] * unit, unit), flat[i].shape[0]), :],
                        w_sem.at[slot, g, i - first[s]],
                    )
                yield dma(
                    b_in[s].at[:, pl.ds(g * units + t * tile, tile)],
                    bb.at[slot, g],
                    b_sem.at[slot, g],
                )

        x_copies, start = [], 0
        for i in range(n_rows):
            x_copies.append(dma(x_in[i], x.at[pl.ds(start, rows[i].shape[0]), :], x_sem.at[i]))
            start += rows[i].shape[0]
        for copy in x_copies:
            copy.start()
        for copy in weight_copies(0, 0):
            copy.start()
        for copy in x_copies:
            copy.wait()
        for step in range(steps):
            slot = step % 2
            if step + 1 < steps:
                for copy in weight_copies(step + 1, 1 - slot):
                    copy.start()
            for copy in weight_copies(step, slot):
                copy.wait()
            s, t = divmod(step, tiles)

            for m in range(total_rows // chunk):
                at = slice(m * chunk, (m + 1) * chunk)
                xs = x[at, :]
                if step == 0:
                    lg[at, :] = masked(dot(xs, ag_ref[...]), adapter_ref[at, :])
                    lu[at, :] = masked(dot(xs, au_ref[...]), adapter_ref[at, :])
                gate = dot(xs, w[slot, 0]) + dot(lg[at, :], bb[slot, 0])
                up = dot(xs, w[slot, 1]) + dot(lu[at, :], bb[slot, 1])
                h = (0.5 * gate * (1.0 + jnp.tanh(0.5 * gate)) * up).astype(BF16)
                hidden[at, step * tile : (step + 1) * tile] = h
                more = dot(h, d_in[s][t * tile : (t + 1) * tile, :])
                if step > 0:
                    more = more + ld[at, :]
                if step < steps - 1:
                    ld[at, :] = more
                else:
                    hidden[at, hidden_width:] = masked(more, adapter_ref[at, :])

    return pl.pallas_call(
        kernel,
        in_specs=[SMEM_SPEC] + [VMEM_SPEC] * 3
        + [HBM_SPEC] * (n_rows + len(flat) + n_sets)
        + [VMEM_SPEC] * n_sets,
        out_specs=VMEM_SPEC,
        out_shape=jax.ShapeDtypeStruct((total_rows, hidden_width + rank), BF16),
        scratch_shapes=[
            VM((total_rows, width), BF16),
            VM((2, 2, width, tile), BF16),
            VM((2, 2, rank, tile), BF16),
            VM((total_rows, rank), BF16),
            VM((total_rows, rank), BF16),
            VM((total_rows, rank), F32),
            pltpu.SemaphoreType.DMA((n_rows,)),
            pltpu.SemaphoreType.DMA((2, 2, most)),
            pltpu.SemaphoreType.DMA((2, 2)),
        ],
        compiler_params=PARAMS,
        cost_estimate=COST,
        name="gated",
    )(places, column, a_gate, a_up, *rows, *flat, *bs, *downs)


def project_down(hidden, b, sets, units, at, which, came=None):
    half, depth = hidden.shape[0] // 2, hidden.shape[1]
    piece, rank = half // 4, b.shape[0]
    size = sets[0][0].shape[1]
    flat = [w for group in sets for w in group]
    n, n_sets, n_weights = 4, len(sets), len(flat)
    extra = [] if came is None else [came]

    def kernel(at_ref, h_in, *refs):
        refs = list(refs)
        came_ref = refs.pop(0) if extra else None
        b_ref, w_in, outs = refs[0], refs[1 : 1 + n_weights], refs[1 + n_weights : -4]
        w, h_ref, sems, h_sems = refs[-4:]
        copies = [
            dma(
                b_ref.at[:, mm(at_ref[0], n * size)],
                w.at[n_sets * units : n_sets * units + rank, :],
                sems.at[n_sets * n],
            )
        ]
        h_copies = [
            dma(
                h_in.at[pl.ds(which * half + m * 2 * piece, 2 * piece), :],
                h_ref.at[pl.ds(m * 2 * piece, 2 * piece), :],
                h_sems.at[m],
            )
            for m in range(2)
        ]
        it = iter(w_in)
        for k, group in enumerate(sets):
            place = 0
            for array in group:
                ref = next(it)
                for i in range(array.shape[0] // units):
                    copies.append(
                        dma(
                            ref.at[pl.ds(i * units, units), :],
                            w.at[k * units : (k + 1) * units, mm(at_ref[1] ^ place, size)],
                            sems.at[k * n + place],
                        )
                    )
                    place += 1
        for copy in copies + h_copies:
            copy.start()
        for copy in copies:
            copy.wait()
        for m in range(2):
            h_copies[m].wait()
            here = slice(m * 2 * piece, (m + 1) * 2 * piece)
            total = dot(h_ref[here, :], w[...])
            if came is None:
                outs[0][here, :] = total.astype(BF16)
            else:
                total = (total + came_ref[here, :].astype(F32)).astype(BF16)
                outs[2 * m][...], outs[2 * m + 1][...] = total[:piece], total[piece:]

    shapes = [jax.ShapeDtypeStruct((half, n * size), BF16)]
    if came is not None:
        shapes = [jax.ShapeDtypeStruct((piece, n * size), BF16)] * 4
    out = pl.pallas_call(
        kernel,
        in_specs=[SMEM_SPEC, HBM_SPEC]
        + [VMEM_SPEC] * len(extra)
        + [HBM_SPEC] * (1 + n_weights),
        out_specs=[VMEM_SPEC] * len(shapes),
        out_shape=shapes,
        scratch_shapes=[
            VM((depth, n * size), BF16),
            VM((half, depth), BF16),
            pltpu.SemaphoreType.DMA((n_sets * n + 1,)),
            pltpu.SemaphoreType.DMA((2,)),
        ],
        compiler_params=PARAMS,
        cost_estimate=COST,
        name="project_down",
    )(at, hidden, *extra, b, *flat)
    return out[0] if came is None else out


def assemble(pieces, places, shape):
    rows, columns = pieces[0].shape

    def kernel(places_ref, *refs):
        out = refs[-1]
        for i in range(len(pieces)):
            to = mm(places_ref[2 * i], rows), mm(places_ref[2 * i + 1], columns)
            out[to] = refs[i][...]

    return pl.pallas_call(
        kernel,
        in_specs=[SMEM_SPEC] + [VMEM_SPEC] * len(pieces),
        out_specs=VMEM_SPEC,
        out_shape=jax.ShapeDtypeStruct(shape, BF16),
        compiler_params=PARAMS,
        cost_estimate=COST,
        name="assemble",
    )(places, *pieces)


@jax.tree_util.register_pytree_node_class
class Live:
    def __init__(self, **arrays):
        self.__dict__.update(arrays)

    def tree_flatten(self):
        names = tuple(sorted(self.__dict__))
        return [self.__dict__[name] for name in names], names

    @classmethod
    def tree_unflatten(cls, names, arrays):
        return cls(**dict(zip(names, arrays)))

    @property
    def pop(self):
        return Pop(self)

    @property
    def drop(self):
        return Drop(self)


class Pop:
    def __init__(self, live):
        self.__dict__.update(live=live)

    def __getattr__(self, name):
        return self.live.__dict__.pop(name)


class Drop(Pop):
    def __getattr__(self, name):
        self.live.__dict__.pop(name)
        return self


def make_body(R, T):
    Z, ZH, Y = R // 2, R // 4, T // 2

    def flat(z, x, y, c):
        return (z * 2 + x) * T + y * 2 + c

    def move(f):
        every = [(r // 2, r % 2, t // 2, t % 2) for r in range(R) for t in range(T)]
        return [(flat(*d), flat(*f(*d))) for d in every]

    def send(value, pairs):
        return lax.ppermute(value, AXES, pairs)

    to_core = move(lambda z, x, y, c: (z, x, y, 1 - c))
    to_x = move(lambda z, x, y, c: (z, 1 - x, y, c))
    z_up = move(lambda z, x, y, c: ((z + 1) % Z, x, y, c))
    z_down = move(lambda z, x, y, c: ((z - 1) % Z, x, y, c))
    from_y = {k: move(lambda z, x, y, c, k=k: (z, x, (y - k) % Y, c)) for k in range(1, Y)}
    same_xzl = [[zh * 4 + b for b in range(4)] for zh in range(ZH)]
    same_zh = [[zh * 4 + b for zh in range(ZH)] for b in range(4)]
    to_xy = {
        (i, k): move(lambda z, x, y, c, i=i, k=k: (z, x ^ i, (y - k) % Y, c))
        for i in (0, 1)
        for k in range(Y)
    }
    to_xzl = {
        (i, j): move(lambda z, x, y, c, i=i, j=j: (z ^ j, x ^ i, y, c))
        for j in (0, 1)
        for i in (0, 1)
    }

    from_zh = {
        k: move(lambda z, x, y, c, k=k: ((z - 2 * k) % Z, x, y, c)) for k in range(1, ZH)
    }
    to_zl = move(lambda z, x, y, c: (z ^ 1, x, y, c))

    def spread(value, axes, groups):
        return lax.all_to_all(value, axes, 0, 0, axis_index_groups=groups, tiled=True)

    def fence(live):
        return lax.optimization_barrier(live)

    def body(
        tokens, lengths, request_adapter, w_qkv, w_out, w_gate, w_up, w_down,
        a_qkv, b_qkv, a_out, b_out, a_gate, b_gate, a_up, b_up, a_down, b_down,
    ):
        r, t = lax.axis_index("req"), lax.axis_index("tp")
        z, x, y, c = r // 2, r % 2, t // 2, t % 2
        zh, zl = z // 2, z % 2
        slots, width = tokens.shape
        piece = slots // T
        block = width // R
        local = w_qkv.shape[2] // 2
        rank = a_qkv.shape[1]
        quarter = w_gate.shape[1] // 4
        span = width // ZH
        count = lengths.shape[1]
        far_y, far_zh, opposite = range(1, Y), range(1, ZH), Z // 2

        def cut(array, start, size, axis):
            return lax.dynamic_slice_in_dim(array, start, size, axis)

        def ints(values):
            return jnp.stack([jnp.asarray(v, jnp.int32) for v in values])

        L = Live(
            tokens=tokens, both=jnp.concatenate([lengths, request_adapter], axis=1), w_gate=w_gate,
            w_up=w_up, a_qkv=a_qkv, a_out=a_out, b_out=b_out, a_gate=a_gate,
            a_up=a_up, b_down=b_down, b_qkv=b_qkv, b_gate=b_gate, b_up=b_up, a_down=a_down,
        )
        keys = [(k, i) for k in range(Z) for i in (0, 1)]
        order = [((z + k) % Z) * 2 + (x ^ i) for k, i in keys]
        there = [(zh + h) % ZH for h in range(ZH)]
        at = [(1 - x) * T + ((y + k) % Y) * 2 + s for s in (c, 1 - c) for k in range(Y)]
        far_places = []
        for h in there[1:]:
            first, other = (h * 2 + zl) * 4, (h * 2 + 1 - zl) * 4
            far_places += [first, first + 2, other, other + 1]
        places = ([(zh * 2 + zl) * 4, (zh * 2 + 1 - zl) * 4] + far_places) * Y
        L.ints = Live(
            t=ints([t]), order=[ints(order[:Z]), ints(order[Z:]), ints(order)], qkv=ints([x, *at, *order]),
            xyc=[ints([x, y, c]), ints([x, y, 1 - c])],
            zyc=ints([zl, y, c, zl * 2 + x]), z=ints([(z + k) % Z for k in range(Z)]),
            gated=ints(places), span=[ints([h]) for h in there],
            down=[ints([h, zl * 2 + x]) for h in there], b=ints([zl * 2 + x]),
        )
        mine = (zl * 2 + x) * quarter

        def heads_of(w, which):
            return cut(w, which * local, local, 2).reshape(w.shape[0], 3 * local)


        def ring_start(own):
            left = right = own
            got = {0: own}
            for k in range(1, opposite):
                left, right = send(left, z_up), send(right, z_down)
                got[Z - k], got[k] = left, right
            return got

        L.first = send(heads_of(w_qkv, 1 - x), to_x)
        L.ring = [ring_start(heads_of(w_qkv, x))]
        L.out = send(cut(w_out, (1 - x) * local, local, 0), to_x)
        L.both = spread(jnp.concatenate([L.both] * 4, axis=0), "req", same_xzl)
        L.normed, L.mine = norm_rows(L.tokens, L.ints.t, T)
        L.b = jnp.concatenate(
            [cut(L.pop.b_gate, mine, quarter, 1), cut(L.pop.b_up, mine, quarter, 1)], axis=1
        )
        L.a_down = cut(L.a_down, mine, quarter, 0)
        L.b_heads = cut(L.pop.b_qkv, x * local, local, 2).reshape(rank, 3 * local)
        L.own_out = cut(w_out, x * local, local, 0)
        me = zl * 2 + x
        L.down_keep = [cut(w_down, (me ^ b) * quarter, quarter, 0) for b in (0, 2)]
        L.down_give = jnp.concatenate([cut(w_down, (me ^ b) * quarter, quarter, 0) for b in (1, 3)], 0)
        L = fence(L)

        L.ring.append(ring_start(L.pop.first))
        L.quarter = send(L.pop.mine, to_x)
        L.b_far = [send(L.b, from_y[k]) for k in far_y]
        L.a_far = [send(L.a_down, from_y[k]) for k in far_y]
        L.gu, L.gu_give = pack(L.pop.w_gate, L.pop.w_up, L.ints.b)
        L.out = jnp.concatenate([L.pop.own_out, L.out], axis=1)
        L = fence(L)

        L.ring[0][opposite] = send(L.ring[0][opposite + 1], z_up)
        L.ring[1][opposite] = send(L.ring[1][opposite - 1], z_down)
        L.quarters = [L.quarter] + [send(L.quarter, from_y[k]) for k in far_y]
        L.out = ring_start(L.out)
        L.gu_came = send(L.pop.gu_give, to_x)
        both = L.pop.both
        L.tables = tables(both[:, :count], both[:, count:], L.ints.zyc, slots, T)
        L = fence(L)
        L.quarters = L.quarters + [send(q, to_core) for q in L.quarters]
        L.for_out = [L.out[opposite + 1][:, :block], L.out[opposite - 1][:, block:]]
        L.near, L.give = join(L.pop.gu, L.pop.gu_came, L.ints.xyc[0])
        L = fence(L)

        one, two = L.pop.for_out
        L.far_out = [send(one, z_up), send(two, z_down)]
        L.far = send(L.pop.give, to_zl)
        L.y = [[send(L.near, from_y[k]) for k in far_y]]
        L.down_came = send(L.pop.down_give, to_x)
        column, line, adapter, cosine, sine, adapters = L.tables
        L.joined = project_qkv(
            L.pop.normed, L.pop.quarters, adapter, L.pop.a_qkv, L.pop.b_heads, cosine,
            sine, [L.ring[i][k] for k, i in keys], L.ints.qkv,
        )
        L.pop.ring
        L = fence(L)

        def over_zh(w):
            return [send(w, from_zh[h]) for h in far_zh]

        def relay(arrays):
            return [[send(w, from_y[k]) for w in arrays] for k in far_y]

        def out_of(chunk, core, came=None):
            return project_out(
                attn, adapter, L.a_out, L.b_out, blocks[chunk], L.ints.order[chunk],
                L.ints.xyc[core], T, came,
            )

        rows = L.near.shape[0] // 2
        L.near_parts = [L.near[:rows], L.near[rows:]]
        L.y.append([send(L.far, from_y[k]) for k in far_y])
        keep, down_came = L.pop.down_keep, L.pop.down_came
        L.down_near = jnp.concatenate([keep[0], down_came[:quarter]], axis=0)
        L.down_far = send(jnp.concatenate([keep[1], down_came[quarter:]], axis=0), to_zl)
        L.zh0 = over_zh(L.near_parts[0])
        column, line, adapter, cosine, sine, adapters = L.pop.tables
        attn = attend(L.pop.joined, column, line)
        blocks = [(L.out[k],) if k != opposite else tuple(L.far_out) for k in range(Z)]
        blocks = [blocks[:opposite], blocks[opposite:], blocks]
        L.gives = [out_of(chunk, 1) for chunk in (0, 1)]
        L.attn, L.adapter, L.adapters, L.blocks = attn, adapter, adapters, blocks
        L.drop.out.far_out.quarter
        L = fence(L)
        part = rows_unit = rows // 2
        L.far_parts = [L.far[:part], L.far[part:]]
        L.zh2 = over_zh(L.far_parts[0])
        L.relay0 = relay(L.zh0)
        attn, adapter, blocks = L.pop.attn, L.pop.adapter, L.pop.blocks
        L.parts = out_of(2, 0, [send(give, to_core) for give in L.pop.gives])
        L.drop.a_out.b_out
        L = fence(L)

        parts = L.pop.parts
        terms = [parts[0]]
        for i in (0, 1):
            for k in range(Y):
                if i or k:
                    terms.append(send(parts[i * Y + k], to_xy[(i, k)]))
        L.zh3 = over_zh(L.far_parts[1])
        L.terms = terms
        L = fence(L)
        L.hidden_state, L.normed2 = residual_norm(
            L.pop.tokens, L.ints.t, L.ints.z, [L.pop.terms]
        )
        L.for_down = [L.pop.down_near, L.pop.down_far]
        L = fence(L)

        own = L.pop.normed2
        L.rows = [own, send(own, to_x), send(own, to_zl)]
        L.relay3 = relay(L.zh3)
        L.zh1 = over_zh(L.near_parts[1])
        L.down_y = [[send(L.for_down[0], from_y[k]) for k in far_y]]
        L.cut = [L.rows[1][: piece // 2], L.rows[2][piece // 2 :]]
        L = fence(L)
        one, two = L.pop.cut
        L.rows += [send(one, to_zl), send(two, to_x)]
        L.relay1, L.relay2 = relay(L.zh1), relay(L.zh2)
        L.down_zh = [over_zh(L.for_down[0])]
        L = fence(L)
        L.rows += [send(row, to_core) for row in L.rows]
        L = fence(L)

        L.down_zh.append(over_zh(L.for_down[1]))
        L.down_y.append([send(L.for_down[1], from_y[k]) for k in far_y])
        L.down_zh_y = [relay(L.down_zh[0])]
        zh_blocks = [part[h] for h in range(ZH - 1) for part in (L.zh0, L.zh1, L.zh2, L.zh3)]
        sets = [([L.near, L.far, *zh_blocks], L.b, L.a_down)]
        for k in range(Y - 1):
            relayed = [part[k][h] for h in range(ZH - 1) for part in (L.relay0, L.relay1, L.relay2, L.relay3)]
            sets.append(([L.y[0][k], L.y[1][k], *relayed], L.b_far[k], L.a_far[k]))
        L.hidden = gated(
            L.rows, L.adapters, L.pop.a_gate, L.pop.a_up, sets, L.ints.gated,
            rows_unit,
        )
        L.drop.near.far.near_parts.far_parts.zh0.zh1.zh2.zh3.relay0.relay1.relay2.relay3
        L.drop.b.a_down.y.b_far.a_far.rows
        L = fence(L)

        L.down_zh_y.append(relay(L.down_zh[1]))
        down_sets = [[L.for_down] + [[part[k] for part in L.down_y] for k in range(Y - 1)]]
        for h in range(ZH - 1):
            far = [[part[k][h] for part in L.down_zh_y] for k in range(Y - 1)]
            down_sets.append([[part[h] for part in L.down_zh]] + far)

        def down_of(h, which, came=None):
            return project_down(
                L.hidden, L.b_down, down_sets[h], quarter, L.ints.down[h], which, came
            )

        came = [send(down_of(h, 1), to_core) for h in range(ZH)]
        pieces, places = [], []
        for h in range(ZH):
            parts = down_of(h, 0, came[h])
            terms = [parts[0]]
            terms += [send(parts[j * 2 + i], to_xzl[(i, j)]) for j in (0, 1) for i in (0, 1) if i or j]
            done = finish(L.hidden_state, terms, L.ints.span[h])
            for k in range(Y):
                there_y = done if k == 0 else send(done, from_y[k])
                for s, got in ((0, there_y), (1, send(there_y, to_core))):
                    pieces.append(got)
                    places += [((y + k) % Y) * 2 + (c ^ s), there[h]]
        return assemble(pieces, ints(places), tokens.shape)

    return body


def solution(mesh):
    in_specs = (
        P("req", None),
        P("req", None),
        P("req", None),
        P("req", None, "tp"),
        P("tp", "req"),
        P("req", "tp"),
        P("req", "tp"),
        P("tp", "req"),
        P(),
        P(None, None, "tp"),
        P("tp", None),
        P(),
        P(),
        P(None, "tp"),
        P(),
        P(None, "tp"),
        P("tp", None),
        P(),
    )
    return jax.shard_map(
        make_body(mesh.shape["req"], mesh.shape["tp"]),
        mesh=mesh, in_specs=in_specs, out_specs=P("req", None), check_vma=False,
    )
```

```python
import math

import jax
import jax.numpy as jnp
from jax import lax
from jax.experimental import pallas as pl
from jax.experimental.pallas import tpu as pltpu
from jax.sharding import PartitionSpec as P

HD = 128
RANK = 16
AXES = ("req", "tp")
epsilon = 1e-05
rope_base = 10000.0
F32 = jnp.float32
BF16 = jnp.bfloat16
VM = pltpu.VMEM
PARAMS = pltpu.CompilerParams(vmem_limit_bytes=56 * 2**20)
COST = pl.CostEstimate(flops=1000, bytes_accessed=1000, transcendentals=0)


def dot(a, b):
    return jnp.dot(a, b, preferred_element_type=F32)


def layer_norm(values):
    row_mean = jnp.mean(values, axis=-1, keepdims=True)
    centred = values - row_mean
    spread = jnp.mean(centred * centred, axis=-1, keepdims=True)
    return (centred * lax.rsqrt(spread + epsilon)).astype(BF16)


def masked(inner, adapter_column):
    rank = lax.broadcasted_iota(jnp.int32, inner.shape, 1) // RANK
    return jnp.where(adapter_column == rank, inner, F32(0.0)).astype(BF16)


def whole(array):
    return pl.BlockSpec(array.shape, lambda *_: (0,) * array.ndim, pipeline_mode=pl.Buffered(1))


def mm(start, size):
    return pl.ds(pl.multiple_of(start * size, size), size)


def dma(source, target, semaphore):
    return pltpu.make_async_copy(source, target, semaphore)


SMEM_SPEC = pl.BlockSpec(memory_space=pltpu.SMEM)
VMEM_SPEC = pl.BlockSpec(memory_space=VM)
HBM_SPEC = pl.BlockSpec(memory_space=pl.ANY)


def norm_rows(tokens, row, T):
    slots, width = tokens.shape
    piece = slots // T

    def kernel(row_ref, tok_ref, out, part):
        i = pl.program_id(0)
        normed = layer_norm(tok_ref[...].astype(F32))
        out[...] = normed

        @pl.when(i == row_ref[0])
        def _():
            part[...] = normed

    return pl.pallas_call(
        kernel,
        grid_spec=pltpu.PrefetchScalarGridSpec(
            num_scalar_prefetch=1,
            grid=(T,),
            in_specs=[pl.BlockSpec((piece, width), lambda i, r: (i, 0))],
            out_specs=[
                pl.BlockSpec((piece, width), lambda i, r: (i, 0)),
                pl.BlockSpec((piece, width), lambda i, r: (0, 0)),
            ],
        ),
        out_shape=[
            jax.ShapeDtypeStruct((slots, width), BF16),
            jax.ShapeDtypeStruct((piece, width), BF16),
        ],
        compiler_params=PARAMS,
        cost_estimate=COST,
        name="norm_rows",
    )(row, tokens)


def pack(gate, up, b):
    rows, columns = gate.shape
    quarter = columns // 4

    def spec(which):
        return pl.BlockSpec((rows, quarter), lambda i, o: (0, o[0] ^ (i * 2 + which)))

    def kernel(b_ref, g0, u0, g1, u1, keep, give):
        keep[0, :, :quarter], keep[0, :, quarter:] = g0[...], u0[...]
        give[0, :, :quarter], give[0, :, quarter:] = g1[...], u1[...]

    out = pl.BlockSpec((1, rows, 2 * quarter), lambda i, o: (i, 0, 0))
    return pl.pallas_call(
        kernel,
        grid_spec=pltpu.PrefetchScalarGridSpec(
            num_scalar_prefetch=1,
            grid=(2,),
            in_specs=[spec(0), spec(0), spec(1), spec(1)],
            out_specs=[out, out],
        ),
        out_shape=[jax.ShapeDtypeStruct((2, rows, 2 * quarter), BF16)] * 2,
        compiler_params=PARAMS,
        cost_estimate=COST,
        name="pack",
    )(b, gate, up, gate, up)


def join(own, came, x):
    rows, columns = own.shape[1:]
    spec = pl.BlockSpec((1, rows, columns), lambda i: (i, 0, 0))
    shape = jax.ShapeDtypeStruct((2 * rows, columns), BF16)

    def kernel(x_ref, own_ref, came_ref, near, give):
        @pl.when(pl.program_id(0) == 0)
        def _():
            near[mm(x_ref[0], rows), :] = own_ref[0]
            near[mm(1 - x_ref[0], rows), :] = came_ref[0]

        @pl.when(pl.program_id(0) == 1)
        def _():
            give[mm(x_ref[0], rows), :] = own_ref[0]
            give[mm(1 - x_ref[0], rows), :] = came_ref[0]

    return pl.pallas_call(
        kernel,
        grid=(2,),
        in_specs=[SMEM_SPEC, spec, spec],
        out_specs=[pl.BlockSpec((2 * rows, columns), lambda i: (0, 0))] * 2,
        out_shape=[shape, shape],
        compiler_params=PARAMS,
        cost_estimate=COST,
        name="join",
    )(x, own, came)


def tables(lengths, adapters, scalars, slots, T):
    count = lengths.shape[1]
    piece = slots // T
    half = HD // 2

    def kernel(len_ref, ad_ref, at_ref, column, line, two, cosine, sine, rows):
        def layout(index, slot, wants):
            end = jnp.int32(0)
            request, start = jnp.zeros(slot.shape, jnp.int32), jnp.zeros(slot.shape, jnp.int32)
            adapter = jnp.full(slot.shape, ad_ref[index, 0], jnp.int32)
            for k in range(count):
                end = end + len_ref[index, k]
                past = slot >= end
                request = request + past.astype(jnp.int32)
                if wants and k + 1 < count:
                    start = jnp.where(past, end, start)
                    adapter = jnp.where(past, ad_ref[index, k + 1], adapter)
            return request, slot - start, adapter

        lane = lax.broadcasted_iota(jnp.int32, (1, HD), 1)
        frequency = jnp.exp((lane % half).astype(F32) * F32(-math.log(rope_base) * 2.0 / HD))
        for i in range(2):
            index = at_ref[0] * 2 + i
            down = lax.broadcasted_iota(jnp.int32, (slots, 1), 0)
            request, position, adapter = layout(index, down, True)
            column[i] = request
            line[i] = layout(index, lax.broadcasted_iota(jnp.int32, (1, slots), 1), False)[0]
            here = slice(i * slots, (i + 1) * slots)
            two[here] = adapter
            angles = position.astype(F32) * frequency
            cosine[here] = jnp.cos(angles)
            sine[here] = jnp.where(lane < half, -jnp.sin(angles), jnp.sin(angles))
        for s in range(2):
            first = (at_ref[1] * 2 + (at_ref[2] ^ s)) * piece
            slot = first + lax.broadcasted_iota(jnp.int32, (piece, 1), 0)
            for b in range(4):
                to = (s * 4 + b) * piece
                rows[to : to + piece] = layout(at_ref[3] ^ b, slot, True)[2]

    table = jax.ShapeDtypeStruct((2 * slots, HD), F32)
    return pl.pallas_call(
        kernel,
        in_specs=[SMEM_SPEC] * 3,
        out_specs=[VMEM_SPEC] * 6,
        out_shape=[
            jax.ShapeDtypeStruct((2, slots, 1), jnp.int32),
            jax.ShapeDtypeStruct((2, 1, slots), jnp.int32),
            jax.ShapeDtypeStruct((2 * slots, 1), jnp.int32),
            table,
            table,
            jax.ShapeDtypeStruct((8 * piece, 1), jnp.int32),
        ],
        compiler_params=PARAMS,
        cost_estimate=COST,
        name="tables",
    )(lengths, adapters, scalars)


def finish(hidden_state, terms, at):
    piece, columns = terms[0].shape
    spec = pl.BlockSpec((piece, columns), lambda i, a: (0, 0))

    def kernel(at_ref, hidden_ref, *refs):
        total = hidden_ref[...]
        for ref in refs[:-1]:
            total = total + ref[...].astype(F32)
        refs[-1][...] = total.astype(BF16)

    return pl.pallas_call(
        kernel,
        grid_spec=pltpu.PrefetchScalarGridSpec(
            num_scalar_prefetch=1,
            grid=(1,),
            in_specs=[pl.BlockSpec((piece, columns), lambda i, a: (0, a[0]))] + [spec] * len(terms),
            out_specs=spec,
        ),
        out_shape=jax.ShapeDtypeStruct((piece, columns), BF16),
        compiler_params=PARAMS,
        cost_estimate=COST,
        name="finish",
    )(at, hidden_state, *terms)


def project_qkv(own, pieces, adapter, a, b, cosine, sine, weights, places):
    slots, width = own.shape
    total_rows, columns, rank = 2 * slots, b.shape[1], b.shape[0]
    piece, size, tile = pieces[0].shape[0], width // len(weights), columns // 3
    n_pieces, n_weights = len(pieces), len(weights)
    chunk = total_rows // 2
    column = adapter

    def kernel(at_ref, adapter_ref, a_ref, cos_ref, sin_ref, own_ref, b_ref, *refs):
        p_in, w_in, rest = refs[:n_pieces], refs[n_pieces : n_pieces + n_weights], refs[-7:]
        out, x, w, bb, low, x_sem, w_sem = rest

        def weight_copies(step, slot):
            to = pl.ds(step * tile, tile)
            for i in range(n_weights):
                yield dma(
                    w_in[i].at[:, to],
                    w.at[slot, mm(at_ref[1 + n_pieces + i], size), :],
                    w_sem.at[slot, i],
                )
            yield dma(b_ref.at[:, to], bb.at[slot], w_sem.at[slot, n_weights])

        x_copies = [dma(own_ref, x.at[mm(at_ref[0], slots), :], x_sem.at[n_pieces])]
        for i in range(n_pieces):
            x_copies.append(dma(p_in[i], x.at[mm(at_ref[1 + i], piece), :], x_sem.at[i]))
        for copy in x_copies:
            copy.start()
        for copy in weight_copies(0, 0):
            copy.start()
        for copy in x_copies:
            copy.wait()
        for step in range(3):
            slot = step % 2
            if step < 2:
                for copy in weight_copies(step + 1, 1 - slot):
                    copy.start()
            for copy in weight_copies(step, slot):
                copy.wait()

            @pl.loop(0, total_rows // chunk)
            def _(m):
                at = mm(m, chunk)
                xs = x[at, :]
                if step == 0:
                    low[at, :] = masked(dot(xs, a_ref[...]), adapter_ref[at, :])
                total = dot(xs, w[slot]) + dot(low[at, :], bb[slot])
                for h in range(tile // HD):
                    v = total[:, h * HD : (h + 1) * HD]
                    if step < 2:
                        v = v * cos_ref[at, :] + pltpu.roll(v, HD // 2, 1) * sin_ref[at, :]
                    start = step * tile + h * HD
                    out[at, start : start + HD] = v.astype(BF16)

    return pl.pallas_call(
        kernel,
        in_specs=[SMEM_SPEC] + [VMEM_SPEC] * 4 + [HBM_SPEC] * (2 + n_pieces + n_weights),
        out_specs=VMEM_SPEC,
        out_shape=jax.ShapeDtypeStruct((total_rows, columns), BF16),
        scratch_shapes=[
            VM((total_rows, width), BF16),
            VM((2, width, tile), BF16),
            VM((2, rank, tile), BF16),
            VM((total_rows, rank), BF16),
            pltpu.SemaphoreType.DMA((n_pieces + 1,)),
            pltpu.SemaphoreType.DMA((2, n_weights + 1)),
        ],
        compiler_params=PARAMS,
        cost_estimate=COST,
        name="project_qkv",
    )(places, column, a, cosine, sine, own, b, *pieces, *weights)


def attend(qkv, column, line):
    indices, slots = column.shape[:2]
    heads = qkv.shape[1] // 3 // HD
    rows = 256 if slots % 256 == 0 else slots

    def kernel(q, k, v, column_ref, line_ref, out):
        for at in range(0, slots, rows):
            seen = at + rows
            s = lax.dot_general(
                q[at:seen], k[:seen], (((1,), (1,)), ((), ())), preferred_element_type=F32
            )
            s = s * (1.0 / math.sqrt(HD))
            here = at + lax.broadcasted_iota(jnp.int32, s.shape, 0)
            there = lax.broadcasted_iota(jnp.int32, s.shape, 1)
            allowed = (column_ref[0, at:seen] == line_ref[0, :, :seen]) & (here >= there)
            s = jnp.where(allowed, s, F32(-1e30))
            e = jnp.exp(s - jnp.max(s, axis=1, keepdims=True))
            weights = (e * (1.0 / jnp.sum(e, axis=1, keepdims=True))).astype(BF16)
            out[at:seen] = dot(weights, v[:seen]).astype(BF16)

    return pl.pallas_call(
        kernel,
        grid=(indices, heads),
        in_specs=[
            pl.BlockSpec((slots, HD), lambda i, h: (i, h)),
            pl.BlockSpec((slots, HD), lambda i, h: (i, heads + h)),
            pl.BlockSpec((slots, HD), lambda i, h: (i, 2 * heads + h)),
            pl.BlockSpec((1, slots, 1), lambda i, h: (i, 0, 0)),
            pl.BlockSpec((1, 1, slots), lambda i, h: (i, 0, 0)),
        ],
        out_specs=pl.BlockSpec((slots, HD), lambda i, h: (i, h)),
        out_shape=jax.ShapeDtypeStruct((indices * slots, heads * HD), BF16),
        compiler_params=PARAMS,
        cost_estimate=COST,
        name="attend",
    )(qkv, qkv, qkv, column, line)


def project_out(attn, adapter, a, b, weights, order, scalars, T, came=None):
    total_rows, depth = attn.shape
    n, slots, piece, Y = len(weights), total_rows // 2, total_rows // 2 // T, T // 2
    extra = list(came or [])
    flat = [p for w in weights for p in w]
    size = sum(p.shape[1] for p in flat) // n // 2
    half, columns = total_rows // 2, n * 2 * size
    per = n // max(1, len(extra))

    def kernel(order_ref, at_ref, attn_ref, adapter_ref, a_ref, b_ref, *refs):
        ws, outs, rows, low = refs[: len(flat)], refs[len(flat) + len(extra) : -2], *refs[-2:]
        x, y, c = at_ref[0], at_ref[1], at_ref[2]
        mine = a_ref[mm(x, depth), :]
        for i in range(2):
            for k in range(Y):
                here = mm((x ^ i) * T + lax.rem(y + Y - k, Y) * 2 + c, piece)
                to = (i * Y + k) * piece
                part = attn_ref[here, :]
                rows[to : to + piece] = part
                low[to : to + piece] = masked(dot(part, mine), adapter_ref[here, :])
        it = iter(ws)
        for k, w in enumerate(weights):
            blocks = []
            for p in w:
                ref = next(it)
                for start in range(0, p.shape[1], size):
                    blocks.append((ref, start))
            for i, (ref, start) in enumerate(blocks):
                there = mm(order_ref[2 * k + i], size)
                to = mm(k * 2 + (x ^ i), size)
                total = dot(rows[...], ref[:, start : start + size]) + dot(low[...], b_ref[:, there])
                if came is None:
                    outs[0][:, to] = total.astype(BF16)
                else:
                    from_core = refs[len(flat) + k // per][:, mm(k % per * 2 + (x ^ i), size)]
                    total = (total + from_core.astype(F32)).astype(BF16)
                    for p in range(2 * Y):
                        outs[p][:, to] = total[p * piece : (p + 1) * piece]

    shapes = [jax.ShapeDtypeStruct((half, columns), BF16)]
    if came is not None:
        shapes = [jax.ShapeDtypeStruct((piece, columns), BF16)] * (2 * Y)
    out = pl.pallas_call(
        kernel,
        in_specs=[SMEM_SPEC, SMEM_SPEC] + [VMEM_SPEC] * (4 + len(flat) + len(extra)),
        out_specs=[VMEM_SPEC] * len(shapes),
        out_shape=shapes,
        scratch_shapes=[VM((half, depth), BF16), VM((half, a.shape[1]), BF16)],
        compiler_params=PARAMS,
        cost_estimate=COST,
        name="project_out",
    )(order, scalars, attn, adapter, a, b, *flat, *extra)
    return out[0] if came is None else out


def residual_norm(tokens, row, order, chunks):
    width = tokens.shape[1]
    n = order.shape[0]
    piece, size, per = chunks[0][0].shape[0], width // n, n // len(chunks)
    flat = [term for chunk in chunks for term in chunk]

    def kernel(row_ref, order_ref, tok_ref, *refs):
        it, hidden, normed = iter(refs[:-2]), refs[-2], refs[-1]
        for c, chunk in enumerate(chunks):
            total = next(it)[...].astype(F32)
            for _ in chunk[1:]:
                total = total + next(it)[...].astype(F32)
            for place in range(per):
                to = mm(order_ref[c * per + place], size)
                more = total[:, place * size : (place + 1) * size]
                hidden[:, to] = tok_ref[:, to].astype(F32) + more
        normed[...] = layer_norm(hidden[...])

    return pl.pallas_call(
        kernel,
        grid_spec=pltpu.PrefetchScalarGridSpec(
            num_scalar_prefetch=2,
            grid=(1,),
            in_specs=[
                pl.BlockSpec((piece, width), lambda n, r, o: (r[0], 0)),
                *[pl.BlockSpec(p.shape, lambda n, r, o: (0, 0)) for p in flat],
            ],
            out_specs=[pl.BlockSpec((piece, width), lambda n, r, o: (0, 0))] * 2,
        ),
        out_shape=[
            jax.ShapeDtypeStruct((piece, width), F32),
            jax.ShapeDtypeStruct((piece, width), BF16),
        ],
        compiler_params=PARAMS,
        cost_estimate=COST,
        name="residual_norm",
    )(row, order, tokens, *flat)


def gated(rows, adapters, a_gate, a_up, sets, places, unit):
    width = rows[0].shape[1]
    total_rows = sum(row.shape[0] for row in rows)
    units = sets[0][1].shape[1] // 2
    tile = min(256, units)
    tiles = units // tile
    rank = a_gate.shape[1]
    column = adapters
    flat = [w for s in sets for w in s[0]]
    first = [sum(len(s[0]) for s in sets[:k]) for k in range(len(sets) + 1)]
    bs = [s[1] for s in sets]
    downs = [s[2] for s in sets]
    n_rows, n_sets = len(rows), len(sets)
    most = max(len(s[0]) for s in sets)
    steps = n_sets * tiles
    chunk = total_rows // 2
    hidden_width = n_sets * units

    def kernel(place_ref, adapter_ref, ag_ref, au_ref, *refs):
        it = iter(refs)
        take = lambda k: [next(it) for _ in range(k)]
        x_in, w_in, b_in, d_in = take(n_rows), take(len(flat)), take(n_sets), take(n_sets)
        hidden, x, w, bb, lg, lu, ld, x_sem, w_sem, b_sem = take(10)

        def weight_copies(step, slot):
            s, t = divmod(step, tiles)
            for g in range(2):
                for i in range(first[s], first[s + 1]):
                    yield dma(
                        w_in[i].at[:, pl.ds(g * units + t * tile, tile)],
                        w.at[slot, g, pl.ds(pl.multiple_of(place_ref[i] * unit, unit), flat[i].shape[0]), :],
                        w_sem.at[slot, g, i - first[s]],
                    )
                yield dma(
                    b_in[s].at[:, pl.ds(g * units + t * tile, tile)],
                    bb.at[slot, g],
                    b_sem.at[slot, g],
                )

        x_copies, start = [], 0
        for i in range(n_rows):
            x_copies.append(dma(x_in[i], x.at[pl.ds(start, rows[i].shape[0]), :], x_sem.at[i]))
            start += rows[i].shape[0]
        for copy in x_copies:
            copy.start()
        for copy in weight_copies(0, 0):
            copy.start()
        for copy in x_copies:
            copy.wait()
        for step in range(steps):
            slot = step % 2
            if step + 1 < steps:
                for copy in weight_copies(step + 1, 1 - slot):
                    copy.start()
            for copy in weight_copies(step, slot):
                copy.wait()
            s, t = divmod(step, tiles)

            for m in range(total_rows // chunk):
                at = slice(m * chunk, (m + 1) * chunk)
                xs = x[at, :]
                if step == 0:
                    lg[at, :] = masked(dot(xs, ag_ref[...]), adapter_ref[at, :])
                    lu[at, :] = masked(dot(xs, au_ref[...]), adapter_ref[at, :])
                gate = dot(xs, w[slot, 0]) + dot(lg[at, :], bb[slot, 0])
                up = dot(xs, w[slot, 1]) + dot(lu[at, :], bb[slot, 1])
                h = (0.5 * gate * (1.0 + jnp.tanh(0.5 * gate)) * up).astype(BF16)
                hidden[at, step * tile : (step + 1) * tile] = h
                more = dot(h, d_in[s][t * tile : (t + 1) * tile, :])
                if step > 0:
                    more = more + ld[at, :]
                if step < steps - 1:
                    ld[at, :] = more
                else:
                    hidden[at, hidden_width:] = masked(more, adapter_ref[at, :])

    return pl.pallas_call(
        kernel,
        in_specs=[SMEM_SPEC] + [VMEM_SPEC] * 3
        + [HBM_SPEC] * (n_rows + len(flat) + n_sets)
        + [VMEM_SPEC] * n_sets,
        out_specs=VMEM_SPEC,
        out_shape=jax.ShapeDtypeStruct((total_rows, hidden_width + rank), BF16),
        scratch_shapes=[
            VM((total_rows, width), BF16),
            VM((2, 2, width, tile), BF16),
            VM((2, 2, rank, tile), BF16),
            VM((total_rows, rank), BF16),
            VM((total_rows, rank), BF16),
            VM((total_rows, rank), F32),
            pltpu.SemaphoreType.DMA((n_rows,)),
            pltpu.SemaphoreType.DMA((2, 2, most)),
            pltpu.SemaphoreType.DMA((2, 2)),
        ],
        compiler_params=PARAMS,
        cost_estimate=COST,
        name="gated",
    )(places, column, a_gate, a_up, *rows, *flat, *bs, *downs)


def project_down(hidden, b, sets, units, at, which, came=None):
    half, depth = hidden.shape[0] // 2, hidden.shape[1]
    piece, rank = half // 4, b.shape[0]
    size = sets[0][0].shape[1]
    flat = [w for group in sets for w in group]
    n, n_sets, n_weights = 4, len(sets), len(flat)
    extra = [] if came is None else [came]

    def kernel(at_ref, h_in, *refs):
        refs = list(refs)
        came_ref = refs.pop(0) if extra else None
        b_ref, w_in, outs = refs[0], refs[1 : 1 + n_weights], refs[1 + n_weights : -4]
        w, h_ref, sems, h_sems = refs[-4:]
        copies = [
            dma(
                b_ref.at[:, mm(at_ref[0], n * size)],
                w.at[n_sets * units : n_sets * units + rank, :],
                sems.at[n_sets * n],
            )
        ]
        h_copies = [
            dma(
                h_in.at[pl.ds(which * half + m * 2 * piece, 2 * piece), :],
                h_ref.at[pl.ds(m * 2 * piece, 2 * piece), :],
                h_sems.at[m],
            )
            for m in range(2)
        ]
        it = iter(w_in)
        for k, group in enumerate(sets):
            place = 0
            for array in group:
                ref = next(it)
                for i in range(array.shape[0] // units):
                    copies.append(
                        dma(
                            ref.at[pl.ds(i * units, units), :],
                            w.at[k * units : (k + 1) * units, place * size : (place + 1) * size],
                            sems.at[k * n + place],
                        )
                    )
                    place += 1
        for copy in copies + h_copies:
            copy.start()
        for copy in copies:
            copy.wait()
        for m in range(2):
            h_copies[m].wait()
            here = slice(m * 2 * piece, (m + 1) * 2 * piece)
            total = dot(h_ref[here, :], w[...])
            if came is None:
                outs[0][here, :] = total.astype(BF16)
            else:
                total = (total + came_ref[here, :].astype(F32)).astype(BF16)
                outs[2 * m][...], outs[2 * m + 1][...] = total[:piece], total[piece:]

    shapes = [jax.ShapeDtypeStruct((half, n * size), BF16)]
    if came is not None:
        shapes = [jax.ShapeDtypeStruct((piece, n * size), BF16)] * 4
    out = pl.pallas_call(
        kernel,
        in_specs=[SMEM_SPEC, HBM_SPEC]
        + [VMEM_SPEC] * len(extra)
        + [HBM_SPEC] * (1 + n_weights),
        out_specs=[VMEM_SPEC] * len(shapes),
        out_shape=shapes,
        scratch_shapes=[
            VM((depth, n * size), BF16),
            VM((half, depth), BF16),
            pltpu.SemaphoreType.DMA((n_sets * n + 1,)),
            pltpu.SemaphoreType.DMA((2,)),
        ],
        compiler_params=PARAMS,
        cost_estimate=COST,
        name="project_down",
    )(at, hidden, *extra, b, *flat)
    return out[0] if came is None else out


def assemble(pieces, places, shape):
    rows, columns = pieces[0].shape

    def kernel(places_ref, *refs):
        out = refs[-1]
        for i in range(len(pieces)):
            to = mm(places_ref[2 * i], rows), mm(places_ref[2 * i + 1], columns)
            out[to] = refs[i][...]

    return pl.pallas_call(
        kernel,
        in_specs=[SMEM_SPEC] + [VMEM_SPEC] * len(pieces),
        out_specs=VMEM_SPEC,
        out_shape=jax.ShapeDtypeStruct(shape, BF16),
        compiler_params=PARAMS,
        cost_estimate=COST,
        name="assemble",
    )(places, *pieces)


@jax.tree_util.register_pytree_node_class
class Live:
    def __init__(self, **arrays):
        self.__dict__.update(arrays)

    def tree_flatten(self):
        names = tuple(sorted(self.__dict__))
        return [self.__dict__[name] for name in names], names

    @classmethod
    def tree_unflatten(cls, names, arrays):
        return cls(**dict(zip(names, arrays)))

    @property
    def pop(self):
        return Pop(self)

    @property
    def drop(self):
        return Drop(self)


class Pop:
    def __init__(self, live):
        self.__dict__.update(live=live)

    def __getattr__(self, name):
        return self.live.__dict__.pop(name)


class Drop(Pop):
    def __getattr__(self, name):
        self.live.__dict__.pop(name)
        return self


def make_body(R, T):
    Z, ZH, Y = R // 2, R // 4, T // 2

    def flat(z, x, y, c):
        return (z * 2 + x) * T + y * 2 + c

    def move(f):
        every = [(r // 2, r % 2, t // 2, t % 2) for r in range(R) for t in range(T)]
        return [(flat(*d), flat(*f(*d))) for d in every]

    def send(value, pairs):
        return lax.ppermute(value, AXES, pairs)

    to_core = move(lambda z, x, y, c: (z, x, y, 1 - c))
    to_x = move(lambda z, x, y, c: (z, 1 - x, y, c))
    z_up = move(lambda z, x, y, c: ((z + 1) % Z, x, y, c))
    z_down = move(lambda z, x, y, c: ((z - 1) % Z, x, y, c))
    from_y = {k: move(lambda z, x, y, c, k=k: (z, x, (y - k) % Y, c)) for k in range(1, Y)}
    same_xzl = [[zh * 4 + b for b in range(4)] for zh in range(ZH)]
    same_zh = [[zh * 4 + b for zh in range(ZH)] for b in range(4)]
    to_xy = {
        (i, k): move(lambda z, x, y, c, i=i, k=k: (z, x ^ i, (y - k) % Y, c))
        for i in (0, 1)
        for k in range(Y)
    }
    to_xzl = {
        (i, j): move(lambda z, x, y, c, i=i, j=j: (z ^ j, x ^ i, y, c))
        for j in (0, 1)
        for i in (0, 1)
    }

    from_zh = {
        k: move(lambda z, x, y, c, k=k: ((z - 2 * k) % Z, x, y, c)) for k in range(1, ZH)
    }
    to_zl = move(lambda z, x, y, c: (z ^ 1, x, y, c))

    def spread(value, axes, groups):
        return lax.all_to_all(value, axes, 0, 0, axis_index_groups=groups, tiled=True)

    def fence(live):
        return lax.optimization_barrier(live)

    def body(
        tokens, lengths, request_adapter, w_qkv, w_out, w_gate, w_up, w_down,
        a_qkv, b_qkv, a_out, b_out, a_gate, b_gate, a_up, b_up, a_down, b_down,
    ):
        r, t = lax.axis_index("req"), lax.axis_index("tp")
        z, x, y, c = r // 2, r % 2, t // 2, t % 2
        zh, zl = z // 2, z % 2
        slots, width = tokens.shape
        piece = slots // T
        block = width // R
        local = w_qkv.shape[2] // 2
        rank = a_qkv.shape[1]
        quarter = w_gate.shape[1] // 4
        span = width // ZH
        count = lengths.shape[1]
        far_y, far_zh, opposite = range(1, Y), range(1, ZH), Z // 2

        def cut(array, start, size, axis):
            return lax.dynamic_slice_in_dim(array, start, size, axis)

        def ints(values):
            return jnp.stack([jnp.asarray(v, jnp.int32) for v in values])

        L = Live(
            tokens=tokens, both=jnp.concatenate([lengths, request_adapter], axis=1), w_gate=w_gate,
            w_up=w_up, w_down=w_down, a_qkv=a_qkv, a_out=a_out, b_out=b_out, a_gate=a_gate,
            a_up=a_up, b_down=b_down, b_qkv=b_qkv, b_gate=b_gate, b_up=b_up, a_down=a_down,
        )
        keys = [(k, i) for k in range(Z) for i in (0, 1)]
        order = [((z + k) % Z) * 2 + (x ^ i) for k, i in keys]
        there = [(zh + h) % ZH for h in range(ZH)]
        at = [(1 - x) * T + ((y + k) % Y) * 2 + s for s in (c, 1 - c) for k in range(Y)]
        far_places = []
        for h in there[1:]:
            first, other = (h * 2 + zl) * 4, (h * 2 + 1 - zl) * 4
            far_places += [first, first + 2, other, other + 1]
        places = ([(zh * 2 + zl) * 4, (zh * 2 + 1 - zl) * 4] + far_places) * Y
        L.ints = Live(
            t=ints([t]), order=[ints(order[:Z]), ints(order[Z:]), ints(order)], qkv=ints([x, *at, *order]),
            xyc=[ints([x, y, c]), ints([x, y, 1 - c])],
            zyc=ints([zl, y, c, zl * 2 + x]), z=ints([(z + k) % Z for k in range(Z)]),
            gated=ints(places), span=[ints([h]) for h in there], b=ints([zl * 2 + x]),
        )
        mine = (zl * 2 + x) * quarter

        def heads_of(w, which):
            return cut(w, which * local, local, 2).reshape(w.shape[0], 3 * local)


        def ring_start(own):
            left = right = own
            got = {0: own}
            for k in range(1, opposite):
                left, right = send(left, z_up), send(right, z_down)
                got[Z - k], got[k] = left, right
            return got

        L.first = send(heads_of(w_qkv, 1 - x), to_x)
        L.ring = [ring_start(heads_of(w_qkv, x))]
        L.out = send(cut(w_out, (1 - x) * local, local, 0), to_x)
        L.both = spread(jnp.concatenate([L.both] * 4, axis=0), "req", same_xzl)
        L.normed, L.mine = norm_rows(L.tokens, L.ints.t, T)
        L.b = jnp.concatenate(
            [cut(L.pop.b_gate, mine, quarter, 1), cut(L.pop.b_up, mine, quarter, 1)], axis=1
        )
        L.a_down = cut(L.a_down, mine, quarter, 0)
        L.b_heads = cut(L.pop.b_qkv, x * local, local, 2).reshape(rank, 3 * local)
        L.own_out = cut(w_out, x * local, local, 0)
        L = fence(L)

        L.ring.append(ring_start(L.pop.first))
        L.quarter = send(L.pop.mine, to_x)
        L.b_far = [send(L.b, from_y[k]) for k in far_y]
        L.a_far = [send(L.a_down, from_y[k]) for k in far_y]
        L.gu, L.gu_give = pack(L.pop.w_gate, L.pop.w_up, L.ints.b)
        L.out = jnp.concatenate([L.pop.own_out, L.out], axis=1)
        L = fence(L)

        L.ring[0][opposite] = send(L.ring[0][opposite + 1], z_up)
        L.ring[1][opposite] = send(L.ring[1][opposite - 1], z_down)
        L.quarters = [L.quarter] + [send(L.quarter, from_y[k]) for k in far_y]
        L.out = ring_start(L.out)
        L.gu_came = send(L.pop.gu_give, to_x)
        both = L.pop.both
        L.tables = tables(both[:, :count], both[:, count:], L.ints.zyc, slots, T)
        L = fence(L)
        L.quarters = L.quarters + [send(q, to_core) for q in L.quarters]
        L.for_out = [L.out[opposite + 1][:, :block], L.out[opposite - 1][:, block:]]
        L.near, L.give = join(L.pop.gu, L.pop.gu_came, L.ints.xyc[0])
        L = fence(L)

        one, two = L.pop.for_out
        L.far_out = [send(one, z_up), send(two, z_down)]
        L.far = send(L.pop.give, to_zl)
        L.y = [[send(L.near, from_y[k]) for k in far_y]]
        column, line, adapter, cosine, sine, adapters = L.tables
        L.joined = project_qkv(
            L.pop.normed, L.pop.quarters, adapter, L.pop.a_qkv, L.pop.b_heads, cosine,
            sine, [L.ring[i][k] for k, i in keys], L.ints.qkv,
        )
        L.pop.ring
        L = fence(L)

        def over_zh(w):
            return [send(w, from_zh[h]) for h in far_zh]

        def relay(arrays):
            return [[send(w, from_y[k]) for w in arrays] for k in far_y]

        def out_of(chunk, core, came=None):
            return project_out(
                attn, adapter, L.a_out, L.b_out, blocks[chunk], L.ints.order[chunk],
                L.ints.xyc[core], T, came,
            )

        rows = L.near.shape[0] // 2
        L.near_parts = [L.near[:rows], L.near[rows:]]
        L.y.append([send(L.far, from_y[k]) for k in far_y])
        L.zh0 = over_zh(L.near_parts[0])
        column, line, adapter, cosine, sine, adapters = L.pop.tables
        attn = attend(L.pop.joined, column, line)
        blocks = [(L.out[k],) if k != opposite else tuple(L.far_out) for k in range(Z)]
        blocks = [blocks[:opposite], blocks[opposite:], blocks]
        L.gives = [out_of(chunk, 1) for chunk in (0, 1)]
        L.attn, L.adapter, L.adapters, L.blocks = attn, adapter, adapters, blocks
        L.drop.out.far_out.quarter
        L = fence(L)
        L.down = spread(L.pop.w_down, "req", same_xzl)
        part = rows_unit = rows // 2
        L.far_parts = [L.far[:part], L.far[part:]]
        L.zh2 = over_zh(L.far_parts[0])
        L.relay0 = relay(L.zh0)
        attn, adapter, blocks = L.pop.attn, L.pop.adapter, L.pop.blocks
        L.parts = out_of(2, 0, [send(give, to_core) for give in L.pop.gives])
        L.drop.a_out.b_out
        L = fence(L)

        parts = L.pop.parts
        terms = [parts[0]]
        for i in (0, 1):
            for k in range(Y):
                if i or k:
                    terms.append(send(parts[i * Y + k], to_xy[(i, k)]))
        L.zh3 = over_zh(L.far_parts[1])
        L.terms = terms
        L = fence(L)
        L.hidden_state, L.normed2 = residual_norm(
            L.pop.tokens, L.ints.t, L.ints.z, [L.pop.terms]
        )
        split = L.down.shape[0] // 2
        L.for_down = [L.down[:split], L.down[split:]]
        L = fence(L)

        own = L.pop.normed2
        L.rows = [own, send(own, to_x), send(own, to_zl)]
        L.relay3 = relay(L.zh3)
        L.zh1 = over_zh(L.near_parts[1])
        L.down_y = [[send(L.for_down[0], from_y[k]) for k in far_y]]
        L.cut = [L.rows[1][: piece // 2], L.rows[2][piece // 2 :]]
        L = fence(L)
        one, two = L.pop.cut
        L.rows += [send(one, to_zl), send(two, to_x)]
        L.relay1, L.relay2 = relay(L.zh1), relay(L.zh2)
        L.down_zh = [over_zh(L.for_down[0])]
        L = fence(L)
        L.rows += [send(row, to_core) for row in L.rows]
        L = fence(L)

        L.down_zh.append(over_zh(L.for_down[1]))
        L.down_y.append([send(L.for_down[1], from_y[k]) for k in far_y])
        L.down_zh_y = [relay(L.down_zh[0])]
        zh_blocks = [part[h] for h in range(ZH - 1) for part in (L.zh0, L.zh1, L.zh2, L.zh3)]
        sets = [([L.near, L.far, *zh_blocks], L.b, L.a_down)]
        for k in range(Y - 1):
            relayed = [part[k][h] for h in range(ZH - 1) for part in (L.relay0, L.relay1, L.relay2, L.relay3)]
            sets.append(([L.y[0][k], L.y[1][k], *relayed], L.b_far[k], L.a_far[k]))
        L.hidden = gated(
            L.rows, L.adapters, L.pop.a_gate, L.pop.a_up, sets, L.ints.gated,
            rows_unit,
        )
        L.drop.near.far.near_parts.far_parts.zh0.zh1.zh2.zh3.relay0.relay1.relay2.relay3
        L.drop.b.a_down.y.b_far.a_far.rows
        L = fence(L)

        L.down_zh_y.append(relay(L.down_zh[1]))
        down_sets = [[[L.down]] + [[part[k] for part in L.down_y] for k in range(Y - 1)]]
        for h in range(ZH - 1):
            far = [[part[k][h] for part in L.down_zh_y] for k in range(Y - 1)]
            down_sets.append([[part[h] for part in L.down_zh]] + far)

        def down_of(h, which, came=None):
            return project_down(
                L.hidden, L.b_down, down_sets[h], quarter, L.ints.span[h], which, came
            )

        came = [send(down_of(h, 1), to_core) for h in range(ZH)]
        pieces, places = [], []
        for h in range(ZH):
            parts = down_of(h, 0, came[h])
            terms = [parts[0]]
            terms += [send(parts[j * 2 + i], to_xzl[(i, j)]) for j in (0, 1) for i in (0, 1) if i or j]
            done = finish(L.hidden_state, terms, L.ints.span[h])
            for k in range(Y):
                there_y = done if k == 0 else send(done, from_y[k])
                for s, got in ((0, there_y), (1, send(there_y, to_core))):
                    pieces.append(got)
                    places += [((y + k) % Y) * 2 + (c ^ s), there[h]]
        return assemble(pieces, ints(places), tokens.shape)

    return body


def solution(mesh):
    in_specs = (
        P("req", None),
        P("req", None),
        P("req", None),
        P("req", None, "tp"),
        P("tp", "req"),
        P("req", "tp"),
        P("req", "tp"),
        P("tp", "req"),
        P(),
        P(None, None, "tp"),
        P("tp", None),
        P(),
        P(),
        P(None, "tp"),
        P(),
        P(None, "tp"),
        P("tp", None),
        P(),
    )
    return jax.shard_map(
        make_body(mesh.shape["req"], mesh.shape["tp"]),
        mesh=mesh, in_specs=in_specs, out_specs=P("req", None), check_vma=False,
    )
```

```python
import math

import jax
import jax.numpy as jnp
from jax import lax
from jax.experimental import pallas as pl
from jax.experimental.pallas import tpu as pltpu
from jax.sharding import PartitionSpec as P

HD = 128
RANK = 16
AXES = ("req", "tp")
epsilon = 1e-05
rope_base = 10000.0
F32 = jnp.float32
BF16 = jnp.bfloat16
VM = pltpu.VMEM
PARAMS = pltpu.CompilerParams(vmem_limit_bytes=56 * 2**20)
COST = pl.CostEstimate(flops=1000, bytes_accessed=1000, transcendentals=0)


def dot(a, b):
    return jnp.dot(a, b, preferred_element_type=F32)


def layer_norm(values):
    row_mean = jnp.mean(values, axis=-1, keepdims=True)
    centred = values - row_mean
    spread = jnp.mean(centred * centred, axis=-1, keepdims=True)
    return (centred * lax.rsqrt(spread + epsilon)).astype(BF16)


def masked(inner, adapter_column):
    rank = lax.broadcasted_iota(jnp.int32, inner.shape, 1) // RANK
    return jnp.where(adapter_column == rank, inner, F32(0.0)).astype(BF16)


def whole(array):
    return pl.BlockSpec(array.shape, lambda *_: (0,) * array.ndim, pipeline_mode=pl.Buffered(1))


def mm(start, size):
    return pl.ds(pl.multiple_of(start * size, size), size)


def dma(source, target, semaphore):
    return pltpu.make_async_copy(source, target, semaphore)


SMEM_SPEC = pl.BlockSpec(memory_space=pltpu.SMEM)
VMEM_SPEC = pl.BlockSpec(memory_space=VM)
HBM_SPEC = pl.BlockSpec(memory_space=pl.ANY)


def norm_rows(tokens, row, T):
    slots, width = tokens.shape
    piece = slots // T

    def kernel(row_ref, tok_ref, out, part):
        i = pl.program_id(0)
        normed = layer_norm(tok_ref[...].astype(F32))
        out[...] = normed

        @pl.when(i == row_ref[0])
        def _():
            part[...] = normed

    return pl.pallas_call(
        kernel,
        grid_spec=pltpu.PrefetchScalarGridSpec(
            num_scalar_prefetch=1,
            grid=(T,),
            in_specs=[pl.BlockSpec((piece, width), lambda i, r: (i, 0))],
            out_specs=[
                pl.BlockSpec((piece, width), lambda i, r: (i, 0)),
                pl.BlockSpec((piece, width), lambda i, r: (0, 0)),
            ],
        ),
        out_shape=[
            jax.ShapeDtypeStruct((slots, width), BF16),
            jax.ShapeDtypeStruct((piece, width), BF16),
        ],
        compiler_params=PARAMS,
        cost_estimate=COST,
        name="norm_rows",
    )(row, tokens)


def pack(gate, up, b):
    rows, columns = gate.shape
    quarter = columns // 4

    def spec(which):
        return pl.BlockSpec((rows, quarter), lambda i, o: (0, o[0] ^ (i * 2 + which)))

    def kernel(b_ref, g0, u0, g1, u1, keep, give):
        keep[0, :, :quarter], keep[0, :, quarter:] = g0[...], u0[...]
        give[0, :, :quarter], give[0, :, quarter:] = g1[...], u1[...]

    out = pl.BlockSpec((1, rows, 2 * quarter), lambda i, o: (i, 0, 0))
    return pl.pallas_call(
        kernel,
        grid_spec=pltpu.PrefetchScalarGridSpec(
            num_scalar_prefetch=1,
            grid=(2,),
            in_specs=[spec(0), spec(0), spec(1), spec(1)],
            out_specs=[out, out],
        ),
        out_shape=[jax.ShapeDtypeStruct((2, rows, 2 * quarter), BF16)] * 2,
        compiler_params=PARAMS,
        cost_estimate=COST,
        name="pack",
    )(b, gate, up, gate, up)


def join(own, came, x):
    rows, columns = own.shape[1:]
    spec = pl.BlockSpec((1, rows, columns), lambda i: (i, 0, 0))
    shape = jax.ShapeDtypeStruct((2 * rows, columns), BF16)

    def kernel(x_ref, own_ref, came_ref, near, give):
        @pl.when(pl.program_id(0) == 0)
        def _():
            near[mm(x_ref[0], rows), :] = own_ref[0]
            near[mm(1 - x_ref[0], rows), :] = came_ref[0]

        @pl.when(pl.program_id(0) == 1)
        def _():
            give[mm(x_ref[0], rows), :] = own_ref[0]
            give[mm(1 - x_ref[0], rows), :] = came_ref[0]

    return pl.pallas_call(
        kernel,
        grid=(2,),
        in_specs=[SMEM_SPEC, spec, spec],
        out_specs=[pl.BlockSpec((2 * rows, columns), lambda i: (0, 0))] * 2,
        out_shape=[shape, shape],
        compiler_params=PARAMS,
        cost_estimate=COST,
        name="join",
    )(x, own, came)


def tables(lengths, adapters, scalars, slots, T):
    count = lengths.shape[1]
    piece = slots // T
    half = HD // 2

    def kernel(len_ref, ad_ref, at_ref, column, line, two, cosine, sine, rows):
        def layout(index, slot, wants):
            end = jnp.int32(0)
            request, start = jnp.zeros(slot.shape, jnp.int32), jnp.zeros(slot.shape, jnp.int32)
            adapter = jnp.full(slot.shape, ad_ref[index, 0], jnp.int32)
            for k in range(count):
                end = end + len_ref[index, k]
                past = slot >= end
                request = request + past.astype(jnp.int32)
                if wants and k + 1 < count:
                    start = jnp.where(past, end, start)
                    adapter = jnp.where(past, ad_ref[index, k + 1], adapter)
            return request, slot - start, adapter

        lane = lax.broadcasted_iota(jnp.int32, (1, HD), 1)
        frequency = jnp.exp((lane % half).astype(F32) * F32(-math.log(rope_base) * 2.0 / HD))
        for i in range(2):
            index = at_ref[0] * 2 + i
            down = lax.broadcasted_iota(jnp.int32, (slots, 1), 0)
            request, position, adapter = layout(index, down, True)
            column[i] = request
            line[i] = layout(index, lax.broadcasted_iota(jnp.int32, (1, slots), 1), False)[0]
            here = slice(i * slots, (i + 1) * slots)
            two[here] = adapter
            angles = position.astype(F32) * frequency
            cosine[here] = jnp.cos(angles)
            sine[here] = jnp.where(lane < half, -jnp.sin(angles), jnp.sin(angles))
        for s in range(2):
            first = (at_ref[1] * 2 + (at_ref[2] ^ s)) * piece
            slot = first + lax.broadcasted_iota(jnp.int32, (piece, 1), 0)
            for b in range(4):
                to = (s * 4 + b) * piece
                rows[to : to + piece] = layout(at_ref[3] ^ b, slot, True)[2]

    table = jax.ShapeDtypeStruct((2 * slots, HD), F32)
    return pl.pallas_call(
        kernel,
        in_specs=[SMEM_SPEC] * 3,
        out_specs=[VMEM_SPEC] * 6,
        out_shape=[
            jax.ShapeDtypeStruct((2, slots, 1), jnp.int32),
            jax.ShapeDtypeStruct((2, 1, slots), jnp.int32),
            jax.ShapeDtypeStruct((2 * slots, 1), jnp.int32),
            table,
            table,
            jax.ShapeDtypeStruct((8 * piece, 1), jnp.int32),
        ],
        compiler_params=PARAMS,
        cost_estimate=COST,
        name="tables",
    )(lengths, adapters, scalars)


def finish(hidden_state, terms, at):
    piece, columns = terms[0].shape
    spec = pl.BlockSpec((piece, columns), lambda i, a: (0, 0))

    def kernel(at_ref, hidden_ref, *refs):
        total = hidden_ref[...]
        for ref in refs[:-1]:
            total = total + ref[...].astype(F32)
        refs[-1][...] = total.astype(BF16)

    return pl.pallas_call(
        kernel,
        grid_spec=pltpu.PrefetchScalarGridSpec(
            num_scalar_prefetch=1,
            grid=(1,),
            in_specs=[pl.BlockSpec((piece, columns), lambda i, a: (0, a[0]))] + [spec] * len(terms),
            out_specs=spec,
        ),
        out_shape=jax.ShapeDtypeStruct((piece, columns), BF16),
        compiler_params=PARAMS,
        cost_estimate=COST,
        name="finish",
    )(at, hidden_state, *terms)


def project_qkv(own, pieces, adapter, a, b, cosine, sine, weights, places):
    slots, width = own.shape
    total_rows, columns, rank = 2 * slots, b.shape[1], b.shape[0]
    piece, size, tile = pieces[0].shape[0], width // len(weights), columns // 3
    n_pieces, n_weights = len(pieces), len(weights)
    chunk = total_rows // 2
    column = adapter

    def kernel(at_ref, adapter_ref, a_ref, cos_ref, sin_ref, own_ref, b_ref, *refs):
        p_in, w_in, rest = refs[:n_pieces], refs[n_pieces : n_pieces + n_weights], refs[-7:]
        out, x, w, bb, low, x_sem, w_sem = rest

        def weight_copies(step, slot):
            to = pl.ds(step * tile, tile)
            for i in range(n_weights):
                yield dma(
                    w_in[i].at[:, to],
                    w.at[slot, mm(at_ref[1 + n_pieces + i], size), :],
                    w_sem.at[slot, i],
                )
            yield dma(b_ref.at[:, to], bb.at[slot], w_sem.at[slot, n_weights])

        x_copies = [dma(own_ref, x.at[mm(at_ref[0], slots), :], x_sem.at[n_pieces])]
        for i in range(n_pieces):
            x_copies.append(dma(p_in[i], x.at[mm(at_ref[1 + i], piece), :], x_sem.at[i]))
        for copy in x_copies:
            copy.start()
        for copy in weight_copies(0, 0):
            copy.start()
        for copy in x_copies:
            copy.wait()
        for step in range(3):
            slot = step % 2
            if step < 2:
                for copy in weight_copies(step + 1, 1 - slot):
                    copy.start()
            for copy in weight_copies(step, slot):
                copy.wait()

            @pl.loop(0, total_rows // chunk)
            def _(m):
                at = mm(m, chunk)
                xs = x[at, :]
                if step == 0:
                    low[at, :] = masked(dot(xs, a_ref[...]), adapter_ref[at, :])
                total = dot(xs, w[slot]) + dot(low[at, :], bb[slot])
                for h in range(tile // HD):
                    v = total[:, h * HD : (h + 1) * HD]
                    if step < 2:
                        v = v * cos_ref[at, :] + pltpu.roll(v, HD // 2, 1) * sin_ref[at, :]
                    start = step * tile + h * HD
                    out[at, start : start + HD] = v.astype(BF16)

    return pl.pallas_call(
        kernel,
        in_specs=[SMEM_SPEC] + [VMEM_SPEC] * 4 + [HBM_SPEC] * (2 + n_pieces + n_weights),
        out_specs=VMEM_SPEC,
        out_shape=jax.ShapeDtypeStruct((total_rows, columns), BF16),
        scratch_shapes=[
            VM((total_rows, width), BF16),
            VM((2, width, tile), BF16),
            VM((2, rank, tile), BF16),
            VM((total_rows, rank), BF16),
            pltpu.SemaphoreType.DMA((n_pieces + 1,)),
            pltpu.SemaphoreType.DMA((2, n_weights + 1)),
        ],
        compiler_params=PARAMS,
        cost_estimate=COST,
        name="project_qkv",
    )(places, column, a, cosine, sine, own, b, *pieces, *weights)


def attend(qkv, column, line):
    indices, slots = column.shape[:2]
    heads = qkv.shape[1] // 3 // HD
    rows = 256 if slots % 256 == 0 else slots

    def kernel(q, k, v, column_ref, line_ref, out):
        for at in range(0, slots, rows):
            seen = at + rows
            s = lax.dot_general(
                q[at:seen], k[:seen], (((1,), (1,)), ((), ())), preferred_element_type=F32
            )
            s = s * (1.0 / math.sqrt(HD))
            here = at + lax.broadcasted_iota(jnp.int32, s.shape, 0)
            there = lax.broadcasted_iota(jnp.int32, s.shape, 1)
            allowed = (column_ref[0, at:seen] == line_ref[0, :, :seen]) & (here >= there)
            s = jnp.where(allowed, s, F32(-1e30))
            e = jnp.exp(s - jnp.max(s, axis=1, keepdims=True))
            weights = (e * (1.0 / jnp.sum(e, axis=1, keepdims=True))).astype(BF16)
            out[at:seen] = dot(weights, v[:seen]).astype(BF16)

    return pl.pallas_call(
        kernel,
        grid=(indices, heads),
        in_specs=[
            pl.BlockSpec((slots, HD), lambda i, h: (i, h)),
            pl.BlockSpec((slots, HD), lambda i, h: (i, heads + h)),
            pl.BlockSpec((slots, HD), lambda i, h: (i, 2 * heads + h)),
            pl.BlockSpec((1, slots, 1), lambda i, h: (i, 0, 0)),
            pl.BlockSpec((1, 1, slots), lambda i, h: (i, 0, 0)),
        ],
        out_specs=pl.BlockSpec((slots, HD), lambda i, h: (i, h)),
        out_shape=jax.ShapeDtypeStruct((indices * slots, heads * HD), BF16),
        compiler_params=PARAMS,
        cost_estimate=COST,
        name="attend",
    )(qkv, qkv, qkv, column, line)


def project_out(attn, adapter, a, b, weights, order, scalars, T, came=None):
    total_rows, depth = attn.shape
    n, slots, piece, Y = len(weights), total_rows // 2, total_rows // 2 // T, T // 2
    extra = list(came or [])
    flat = [p for w in weights for p in w]
    size = sum(p.shape[1] for p in flat) // n // 2
    half, columns = total_rows // 2, n * 2 * size
    per = n // max(1, len(extra))

    def kernel(order_ref, at_ref, attn_ref, adapter_ref, a_ref, b_ref, *refs):
        ws, outs, rows, low = refs[: len(flat)], refs[len(flat) + len(extra) : -2], *refs[-2:]
        x, y, c = at_ref[0], at_ref[1], at_ref[2]
        mine = a_ref[mm(x, depth), :]
        for i in range(2):
            for k in range(Y):
                here = mm((x ^ i) * T + lax.rem(y + Y - k, Y) * 2 + c, piece)
                to = (i * Y + k) * piece
                part = attn_ref[here, :]
                rows[to : to + piece] = part
                low[to : to + piece] = masked(dot(part, mine), adapter_ref[here, :])
        it = iter(ws)
        for k, w in enumerate(weights):
            blocks = []
            for p in w:
                ref = next(it)
                for start in range(0, p.shape[1], size):
                    blocks.append((ref, start))
            for i, (ref, start) in enumerate(blocks):
                there = mm(order_ref[2 * k + i], size)
                to = mm(k * 2 + (x ^ i), size)
                total = dot(rows[...], ref[:, start : start + size]) + dot(low[...], b_ref[:, there])
                if came is None:
                    outs[0][:, to] = total.astype(BF16)
                else:
                    from_core = refs[len(flat) + k // per][:, mm(k % per * 2 + (x ^ i), size)]
                    total = (total + from_core.astype(F32)).astype(BF16)
                    for p in range(2 * Y):
                        outs[p][:, to] = total[p * piece : (p + 1) * piece]

    shapes = [jax.ShapeDtypeStruct((half, columns), BF16)]
    if came is not None:
        shapes = [jax.ShapeDtypeStruct((piece, columns), BF16)] * (2 * Y)
    out = pl.pallas_call(
        kernel,
        in_specs=[SMEM_SPEC, SMEM_SPEC] + [VMEM_SPEC] * (4 + len(flat) + len(extra)),
        out_specs=[VMEM_SPEC] * len(shapes),
        out_shape=shapes,
        scratch_shapes=[VM((half, depth), BF16), VM((half, a.shape[1]), BF16)],
        compiler_params=PARAMS,
        cost_estimate=COST,
        name="project_out",
    )(order, scalars, attn, adapter, a, b, *flat, *extra)
    return out[0] if came is None else out


def residual_norm(tokens, row, order, chunks):
    width = tokens.shape[1]
    n = order.shape[0]
    piece, size, per = chunks[0][0].shape[0], width // n, n // len(chunks)
    flat = [term for chunk in chunks for term in chunk]

    def kernel(row_ref, order_ref, tok_ref, *refs):
        it, hidden, normed = iter(refs[:-2]), refs[-2], refs[-1]
        for c, chunk in enumerate(chunks):
            total = next(it)[...].astype(F32)
            for _ in chunk[1:]:
                total = total + next(it)[...].astype(F32)
            for place in range(per):
                to = mm(order_ref[c * per + place], size)
                more = total[:, place * size : (place + 1) * size]
                hidden[:, to] = tok_ref[:, to].astype(F32) + more
        normed[...] = layer_norm(hidden[...])

    return pl.pallas_call(
        kernel,
        grid_spec=pltpu.PrefetchScalarGridSpec(
            num_scalar_prefetch=2,
            grid=(1,),
            in_specs=[
                pl.BlockSpec((piece, width), lambda n, r, o: (r[0], 0)),
                *[pl.BlockSpec(p.shape, lambda n, r, o: (0, 0)) for p in flat],
            ],
            out_specs=[pl.BlockSpec((piece, width), lambda n, r, o: (0, 0))] * 2,
        ),
        out_shape=[
            jax.ShapeDtypeStruct((piece, width), F32),
            jax.ShapeDtypeStruct((piece, width), BF16),
        ],
        compiler_params=PARAMS,
        cost_estimate=COST,
        name="residual_norm",
    )(row, order, tokens, *flat)


def gated(rows, adapters, a_gate, a_up, sets, places, unit):
    width = rows[0].shape[1]
    total_rows = sum(row.shape[0] for row in rows)
    units = sets[0][1].shape[1] // 2
    tile = min(256, units)
    tiles = units // tile
    rank = a_gate.shape[1]
    column = adapters
    flat = [w for s in sets for w in s[0]]
    first = [sum(len(s[0]) for s in sets[:k]) for k in range(len(sets) + 1)]
    bs = [s[1] for s in sets]
    downs = [s[2] for s in sets]
    n_rows, n_sets = len(rows), len(sets)
    most = max(len(s[0]) for s in sets)
    steps = n_sets * tiles
    chunk = total_rows // 2
    hidden_width = n_sets * units

    def kernel(place_ref, adapter_ref, ag_ref, au_ref, *refs):
        it = iter(refs)
        take = lambda k: [next(it) for _ in range(k)]
        x_in, w_in, b_in, d_in = take(n_rows), take(len(flat)), take(n_sets), take(n_sets)
        hidden, x, w, bb, lg, lu, ld, x_sem, w_sem, b_sem = take(10)

        def weight_copies(step, slot):
            s, t = divmod(step, tiles)
            for g in range(2):
                for i in range(first[s], first[s + 1]):
                    yield dma(
                        w_in[i].at[:, pl.ds(g * units + t * tile, tile)],
                        w.at[slot, g, pl.ds(pl.multiple_of(place_ref[i] * unit, unit), flat[i].shape[0]), :],
                        w_sem.at[slot, g, i - first[s]],
                    )
                yield dma(
                    b_in[s].at[:, pl.ds(g * units + t * tile, tile)],
                    bb.at[slot, g],
                    b_sem.at[slot, g],
                )

        x_copies, start = [], 0
        for i in range(n_rows):
            x_copies.append(dma(x_in[i], x.at[pl.ds(start, rows[i].shape[0]), :], x_sem.at[i]))
            start += rows[i].shape[0]
        for copy in x_copies:
            copy.start()
        for copy in weight_copies(0, 0):
            copy.start()
        for copy in x_copies:
            copy.wait()
        for step in range(steps):
            slot = step % 2
            if step + 1 < steps:
                for copy in weight_copies(step + 1, 1 - slot):
                    copy.start()
            for copy in weight_copies(step, slot):
                copy.wait()
            s, t = divmod(step, tiles)

            @pl.loop(0, total_rows // chunk)
            def _(m):
                at = mm(m, chunk)
                xs = x[at, :]
                if step == 0:
                    lg[at, :] = masked(dot(xs, ag_ref[...]), adapter_ref[at, :])
                    lu[at, :] = masked(dot(xs, au_ref[...]), adapter_ref[at, :])
                gate = dot(xs, w[slot, 0]) + dot(lg[at, :], bb[slot, 0])
                up = dot(xs, w[slot, 1]) + dot(lu[at, :], bb[slot, 1])
                h = (0.5 * gate * (1.0 + jnp.tanh(0.5 * gate)) * up).astype(BF16)
                hidden[at, step * tile : (step + 1) * tile] = h
                more = dot(h, d_in[s][t * tile : (t + 1) * tile, :])
                if step > 0:
                    more = more + ld[at, :]
                if step < steps - 1:
                    ld[at, :] = more
                else:
                    hidden[at, hidden_width:] = masked(more, adapter_ref[at, :])

    return pl.pallas_call(
        kernel,
        in_specs=[SMEM_SPEC] + [VMEM_SPEC] * 3
        + [HBM_SPEC] * (n_rows + len(flat) + n_sets)
        + [VMEM_SPEC] * n_sets,
        out_specs=VMEM_SPEC,
        out_shape=jax.ShapeDtypeStruct((total_rows, hidden_width + rank), BF16),
        scratch_shapes=[
            VM((total_rows, width), BF16),
            VM((2, 2, width, tile), BF16),
            VM((2, 2, rank, tile), BF16),
            VM((total_rows, rank), BF16),
            VM((total_rows, rank), BF16),
            VM((total_rows, rank), F32),
            pltpu.SemaphoreType.DMA((n_rows,)),
            pltpu.SemaphoreType.DMA((2, 2, most)),
            pltpu.SemaphoreType.DMA((2, 2)),
        ],
        compiler_params=PARAMS,
        cost_estimate=COST,
        name="gated",
    )(places, column, a_gate, a_up, *rows, *flat, *bs, *downs)


def project_down(hidden, b, sets, units, at, which, came=None):
    half, depth = hidden.shape[0] // 2, hidden.shape[1]
    piece, rank = half // 4, b.shape[0]
    size = sets[0][0].shape[1]
    flat = [w for group in sets for w in group]
    n, n_sets, n_weights = 4, len(sets), len(flat)
    extra = [] if came is None else [came]

    def kernel(at_ref, h_in, *refs):
        refs = list(refs)
        came_ref = refs.pop(0) if extra else None
        b_ref, w_in, outs = refs[0], refs[1 : 1 + n_weights], refs[1 + n_weights : -4]
        w, h_ref, sems, h_sems = refs[-4:]
        copies = [
            dma(
                b_ref.at[:, mm(at_ref[0], n * size)],
                w.at[n_sets * units : n_sets * units + rank, :],
                sems.at[n_sets * n],
            )
        ]
        h_copies = [
            dma(
                h_in.at[pl.ds(which * half + m * 2 * piece, 2 * piece), :],
                h_ref.at[pl.ds(m * 2 * piece, 2 * piece), :],
                h_sems.at[m],
            )
            for m in range(2)
        ]
        it = iter(w_in)
        for k, group in enumerate(sets):
            place = 0
            for array in group:
                ref = next(it)
                for i in range(array.shape[0] // units):
                    copies.append(
                        dma(
                            ref.at[pl.ds(i * units, units), :],
                            w.at[k * units : (k + 1) * units, place * size : (place + 1) * size],
                            sems.at[k * n + place],
                        )
                    )
                    place += 1
        for copy in copies + h_copies:
            copy.start()
        for copy in copies:
            copy.wait()
        for m in range(2):
            h_copies[m].wait()
            here = slice(m * 2 * piece, (m + 1) * 2 * piece)
            total = dot(h_ref[here, :], w[...])
            if came is None:
                outs[0][here, :] = total.astype(BF16)
            else:
                total = (total + came_ref[here, :].astype(F32)).astype(BF16)
                outs[2 * m][...], outs[2 * m + 1][...] = total[:piece], total[piece:]

    shapes = [jax.ShapeDtypeStruct((half, n * size), BF16)]
    if came is not None:
        shapes = [jax.ShapeDtypeStruct((piece, n * size), BF16)] * 4
    out = pl.pallas_call(
        kernel,
        in_specs=[SMEM_SPEC, HBM_SPEC]
        + [VMEM_SPEC] * len(extra)
        + [HBM_SPEC] * (1 + n_weights),
        out_specs=[VMEM_SPEC] * len(shapes),
        out_shape=shapes,
        scratch_shapes=[
            VM((depth, n * size), BF16),
            VM((half, depth), BF16),
            pltpu.SemaphoreType.DMA((n_sets * n + 1,)),
            pltpu.SemaphoreType.DMA((2,)),
        ],
        compiler_params=PARAMS,
        cost_estimate=COST,
        name="project_down",
    )(at, hidden, *extra, b, *flat)
    return out[0] if came is None else out


def assemble(pieces, places, shape):
    rows, columns = pieces[0].shape

    def kernel(places_ref, *refs):
        out = refs[-1]
        for i in range(len(pieces)):
            to = mm(places_ref[2 * i], rows), mm(places_ref[2 * i + 1], columns)
            out[to] = refs[i][...]

    return pl.pallas_call(
        kernel,
        in_specs=[SMEM_SPEC] + [VMEM_SPEC] * len(pieces),
        out_specs=VMEM_SPEC,
        out_shape=jax.ShapeDtypeStruct(shape, BF16),
        compiler_params=PARAMS,
        cost_estimate=COST,
        name="assemble",
    )(places, *pieces)


@jax.tree_util.register_pytree_node_class
class Live:
    def __init__(self, **arrays):
        self.__dict__.update(arrays)

    def tree_flatten(self):
        names = tuple(sorted(self.__dict__))
        return [self.__dict__[name] for name in names], names

    @classmethod
    def tree_unflatten(cls, names, arrays):
        return cls(**dict(zip(names, arrays)))

    @property
    def pop(self):
        return Pop(self)

    @property
    def drop(self):
        return Drop(self)


class Pop:
    def __init__(self, live):
        self.__dict__.update(live=live)

    def __getattr__(self, name):
        return self.live.__dict__.pop(name)


class Drop(Pop):
    def __getattr__(self, name):
        self.live.__dict__.pop(name)
        return self


def make_body(R, T):
    Z, ZH, Y = R // 2, R // 4, T // 2

    def flat(z, x, y, c):
        return (z * 2 + x) * T + y * 2 + c

    def move(f):
        every = [(r // 2, r % 2, t // 2, t % 2) for r in range(R) for t in range(T)]
        return [(flat(*d), flat(*f(*d))) for d in every]

    def send(value, pairs):
        return lax.ppermute(value, AXES, pairs)

    to_core = move(lambda z, x, y, c: (z, x, y, 1 - c))
    to_x = move(lambda z, x, y, c: (z, 1 - x, y, c))
    z_up = move(lambda z, x, y, c: ((z + 1) % Z, x, y, c))
    z_down = move(lambda z, x, y, c: ((z - 1) % Z, x, y, c))
    from_y = {k: move(lambda z, x, y, c, k=k: (z, x, (y - k) % Y, c)) for k in range(1, Y)}
    same_xzl = [[zh * 4 + b for b in range(4)] for zh in range(ZH)]
    same_zh = [[zh * 4 + b for zh in range(ZH)] for b in range(4)]
    to_xy = {
        (i, k): move(lambda z, x, y, c, i=i, k=k: (z, x ^ i, (y - k) % Y, c))
        for i in (0, 1)
        for k in range(Y)
    }
    to_xzl = {
        (i, j): move(lambda z, x, y, c, i=i, j=j: (z ^ j, x ^ i, y, c))
        for j in (0, 1)
        for i in (0, 1)
    }

    from_zh = {
        k: move(lambda z, x, y, c, k=k: ((z - 2 * k) % Z, x, y, c)) for k in range(1, ZH)
    }
    to_zl = move(lambda z, x, y, c: (z ^ 1, x, y, c))

    def spread(value, axes, groups):
        return lax.all_to_all(value, axes, 0, 0, axis_index_groups=groups, tiled=True)

    def fence(live):
        return lax.optimization_barrier(live)

    def body(
        tokens, lengths, request_adapter, w_qkv, w_out, w_gate, w_up, w_down,
        a_qkv, b_qkv, a_out, b_out, a_gate, b_gate, a_up, b_up, a_down, b_down,
    ):
        r, t = lax.axis_index("req"), lax.axis_index("tp")
        z, x, y, c = r // 2, r % 2, t // 2, t % 2
        zh, zl = z // 2, z % 2
        slots, width = tokens.shape
        piece = slots // T
        block = width // R
        local = w_qkv.shape[2] // 2
        rank = a_qkv.shape[1]
        quarter = w_gate.shape[1] // 4
        span = width // ZH
        count = lengths.shape[1]
        far_y, far_zh, opposite = range(1, Y), range(1, ZH), Z // 2

        def cut(array, start, size, axis):
            return lax.dynamic_slice_in_dim(array, start, size, axis)

        def ints(values):
            return jnp.stack([jnp.asarray(v, jnp.int32) for v in values])

        L = Live(
            tokens=tokens, both=jnp.concatenate([lengths, request_adapter], axis=1), w_gate=w_gate,
            w_up=w_up, w_down=w_down, a_qkv=a_qkv, a_out=a_out, b_out=b_out, a_gate=a_gate,
            a_up=a_up, b_down=b_down, b_qkv=b_qkv, b_gate=b_gate, b_up=b_up, a_down=a_down,
        )
        keys = [(k, i) for k in range(Z) for i in (0, 1)]
        order = [((z + k) % Z) * 2 + (x ^ i) for k, i in keys]
        there = [(zh + h) % ZH for h in range(ZH)]
        at = [(1 - x) * T + ((y + k) % Y) * 2 + s for s in (c, 1 - c) for k in range(Y)]
        far_places = []
        for h in there[1:]:
            first, other = (h * 2 + zl) * 4, (h * 2 + 1 - zl) * 4
            far_places += [first, first + 2, other, other + 1]
        places = ([(zh * 2 + zl) * 4, (zh * 2 + 1 - zl) * 4] + far_places) * Y
        L.ints = Live(
            t=ints([t]), order=[ints(order[:Z]), ints(order[Z:]), ints(order)], qkv=ints([x, *at, *order]),
            xyc=[ints([x, y, c]), ints([x, y, 1 - c])],
            zyc=ints([zl, y, c, zl * 2 + x]), z=ints([(z + k) % Z for k in range(Z)]),
            gated=ints(places), span=[ints([h]) for h in there], b=ints([zl * 2 + x]),
        )
        mine = (zl * 2 + x) * quarter

        def heads_of(w, which):
            return cut(w, which * local, local, 2).reshape(w.shape[0], 3 * local)


        def ring_start(own):
            left = right = own
            got = {0: own}
            for k in range(1, opposite):
                left, right = send(left, z_up), send(right, z_down)
                got[Z - k], got[k] = left, right
            return got

        L.first = send(heads_of(w_qkv, 1 - x), to_x)
        L.ring = [ring_start(heads_of(w_qkv, x))]
        L.out = send(cut(w_out, (1 - x) * local, local, 0), to_x)
        L.both = spread(jnp.concatenate([L.both] * 4, axis=0), "req", same_xzl)
        L.normed, L.mine = norm_rows(L.tokens, L.ints.t, T)
        L.b = jnp.concatenate(
            [cut(L.pop.b_gate, mine, quarter, 1), cut(L.pop.b_up, mine, quarter, 1)], axis=1
        )
        L.a_down = cut(L.a_down, mine, quarter, 0)
        L.b_heads = cut(L.pop.b_qkv, x * local, local, 2).reshape(rank, 3 * local)
        L.own_out = cut(w_out, x * local, local, 0)
        L = fence(L)

        L.ring.append(ring_start(L.pop.first))
        L.quarter = send(L.pop.mine, to_x)
        L.b_far = [send(L.b, from_y[k]) for k in far_y]
        L.a_far = [send(L.a_down, from_y[k]) for k in far_y]
        L.gu, L.gu_give = pack(L.pop.w_gate, L.pop.w_up, L.ints.b)
        L.out = jnp.concatenate([L.pop.own_out, L.out], axis=1)
        L = fence(L)

        L.ring[0][opposite] = send(L.ring[0][opposite + 1], z_up)
        L.ring[1][opposite] = send(L.ring[1][opposite - 1], z_down)
        L.quarters = [L.quarter] + [send(L.quarter, from_y[k]) for k in far_y]
        L.out = ring_start(L.out)
        L.gu_came = send(L.pop.gu_give, to_x)
        both = L.pop.both
        L.tables = tables(both[:, :count], both[:, count:], L.ints.zyc, slots, T)
        L = fence(L)
        L.quarters = L.quarters + [send(q, to_core) for q in L.quarters]
        L.for_out = [L.out[opposite + 1][:, :block], L.out[opposite - 1][:, block:]]
        L.near, L.give = join(L.pop.gu, L.pop.gu_came, L.ints.xyc[0])
        L = fence(L)

        one, two = L.pop.for_out
        L.far_out = [send(one, z_up), send(two, z_down)]
        L.far = send(L.pop.give, to_zl)
        L.y = [[send(L.near, from_y[k]) for k in far_y]]
        column, line, adapter, cosine, sine, adapters = L.tables
        L.joined = project_qkv(
            L.pop.normed, L.pop.quarters, adapter, L.pop.a_qkv, L.pop.b_heads, cosine,
            sine, [L.ring[i][k] for k, i in keys], L.ints.qkv,
        )
        L.pop.ring
        L = fence(L)

        def over_zh(w):
            return [send(w, from_zh[h]) for h in far_zh]

        def relay(arrays):
            return [[send(w, from_y[k]) for w in arrays] for k in far_y]

        def out_of(chunk, core, came=None):
            return project_out(
                attn, adapter, L.a_out, L.b_out, blocks[chunk], L.ints.order[chunk],
                L.ints.xyc[core], T, came,
            )

        rows = L.near.shape[0] // 2
        L.near_parts = [L.near[:rows], L.near[rows:]]
        L.y.append([send(L.far, from_y[k]) for k in far_y])
        L.zh0 = over_zh(L.near_parts[0])
        column, line, adapter, cosine, sine, adapters = L.pop.tables
        attn = attend(L.pop.joined, column, line)
        blocks = [(L.out[k],) if k != opposite else tuple(L.far_out) for k in range(Z)]
        blocks = [blocks[:opposite], blocks[opposite:], blocks]
        L.gives = [out_of(chunk, 1) for chunk in (0, 1)]
        L.attn, L.adapter, L.adapters, L.blocks = attn, adapter, adapters, blocks
        L.drop.out.far_out.quarter
        L = fence(L)
        L.down = spread(L.pop.w_down, "req", same_xzl)
        part = rows_unit = rows // 2
        L.far_parts = [L.far[:part], L.far[part:]]
        L.zh2 = over_zh(L.far_parts[0])
        L.relay0 = relay(L.zh0)
        attn, adapter, blocks = L.pop.attn, L.pop.adapter, L.pop.blocks
        L.parts = out_of(2, 0, [send(give, to_core) for give in L.pop.gives])
        L.drop.a_out.b_out
        L = fence(L)

        parts = L.pop.parts
        terms = [parts[0]]
        for i in (0, 1):
            for k in range(Y):
                if i or k:
                    terms.append(send(parts[i * Y + k], to_xy[(i, k)]))
        L.zh3 = over_zh(L.far_parts[1])
        L.terms = terms
        L = fence(L)
        L.hidden_state, L.normed2 = residual_norm(
            L.pop.tokens, L.ints.t, L.ints.z, [L.pop.terms]
        )
        split = L.down.shape[0] // 2
        L.for_down = [L.down[:split], L.down[split:]]
        L = fence(L)

        own = L.pop.normed2
        L.rows = [own, send(own, to_x), send(own, to_zl)]
        L.relay3 = relay(L.zh3)
        L.zh1 = over_zh(L.near_parts[1])
        L.down_y = [[send(L.for_down[0], from_y[k]) for k in far_y]]
        L.cut = [L.rows[1][: piece // 2], L.rows[2][piece // 2 :]]
        L = fence(L)
        one, two = L.pop.cut
        L.rows += [send(one, to_zl), send(two, to_x)]
        L.relay1, L.relay2 = relay(L.zh1), relay(L.zh2)
        L.down_zh = [over_zh(L.for_down[0])]
        L = fence(L)
        L.rows += [send(row, to_core) for row in L.rows]
        L = fence(L)

        L.down_zh.append(over_zh(L.for_down[1]))
        L.down_y.append([send(L.for_down[1], from_y[k]) for k in far_y])
        L.down_zh_y = [relay(L.down_zh[0])]
        zh_blocks = [part[h] for h in range(ZH - 1) for part in (L.zh0, L.zh1, L.zh2, L.zh3)]
        sets = [([L.near, L.far, *zh_blocks], L.b, L.a_down)]
        for k in range(Y - 1):
            relayed = [part[k][h] for h in range(ZH - 1) for part in (L.relay0, L.relay1, L.relay2, L.relay3)]
            sets.append(([L.y[0][k], L.y[1][k], *relayed], L.b_far[k], L.a_far[k]))
        L.hidden = gated(
            L.rows, L.adapters, L.pop.a_gate, L.pop.a_up, sets, L.ints.gated,
            rows_unit,
        )
        L.drop.near.far.near_parts.far_parts.zh0.zh1.zh2.zh3.relay0.relay1.relay2.relay3
        L.drop.b.a_down.y.b_far.a_far.rows
        L = fence(L)

        L.down_zh_y.append(relay(L.down_zh[1]))
        down_sets = [[[L.down]] + [[part[k] for part in L.down_y] for k in range(Y - 1)]]
        for h in range(ZH - 1):
            far = [[part[k][h] for part in L.down_zh_y] for k in range(Y - 1)]
            down_sets.append([[part[h] for part in L.down_zh]] + far)

        def down_of(h, which, came=None):
            return project_down(
                L.hidden, L.b_down, down_sets[h], quarter, L.ints.span[h], which, came
            )

        came = [send(down_of(h, 1), to_core) for h in range(ZH)]
        pieces, places = [], []
        for h in range(ZH):
            parts = down_of(h, 0, came[h])
            terms = [parts[0]]
            terms += [send(parts[j * 2 + i], to_xzl[(i, j)]) for j in (0, 1) for i in (0, 1) if i or j]
            done = finish(L.hidden_state, terms, L.ints.span[h])
            for k in range(Y):
                there_y = done if k == 0 else send(done, from_y[k])
                for s, got in ((0, there_y), (1, send(there_y, to_core))):
                    pieces.append(got)
                    places += [((y + k) % Y) * 2 + (c ^ s), there[h]]
        return assemble(pieces, ints(places), tokens.shape)

    return body


def solution(mesh):
    in_specs = (
        P("req", None),
        P("req", None),
        P("req", None),
        P("req", None, "tp"),
        P("tp", "req"),
        P("req", "tp"),
        P("req", "tp"),
        P("tp", "req"),
        P(),
        P(None, None, "tp"),
        P("tp", None),
        P(),
        P(),
        P(None, "tp"),
        P(),
        P(None, "tp"),
        P("tp", None),
        P(),
    )
    return jax.shard_map(
        make_body(mesh.shape["req"], mesh.shape["tp"]),
        mesh=mesh, in_specs=in_specs, out_specs=P("req", None), check_vma=False,
    )
```

```python
import math

import jax
import jax.numpy as jnp
from jax import lax
from jax.experimental import pallas as pl
from jax.experimental.pallas import tpu as pltpu
from jax.sharding import PartitionSpec as P

HD = 128
RANK = 16
AXES = ("req", "tp")
epsilon = 1e-05
rope_base = 10000.0
F32 = jnp.float32
BF16 = jnp.bfloat16
VM = pltpu.VMEM
PARAMS = pltpu.CompilerParams(vmem_limit_bytes=56 * 2**20)
COST = pl.CostEstimate(flops=1000, bytes_accessed=1000, transcendentals=0)


def dot(a, b):
    return jnp.dot(a, b, preferred_element_type=F32)


def layer_norm(values):
    row_mean = jnp.mean(values, axis=-1, keepdims=True)
    centred = values - row_mean
    spread = jnp.mean(centred * centred, axis=-1, keepdims=True)
    return (centred * lax.rsqrt(spread + epsilon)).astype(BF16)


def masked(inner, adapter_column):
    rank = lax.broadcasted_iota(jnp.int32, inner.shape, 1) // RANK
    return jnp.where(adapter_column == rank, inner, F32(0.0)).astype(BF16)


def whole(array):
    return pl.BlockSpec(array.shape, lambda *_: (0,) * array.ndim, pipeline_mode=pl.Buffered(1))


def mm(start, size):
    return pl.ds(pl.multiple_of(start * size, size), size)


def dma(source, target, semaphore):
    return pltpu.make_async_copy(source, target, semaphore)


SMEM_SPEC = pl.BlockSpec(memory_space=pltpu.SMEM)
VMEM_SPEC = pl.BlockSpec(memory_space=VM)
HBM_SPEC = pl.BlockSpec(memory_space=pl.ANY)


def norm_rows(tokens, row, T):
    slots, width = tokens.shape
    piece = slots // T

    def kernel(row_ref, tok_ref, out, part):
        i = pl.program_id(0)
        normed = layer_norm(tok_ref[...].astype(F32))
        out[...] = normed

        @pl.when(i == row_ref[0])
        def _():
            part[...] = normed

    return pl.pallas_call(
        kernel,
        grid_spec=pltpu.PrefetchScalarGridSpec(
            num_scalar_prefetch=1,
            grid=(T,),
            in_specs=[pl.BlockSpec((piece, width), lambda i, r: (i, 0))],
            out_specs=[
                pl.BlockSpec((piece, width), lambda i, r: (i, 0)),
                pl.BlockSpec((piece, width), lambda i, r: (0, 0)),
            ],
        ),
        out_shape=[
            jax.ShapeDtypeStruct((slots, width), BF16),
            jax.ShapeDtypeStruct((piece, width), BF16),
        ],
        compiler_params=PARAMS,
        cost_estimate=COST,
        name="norm_rows",
    )(row, tokens)


def pack(gate, up, b):
    rows, columns = gate.shape
    quarter = columns // 4

    def spec(which):
        return pl.BlockSpec((rows, quarter), lambda i, o: (0, o[0] ^ (i * 2 + which)))

    def kernel(b_ref, g0, u0, g1, u1, keep, give):
        keep[0, :, :quarter], keep[0, :, quarter:] = g0[...], u0[...]
        give[0, :, :quarter], give[0, :, quarter:] = g1[...], u1[...]

    out = pl.BlockSpec((1, rows, 2 * quarter), lambda i, o: (i, 0, 0))
    return pl.pallas_call(
        kernel,
        grid_spec=pltpu.PrefetchScalarGridSpec(
            num_scalar_prefetch=1,
            grid=(2,),
            in_specs=[spec(0), spec(0), spec(1), spec(1)],
            out_specs=[out, out],
        ),
        out_shape=[jax.ShapeDtypeStruct((2, rows, 2 * quarter), BF16)] * 2,
        compiler_params=PARAMS,
        cost_estimate=COST,
        name="pack",
    )(b, gate, up, gate, up)


def join(own, came, x):
    rows, columns = own.shape[1:]
    spec = pl.BlockSpec((1, rows, columns), lambda i: (i, 0, 0))
    shape = jax.ShapeDtypeStruct((2 * rows, columns), BF16)

    def kernel(x_ref, own_ref, came_ref, near, give):
        @pl.when(pl.program_id(0) == 0)
        def _():
            near[mm(x_ref[0], rows), :] = own_ref[0]
            near[mm(1 - x_ref[0], rows), :] = came_ref[0]

        @pl.when(pl.program_id(0) == 1)
        def _():
            give[mm(x_ref[0], rows), :] = own_ref[0]
            give[mm(1 - x_ref[0], rows), :] = came_ref[0]

    return pl.pallas_call(
        kernel,
        grid=(2,),
        in_specs=[SMEM_SPEC, spec, spec],
        out_specs=[pl.BlockSpec((2 * rows, columns), lambda i: (0, 0))] * 2,
        out_shape=[shape, shape],
        compiler_params=PARAMS,
        cost_estimate=COST,
        name="join",
    )(x, own, came)


def tables(lengths, adapters, scalars, slots, T):
    count = lengths.shape[1]
    piece = slots // T
    half = HD // 2

    def kernel(len_ref, ad_ref, at_ref, column, line, two, cosine, sine, rows):
        def layout(index, slot, wants):
            end = jnp.int32(0)
            request, start = jnp.zeros(slot.shape, jnp.int32), jnp.zeros(slot.shape, jnp.int32)
            adapter = jnp.full(slot.shape, ad_ref[index, 0], jnp.int32)
            for k in range(count):
                end = end + len_ref[index, k]
                past = slot >= end
                request = request + past.astype(jnp.int32)
                if wants and k + 1 < count:
                    start = jnp.where(past, end, start)
                    adapter = jnp.where(past, ad_ref[index, k + 1], adapter)
            return request, slot - start, adapter

        lane = lax.broadcasted_iota(jnp.int32, (1, HD), 1)
        frequency = jnp.exp((lane % half).astype(F32) * F32(-math.log(rope_base) * 2.0 / HD))
        for i in range(2):
            index = at_ref[0] * 2 + i
            down = lax.broadcasted_iota(jnp.int32, (slots, 1), 0)
            request, position, adapter = layout(index, down, True)
            column[i] = request
            line[i] = layout(index, lax.broadcasted_iota(jnp.int32, (1, slots), 1), False)[0]
            here = slice(i * slots, (i + 1) * slots)
            two[here] = adapter
            angles = position.astype(F32) * frequency
            cosine[here] = jnp.cos(angles)
            sine[here] = jnp.where(lane < half, -jnp.sin(angles), jnp.sin(angles))
        for s in range(2):
            first = (at_ref[1] * 2 + (at_ref[2] ^ s)) * piece
            slot = first + lax.broadcasted_iota(jnp.int32, (piece, 1), 0)
            for b in range(4):
                to = (s * 4 + b) * piece
                rows[to : to + piece] = layout(at_ref[3] ^ b, slot, True)[2]

    table = jax.ShapeDtypeStruct((2 * slots, HD), F32)
    return pl.pallas_call(
        kernel,
        in_specs=[SMEM_SPEC] * 3,
        out_specs=[VMEM_SPEC] * 6,
        out_shape=[
            jax.ShapeDtypeStruct((2, slots, 1), jnp.int32),
            jax.ShapeDtypeStruct((2, 1, slots), jnp.int32),
            jax.ShapeDtypeStruct((2 * slots, 1), jnp.int32),
            table,
            table,
            jax.ShapeDtypeStruct((8 * piece, 1), jnp.int32),
        ],
        compiler_params=PARAMS,
        cost_estimate=COST,
        name="tables",
    )(lengths, adapters, scalars)


def finish(hidden_state, terms, at):
    piece, columns = terms[0].shape
    spec = pl.BlockSpec((piece, columns), lambda i, a: (0, 0))

    def kernel(at_ref, hidden_ref, *refs):
        total = hidden_ref[...]
        for ref in refs[:-1]:
            total = total + ref[...].astype(F32)
        refs[-1][...] = total.astype(BF16)

    return pl.pallas_call(
        kernel,
        grid_spec=pltpu.PrefetchScalarGridSpec(
            num_scalar_prefetch=1,
            grid=(1,),
            in_specs=[pl.BlockSpec((piece, columns), lambda i, a: (0, a[0]))] + [spec] * len(terms),
            out_specs=spec,
        ),
        out_shape=jax.ShapeDtypeStruct((piece, columns), BF16),
        compiler_params=PARAMS,
        cost_estimate=COST,
        name="finish",
    )(at, hidden_state, *terms)


def project_qkv(own, pieces, adapter, a, b, cosine, sine, weights, places):
    slots, width = own.shape
    total_rows, columns, rank = 2 * slots, b.shape[1], b.shape[0]
    piece, size, tile = pieces[0].shape[0], width // len(weights), columns // 3
    n_pieces, n_weights = len(pieces), len(weights)
    chunk = total_rows // 2
    column = adapter

    def kernel(at_ref, adapter_ref, a_ref, cos_ref, sin_ref, own_ref, b_ref, *refs):
        p_in, w_in, rest = refs[:n_pieces], refs[n_pieces : n_pieces + n_weights], refs[-7:]
        out, x, w, bb, low, x_sem, w_sem = rest

        def weight_copies(step, slot):
            to = pl.ds(step * tile, tile)
            for i in range(n_weights):
                yield dma(
                    w_in[i].at[:, to],
                    w.at[slot, mm(at_ref[1 + n_pieces + i], size), :],
                    w_sem.at[slot, i],
                )
            yield dma(b_ref.at[:, to], bb.at[slot], w_sem.at[slot, n_weights])

        x_copies = [dma(own_ref, x.at[mm(at_ref[0], slots), :], x_sem.at[n_pieces])]
        for i in range(n_pieces):
            x_copies.append(dma(p_in[i], x.at[mm(at_ref[1 + i], piece), :], x_sem.at[i]))
        for copy in x_copies:
            copy.start()
        for copy in weight_copies(0, 0):
            copy.start()
        for copy in x_copies:
            copy.wait()
        for step in range(3):
            slot = step % 2
            if step < 2:
                for copy in weight_copies(step + 1, 1 - slot):
                    copy.start()
            for copy in weight_copies(step, slot):
                copy.wait()

            @pl.loop(0, total_rows // chunk)
            def _(m):
                at = mm(m, chunk)
                xs = x[at, :]
                if step == 0:
                    low[at, :] = masked(dot(xs, a_ref[...]), adapter_ref[at, :])
                total = dot(xs, w[slot]) + dot(low[at, :], bb[slot])
                for h in range(tile // HD):
                    v = total[:, h * HD : (h + 1) * HD]
                    if step < 2:
                        v = v * cos_ref[at, :] + pltpu.roll(v, HD // 2, 1) * sin_ref[at, :]
                    start = step * tile + h * HD
                    out[at, start : start + HD] = v.astype(BF16)

    return pl.pallas_call(
        kernel,
        in_specs=[SMEM_SPEC] + [VMEM_SPEC] * 4 + [HBM_SPEC] * (2 + n_pieces + n_weights),
        out_specs=VMEM_SPEC,
        out_shape=jax.ShapeDtypeStruct((total_rows, columns), BF16),
        scratch_shapes=[
            VM((total_rows, width), BF16),
            VM((2, width, tile), BF16),
            VM((2, rank, tile), BF16),
            VM((total_rows, rank), BF16),
            pltpu.SemaphoreType.DMA((n_pieces + 1,)),
            pltpu.SemaphoreType.DMA((2, n_weights + 1)),
        ],
        compiler_params=PARAMS,
        cost_estimate=COST,
        name="project_qkv",
    )(places, column, a, cosine, sine, own, b, *pieces, *weights)


def attend(qkv, column, line):
    indices, slots = column.shape[:2]
    heads = qkv.shape[1] // 3 // HD
    rows = 256 if slots % 256 == 0 else slots

    def kernel(q, k, v, column_ref, line_ref, out):
        for at in range(0, slots, rows):
            seen = at + rows
            s = lax.dot_general(
                q[at:seen], k[:seen], (((1,), (1,)), ((), ())), preferred_element_type=F32
            )
            s = s * (1.0 / math.sqrt(HD))
            here = at + lax.broadcasted_iota(jnp.int32, s.shape, 0)
            there = lax.broadcasted_iota(jnp.int32, s.shape, 1)
            allowed = (column_ref[0, at:seen] == line_ref[0, :, :seen]) & (here >= there)
            s = jnp.where(allowed, s, F32(-1e30))
            e = jnp.exp(s - jnp.max(s, axis=1, keepdims=True))
            weights = (e * (1.0 / jnp.sum(e, axis=1, keepdims=True))).astype(BF16)
            out[at:seen] = dot(weights, v[:seen]).astype(BF16)

    return pl.pallas_call(
        kernel,
        grid=(indices, heads),
        in_specs=[
            pl.BlockSpec((slots, HD), lambda i, h: (i, h)),
            pl.BlockSpec((slots, HD), lambda i, h: (i, heads + h)),
            pl.BlockSpec((slots, HD), lambda i, h: (i, 2 * heads + h)),
            pl.BlockSpec((1, slots, 1), lambda i, h: (i, 0, 0)),
            pl.BlockSpec((1, 1, slots), lambda i, h: (i, 0, 0)),
        ],
        out_specs=pl.BlockSpec((slots, HD), lambda i, h: (i, h)),
        out_shape=jax.ShapeDtypeStruct((indices * slots, heads * HD), BF16),
        compiler_params=PARAMS,
        cost_estimate=COST,
        name="attend",
    )(qkv, qkv, qkv, column, line)


def project_out(attn, adapter, a, b, weights, order, scalars, T, came=None):
    total_rows, depth = attn.shape
    n, slots, piece, Y = len(weights), total_rows // 2, total_rows // 2 // T, T // 2
    extra = list(came or [])
    flat = [p for w in weights for p in w]
    size = sum(p.shape[1] for p in flat) // n // 2
    half, columns = total_rows // 2, n * 2 * size
    per = n // max(1, len(extra))

    def kernel(order_ref, at_ref, attn_ref, adapter_ref, a_ref, b_ref, *refs):
        ws, outs, rows, low = refs[: len(flat)], refs[len(flat) + len(extra) : -2], *refs[-2:]
        x, y, c = at_ref[0], at_ref[1], at_ref[2]
        mine = a_ref[mm(x, depth), :]
        for i in range(2):
            for k in range(Y):
                here = mm((x ^ i) * T + lax.rem(y + Y - k, Y) * 2 + c, piece)
                to = (i * Y + k) * piece
                part = attn_ref[here, :]
                rows[to : to + piece] = part
                low[to : to + piece] = masked(dot(part, mine), adapter_ref[here, :])
        it = iter(ws)
        for k, w in enumerate(weights):
            blocks = []
            for p in w:
                ref = next(it)
                for start in range(0, p.shape[1], size):
                    blocks.append((ref, start))
            for i, (ref, start) in enumerate(blocks):
                there = mm(order_ref[2 * k + i], size)
                to = mm(k * 2 + (x ^ i), size)
                total = dot(rows[...], ref[:, start : start + size]) + dot(low[...], b_ref[:, there])
                if came is None:
                    outs[0][:, to] = total.astype(BF16)
                else:
                    from_core = refs[len(flat) + k // per][:, mm(k % per * 2 + (x ^ i), size)]
                    total = (total + from_core.astype(F32)).astype(BF16)
                    for p in range(2 * Y):
                        outs[p][:, to] = total[p * piece : (p + 1) * piece]

    shapes = [jax.ShapeDtypeStruct((half, columns), BF16)]
    if came is not None:
        shapes = [jax.ShapeDtypeStruct((piece, columns), BF16)] * (2 * Y)
    out = pl.pallas_call(
        kernel,
        in_specs=[SMEM_SPEC, SMEM_SPEC] + [VMEM_SPEC] * (4 + len(flat) + len(extra)),
        out_specs=[VMEM_SPEC] * len(shapes),
        out_shape=shapes,
        scratch_shapes=[VM((half, depth), BF16), VM((half, a.shape[1]), BF16)],
        compiler_params=PARAMS,
        cost_estimate=COST,
        name="project_out",
    )(order, scalars, attn, adapter, a, b, *flat, *extra)
    return out[0] if came is None else out


def residual_norm(tokens, row, order, chunks):
    width = tokens.shape[1]
    n = order.shape[0]
    piece, size, per = chunks[0][0].shape[0], width // n, n // len(chunks)
    flat = [term for chunk in chunks for term in chunk]

    def kernel(row_ref, order_ref, tok_ref, *refs):
        it, hidden, normed = iter(refs[:-2]), refs[-2], refs[-1]
        for c, chunk in enumerate(chunks):
            total = next(it)[...].astype(F32)
            for _ in chunk[1:]:
                total = total + next(it)[...].astype(F32)
            for place in range(per):
                to = mm(order_ref[c * per + place], size)
                more = total[:, place * size : (place + 1) * size]
                hidden[:, to] = tok_ref[:, to].astype(F32) + more
        normed[...] = layer_norm(hidden[...])

    return pl.pallas_call(
        kernel,
        grid_spec=pltpu.PrefetchScalarGridSpec(
            num_scalar_prefetch=2,
            grid=(1,),
            in_specs=[
                pl.BlockSpec((piece, width), lambda n, r, o: (r[0], 0)),
                *[pl.BlockSpec(p.shape, lambda n, r, o: (0, 0)) for p in flat],
            ],
            out_specs=[pl.BlockSpec((piece, width), lambda n, r, o: (0, 0))] * 2,
        ),
        out_shape=[
            jax.ShapeDtypeStruct((piece, width), F32),
            jax.ShapeDtypeStruct((piece, width), BF16),
        ],
        compiler_params=PARAMS,
        cost_estimate=COST,
        name="residual_norm",
    )(row, order, tokens, *flat)


def gated(rows, adapters, a_gate, a_up, sets, places, unit):
    width = rows[0].shape[1]
    total_rows = sum(row.shape[0] for row in rows)
    units = sets[0][1].shape[1] // 2
    tile = min(256, units)
    tiles = units // tile
    rank = a_gate.shape[1]
    column = adapters
    flat = [w for s in sets for w in s[0]]
    first = [sum(len(s[0]) for s in sets[:k]) for k in range(len(sets) + 1)]
    bs = [s[1] for s in sets]
    downs = [s[2] for s in sets]
    n_rows, n_sets = len(rows), len(sets)
    most = max(len(s[0]) for s in sets)
    steps = n_sets * tiles
    chunk = total_rows // 2
    hidden_width = n_sets * units

    def kernel(place_ref, adapter_ref, ag_ref, au_ref, *refs):
        it = iter(refs)
        take = lambda k: [next(it) for _ in range(k)]
        x_in, w_in, b_in, d_in = take(n_rows), take(len(flat)), take(n_sets), take(n_sets)
        hidden, x, w, bb, lg, lu, ld, x_sem, w_sem, b_sem = take(10)

        def weight_copies(step, slot):
            s, t = divmod(step, tiles)
            for g in range(2):
                for i in range(first[s], first[s + 1]):
                    yield dma(
                        w_in[i].at[:, pl.ds(g * units + t * tile, tile)],
                        w.at[slot, g, pl.ds(pl.multiple_of(place_ref[i] * unit, unit), flat[i].shape[0]), :],
                        w_sem.at[slot, g, i - first[s]],
                    )
                yield dma(
                    b_in[s].at[:, pl.ds(g * units + t * tile, tile)],
                    bb.at[slot, g],
                    b_sem.at[slot, g],
                )

        x_copies, start = [], 0
        for i in range(n_rows):
            x_copies.append(dma(x_in[i], x.at[pl.ds(start, rows[i].shape[0]), :], x_sem.at[i]))
            start += rows[i].shape[0]
        for copy in x_copies:
            copy.start()
        for copy in weight_copies(0, 0):
            copy.start()
        for copy in x_copies:
            copy.wait()
        for step in range(steps):
            slot = step % 2
            if step + 1 < steps:
                for copy in weight_copies(step + 1, 1 - slot):
                    copy.start()
            for copy in weight_copies(step, slot):
                copy.wait()
            s, t = divmod(step, tiles)

            @pl.loop(0, total_rows // chunk)
            def _(m):
                at = mm(m, chunk)
                xs = x[at, :]
                if step == 0:
                    lg[at, :] = masked(dot(xs, ag_ref[...]), adapter_ref[at, :])
                    lu[at, :] = masked(dot(xs, au_ref[...]), adapter_ref[at, :])
                gate = dot(xs, w[slot, 0]) + dot(lg[at, :], bb[slot, 0])
                up = dot(xs, w[slot, 1]) + dot(lu[at, :], bb[slot, 1])
                h = (0.5 * gate * (1.0 + jnp.tanh(0.5 * gate)) * up).astype(BF16)
                hidden[at, step * tile : (step + 1) * tile] = h
                more = dot(h, d_in[s][t * tile : (t + 1) * tile, :])
                if step > 0:
                    more = more + ld[at, :]
                if step < steps - 1:
                    ld[at, :] = more
                else:
                    hidden[at, hidden_width:] = masked(more, adapter_ref[at, :])

    return pl.pallas_call(
        kernel,
        in_specs=[SMEM_SPEC] + [VMEM_SPEC] * 3
        + [HBM_SPEC] * (n_rows + len(flat) + n_sets)
        + [VMEM_SPEC] * n_sets,
        out_specs=VMEM_SPEC,
        out_shape=jax.ShapeDtypeStruct((total_rows, hidden_width + rank), BF16),
        scratch_shapes=[
            VM((total_rows, width), BF16),
            VM((2, 2, width, tile), BF16),
            VM((2, 2, rank, tile), BF16),
            VM((total_rows, rank), BF16),
            VM((total_rows, rank), BF16),
            VM((total_rows, rank), F32),
            pltpu.SemaphoreType.DMA((n_rows,)),
            pltpu.SemaphoreType.DMA((2, 2, most)),
            pltpu.SemaphoreType.DMA((2, 2)),
        ],
        compiler_params=PARAMS,
        cost_estimate=COST,
        name="gated",
    )(places, column, a_gate, a_up, *rows, *flat, *bs, *downs)


def project_down(hidden, b, sets, units, at, which, came=None):
    half, depth = hidden.shape[0] // 2, hidden.shape[1]
    piece, rank = half // 4, b.shape[0]
    size = sets[0][0].shape[1]
    flat = [w for group in sets for w in group]
    n, n_sets, n_weights = 4, len(sets), len(flat)
    extra = [] if came is None else [came]

    def kernel(at_ref, h_in, *refs):
        refs = list(refs)
        came_ref = refs.pop(0) if extra else None
        b_ref, w_in, outs = refs[0], refs[1 : 1 + n_weights], refs[1 + n_weights : -4]
        w, h_ref, sems, h_sems = refs[-4:]
        copies = [
            dma(
                b_ref.at[:, mm(at_ref[0], n * size)],
                w.at[n_sets * units : n_sets * units + rank, :],
                sems.at[n_sets * n],
            )
        ]
        h_copies = [
            dma(
                h_in.at[pl.ds(which * half + m * 2 * piece, 2 * piece), :],
                h_ref.at[pl.ds(m * 2 * piece, 2 * piece), :],
                h_sems.at[m],
            )
            for m in range(2)
        ]
        it = iter(w_in)
        for k, group in enumerate(sets):
            place = 0
            for array in group:
                ref = next(it)
                for i in range(array.shape[0] // units):
                    copies.append(
                        dma(
                            ref.at[pl.ds(i * units, units), :],
                            w.at[k * units : (k + 1) * units, place * size : (place + 1) * size],
                            sems.at[k * n + place],
                        )
                    )
                    place += 1
        for copy in copies + h_copies:
            copy.start()
        for copy in copies:
            copy.wait()
        for copy in h_copies:
            copy.wait()

        @pl.loop(0, 2)
        def _(m):
            to = mm(m, n * size // 2)
            total = dot(h_ref[...], w[:, to])
            if came is None:
                outs[0][:, to] = total.astype(BF16)
            else:
                total = (total + came_ref[:, to].astype(F32)).astype(BF16)
                for p in range(4):
                    outs[p][:, to] = total[p * piece : (p + 1) * piece]


    shapes = [jax.ShapeDtypeStruct((half, n * size), BF16)]
    if came is not None:
        shapes = [jax.ShapeDtypeStruct((piece, n * size), BF16)] * 4
    out = pl.pallas_call(
        kernel,
        in_specs=[SMEM_SPEC, HBM_SPEC]
        + [VMEM_SPEC] * len(extra)
        + [HBM_SPEC] * (1 + n_weights),
        out_specs=[VMEM_SPEC] * len(shapes),
        out_shape=shapes,
        scratch_shapes=[
            VM((depth, n * size), BF16),
            VM((half, depth), BF16),
            pltpu.SemaphoreType.DMA((n_sets * n + 1,)),
            pltpu.SemaphoreType.DMA((2,)),
        ],
        compiler_params=PARAMS,
        cost_estimate=COST,
        name="project_down",
    )(at, hidden, *extra, b, *flat)
    return out[0] if came is None else out


def assemble(pieces, places, shape):
    rows, columns = pieces[0].shape

    def kernel(places_ref, *refs):
        out = refs[-1]
        for i in range(len(pieces)):
            to = mm(places_ref[2 * i], rows), mm(places_ref[2 * i + 1], columns)
            out[to] = refs[i][...]

    return pl.pallas_call(
        kernel,
        in_specs=[SMEM_SPEC] + [VMEM_SPEC] * len(pieces),
        out_specs=VMEM_SPEC,
        out_shape=jax.ShapeDtypeStruct(shape, BF16),
        compiler_params=PARAMS,
        cost_estimate=COST,
        name="assemble",
    )(places, *pieces)


@jax.tree_util.register_pytree_node_class
class Live:
    def __init__(self, **arrays):
        self.__dict__.update(arrays)

    def tree_flatten(self):
        names = tuple(sorted(self.__dict__))
        return [self.__dict__[name] for name in names], names

    @classmethod
    def tree_unflatten(cls, names, arrays):
        return cls(**dict(zip(names, arrays)))

    @property
    def pop(self):
        return Pop(self)

    @property
    def drop(self):
        return Drop(self)


class Pop:
    def __init__(self, live):
        self.__dict__.update(live=live)

    def __getattr__(self, name):
        return self.live.__dict__.pop(name)


class Drop(Pop):
    def __getattr__(self, name):
        self.live.__dict__.pop(name)
        return self


def make_body(R, T):
    Z, ZH, Y = R // 2, R // 4, T // 2

    def flat(z, x, y, c):
        return (z * 2 + x) * T + y * 2 + c

    def move(f):
        every = [(r // 2, r % 2, t // 2, t % 2) for r in range(R) for t in range(T)]
        return [(flat(*d), flat(*f(*d))) for d in every]

    def send(value, pairs):
        return lax.ppermute(value, AXES, pairs)

    to_core = move(lambda z, x, y, c: (z, x, y, 1 - c))
    to_x = move(lambda z, x, y, c: (z, 1 - x, y, c))
    z_up = move(lambda z, x, y, c: ((z + 1) % Z, x, y, c))
    z_down = move(lambda z, x, y, c: ((z - 1) % Z, x, y, c))
    from_y = {k: move(lambda z, x, y, c, k=k: (z, x, (y - k) % Y, c)) for k in range(1, Y)}
    same_xzl = [[zh * 4 + b for b in range(4)] for zh in range(ZH)]
    same_zh = [[zh * 4 + b for zh in range(ZH)] for b in range(4)]
    to_xy = {
        (i, k): move(lambda z, x, y, c, i=i, k=k: (z, x ^ i, (y - k) % Y, c))
        for i in (0, 1)
        for k in range(Y)
    }
    to_xzl = {
        (i, j): move(lambda z, x, y, c, i=i, j=j: (z ^ j, x ^ i, y, c))
        for j in (0, 1)
        for i in (0, 1)
    }

    from_zh = {
        k: move(lambda z, x, y, c, k=k: ((z - 2 * k) % Z, x, y, c)) for k in range(1, ZH)
    }
    to_zl = move(lambda z, x, y, c: (z ^ 1, x, y, c))

    def spread(value, axes, groups):
        return lax.all_to_all(value, axes, 0, 0, axis_index_groups=groups, tiled=True)

    def fence(live):
        return lax.optimization_barrier(live)

    def body(
        tokens, lengths, request_adapter, w_qkv, w_out, w_gate, w_up, w_down,
        a_qkv, b_qkv, a_out, b_out, a_gate, b_gate, a_up, b_up, a_down, b_down,
    ):
        r, t = lax.axis_index("req"), lax.axis_index("tp")
        z, x, y, c = r // 2, r % 2, t // 2, t % 2
        zh, zl = z // 2, z % 2
        slots, width = tokens.shape
        piece = slots // T
        block = width // R
        local = w_qkv.shape[2] // 2
        rank = a_qkv.shape[1]
        quarter = w_gate.shape[1] // 4
        span = width // ZH
        count = lengths.shape[1]
        far_y, far_zh, opposite = range(1, Y), range(1, ZH), Z // 2

        def cut(array, start, size, axis):
            return lax.dynamic_slice_in_dim(array, start, size, axis)

        def ints(values):
            return jnp.stack([jnp.asarray(v, jnp.int32) for v in values])

        L = Live(
            tokens=tokens, both=jnp.concatenate([lengths, request_adapter], axis=1), w_gate=w_gate,
            w_up=w_up, w_down=w_down, a_qkv=a_qkv, a_out=a_out, b_out=b_out, a_gate=a_gate,
            a_up=a_up, b_down=b_down, b_qkv=b_qkv, b_gate=b_gate, b_up=b_up, a_down=a_down,
        )
        keys = [(k, i) for k in range(Z) for i in (0, 1)]
        order = [((z + k) % Z) * 2 + (x ^ i) for k, i in keys]
        there = [(zh + h) % ZH for h in range(ZH)]
        at = [(1 - x) * T + ((y + k) % Y) * 2 + s for s in (c, 1 - c) for k in range(Y)]
        far_places = []
        for h in there[1:]:
            first, other = (h * 2 + zl) * 4, (h * 2 + 1 - zl) * 4
            far_places += [first, first + 2, other, other + 1]
        places = ([(zh * 2 + zl) * 4, (zh * 2 + 1 - zl) * 4] + far_places) * Y
        L.ints = Live(
            t=ints([t]), order=[ints(order[:Z]), ints(order[Z:]), ints(order)], qkv=ints([x, *at, *order]),
            xyc=[ints([x, y, c]), ints([x, y, 1 - c])],
            zyc=ints([zl, y, c, zl * 2 + x]), z=ints([(z + k) % Z for k in range(Z)]),
            gated=ints(places), span=[ints([h]) for h in there], b=ints([zl * 2 + x]),
        )
        mine = (zl * 2 + x) * quarter

        def heads_of(w, which):
            return cut(w, which * local, local, 2).reshape(w.shape[0], 3 * local)


        def ring_start(own):
            left = right = own
            got = {0: own}
            for k in range(1, opposite):
                left, right = send(left, z_up), send(right, z_down)
                got[Z - k], got[k] = left, right
            return got

        L.first = send(heads_of(w_qkv, 1 - x), to_x)
        L.ring = [ring_start(heads_of(w_qkv, x))]
        L.out = send(cut(w_out, (1 - x) * local, local, 0), to_x)
        L.both = spread(jnp.concatenate([L.both] * 4, axis=0), "req", same_xzl)
        L.normed, L.mine = norm_rows(L.tokens, L.ints.t, T)
        L.b = jnp.concatenate(
            [cut(L.pop.b_gate, mine, quarter, 1), cut(L.pop.b_up, mine, quarter, 1)], axis=1
        )
        L.a_down = cut(L.a_down, mine, quarter, 0)
        L.b_heads = cut(L.pop.b_qkv, x * local, local, 2).reshape(rank, 3 * local)
        L.own_out = cut(w_out, x * local, local, 0)
        L = fence(L)

        L.ring.append(ring_start(L.pop.first))
        L.quarter = send(L.pop.mine, to_x)
        L.b_far = [send(L.b, from_y[k]) for k in far_y]
        L.a_far = [send(L.a_down, from_y[k]) for k in far_y]
        L.gu, L.gu_give = pack(L.pop.w_gate, L.pop.w_up, L.ints.b)
        L.out = jnp.concatenate([L.pop.own_out, L.out], axis=1)
        L = fence(L)

        L.ring[0][opposite] = send(L.ring[0][opposite + 1], z_up)
        L.ring[1][opposite] = send(L.ring[1][opposite - 1], z_down)
        L.quarters = [L.quarter] + [send(L.quarter, from_y[k]) for k in far_y]
        L.out = ring_start(L.out)
        L.gu_came = send(L.pop.gu_give, to_x)
        both = L.pop.both
        L.tables = tables(both[:, :count], both[:, count:], L.ints.zyc, slots, T)
        L = fence(L)
        L.quarters = L.quarters + [send(q, to_core) for q in L.quarters]
        L.for_out = [L.out[opposite + 1][:, :block], L.out[opposite - 1][:, block:]]
        L.near, L.give = join(L.pop.gu, L.pop.gu_came, L.ints.xyc[0])
        L = fence(L)

        one, two = L.pop.for_out
        L.far_out = [send(one, z_up), send(two, z_down)]
        L.far = send(L.pop.give, to_zl)
        L.y = [[send(L.near, from_y[k]) for k in far_y]]
        column, line, adapter, cosine, sine, adapters = L.tables
        L.joined = project_qkv(
            L.pop.normed, L.pop.quarters, adapter, L.pop.a_qkv, L.pop.b_heads, cosine,
            sine, [L.ring[i][k] for k, i in keys], L.ints.qkv,
        )
        L.pop.ring
        L = fence(L)

        def over_zh(w):
            return [send(w, from_zh[h]) for h in far_zh]

        def relay(arrays):
            return [[send(w, from_y[k]) for w in arrays] for k in far_y]

        def out_of(chunk, core, came=None):
            return project_out(
                attn, adapter, L.a_out, L.b_out, blocks[chunk], L.ints.order[chunk],
                L.ints.xyc[core], T, came,
            )

        rows = L.near.shape[0] // 2
        L.near_parts = [L.near[:rows], L.near[rows:]]
        L.y.append([send(L.far, from_y[k]) for k in far_y])
        L.zh0 = over_zh(L.near_parts[0])
        column, line, adapter, cosine, sine, adapters = L.pop.tables
        attn = attend(L.pop.joined, column, line)
        blocks = [(L.out[k],) if k != opposite else tuple(L.far_out) for k in range(Z)]
        blocks = [blocks[:opposite], blocks[opposite:], blocks]
        L.gives = [out_of(chunk, 1) for chunk in (0, 1)]
        L.attn, L.adapter, L.adapters, L.blocks = attn, adapter, adapters, blocks
        L.drop.out.far_out.quarter
        L = fence(L)
        L.down = spread(L.pop.w_down, "req", same_xzl)
        part = rows_unit = rows // 2
        L.far_parts = [L.far[:part], L.far[part:]]
        L.zh2 = over_zh(L.far_parts[0])
        L.relay0 = relay(L.zh0)
        attn, adapter, blocks = L.pop.attn, L.pop.adapter, L.pop.blocks
        L.parts = out_of(2, 0, [send(give, to_core) for give in L.pop.gives])
        L.drop.a_out.b_out
        L = fence(L)

        parts = L.pop.parts
        terms = [parts[0]]
        for i in (0, 1):
            for k in range(Y):
                if i or k:
                    terms.append(send(parts[i * Y + k], to_xy[(i, k)]))
        L.zh3 = over_zh(L.far_parts[1])
        L.terms = terms
        L = fence(L)
        L.hidden_state, L.normed2 = residual_norm(
            L.pop.tokens, L.ints.t, L.ints.z, [L.pop.terms]
        )
        split = L.down.shape[0] // 2
        L.for_down = [L.down[:split], L.down[split:]]
        L = fence(L)

        own = L.pop.normed2
        L.rows = [own, send(own, to_x), send(own, to_zl)]
        L.relay3 = relay(L.zh3)
        L.zh1 = over_zh(L.near_parts[1])
        L.down_y = [[send(L.for_down[0], from_y[k]) for k in far_y]]
        L.cut = [L.rows[1][: piece // 2], L.rows[2][piece // 2 :]]
        L = fence(L)
        one, two = L.pop.cut
        L.rows += [send(one, to_zl), send(two, to_x)]
        L.relay1, L.relay2 = relay(L.zh1), relay(L.zh2)
        L.down_zh = [over_zh(L.for_down[0])]
        L = fence(L)
        L.rows += [send(row, to_core) for row in L.rows]
        L = fence(L)

        L.down_zh.append(over_zh(L.for_down[1]))
        L.down_y.append([send(L.for_down[1], from_y[k]) for k in far_y])
        L.down_zh_y = [relay(L.down_zh[0])]
        zh_blocks = [part[h] for h in range(ZH - 1) for part in (L.zh0, L.zh1, L.zh2, L.zh3)]
        sets = [([L.near, L.far, *zh_blocks], L.b, L.a_down)]
        for k in range(Y - 1):
            relayed = [part[k][h] for h in range(ZH - 1) for part in (L.relay0, L.relay1, L.relay2, L.relay3)]
            sets.append(([L.y[0][k], L.y[1][k], *relayed], L.b_far[k], L.a_far[k]))
        L.hidden = gated(
            L.rows, L.adapters, L.pop.a_gate, L.pop.a_up, sets, L.ints.gated,
            rows_unit,
        )
        L.drop.near.far.near_parts.far_parts.zh0.zh1.zh2.zh3.relay0.relay1.relay2.relay3
        L.drop.b.a_down.y.b_far.a_far.rows
        L = fence(L)

        L.down_zh_y.append(relay(L.down_zh[1]))
        down_sets = [[[L.down]] + [[part[k] for part in L.down_y] for k in range(Y - 1)]]
        for h in range(ZH - 1):
            far = [[part[k][h] for part in L.down_zh_y] for k in range(Y - 1)]
            down_sets.append([[part[h] for part in L.down_zh]] + far)

        def down_of(h, which, came=None):
            return project_down(
                L.hidden, L.b_down, down_sets[h], quarter, L.ints.span[h], which, came
            )

        came = [send(down_of(h, 1), to_core) for h in range(ZH)]
        pieces, places = [], []
        for h in range(ZH):
            parts = down_of(h, 0, came[h])
            terms = [parts[0]]
            terms += [send(parts[j * 2 + i], to_xzl[(i, j)]) for j in (0, 1) for i in (0, 1) if i or j]
            done = finish(L.hidden_state, terms, L.ints.span[h])
            for k in range(Y):
                there_y = done if k == 0 else send(done, from_y[k])
                for s, got in ((0, there_y), (1, send(there_y, to_core))):
                    pieces.append(got)
                    places += [((y + k) % Y) * 2 + (c ^ s), there[h]]
        return assemble(pieces, ints(places), tokens.shape)

    return body


def solution(mesh):
    in_specs = (
        P("req", None),
        P("req", None),
        P("req", None),
        P("req", None, "tp"),
        P("tp", "req"),
        P("req", "tp"),
        P("req", "tp"),
        P("tp", "req"),
        P(),
        P(None, None, "tp"),
        P("tp", None),
        P(),
        P(),
        P(None, "tp"),
        P(),
        P(None, "tp"),
        P("tp", None),
        P(),
    )
    return jax.shard_map(
        make_body(mesh.shape["req"], mesh.shape["tp"]),
        mesh=mesh, in_specs=in_specs, out_specs=P("req", None), check_vma=False,
    )
```
